128 devices in a mesh: dp: 64 (over z_lo, x, y, core), mp: 2 (over z_hi).
Axes of the slice: x: 4, y: 4, z: 4 (z_hi: 2, z_lo: 2; z = z_hi * 2 + z_lo), core: 2. Of those that a mesh axis runs over, the one named last changes fastest.
Arguments:
- tokens: bfloat16 [16384, 2048], P(('dp', 'mp')), may hold values from -6 to 6
- layernorm_gain: float32 [2048], replicated, may hold values from 0.5 to 1.5
- layernorm_bias: float32 [2048], replicated, may hold values from -1.75 to 1.75
- w_qkv: bfloat16 [2048, 3, 2048], P('dp', None, 'mp'), may hold values from -0.125 to 0.125
- b_qkv: float32 [3, 2048], P(None, 'mp'), may hold values from -3 to 3
- w_out: bfloat16 [2048, 2048], P('mp', 'dp'), may hold values from -0.5 to 0.5
- b_out: float32 [2048], replicated, may hold values from -1.75 to 1.75
- w_up: bfloat16 [2048, 8192], P('dp', 'mp'), may hold values from -0.125 to 0.125
- b_up: float32 [8192], P('mp'), may hold values from -3 to 3
- w_down: bfloat16 [8192, 2048], P('mp', 'dp'), may hold values from -0.0625 to 0.0625
- b_down: float32 [2048], replicated, may hold values from -1.75 to 1.75
- segments: int32 [16384], P('dp'), may hold values from 0 to 1, as said below
- cotangent: bfloat16 [16384, 2048], P(('dp', 'mp')), may hold values from -6 to 6
Outputs:
- mixed: bfloat16 [16384, 2048], P(('dp', 'mp'))
- d_tokens: float32 [16384, 2048], P(('dp', 'mp'))
- d_ln_gain: float32 [2048], replicated
- d_ln_bias: float32 [2048], replicated
- d_w_qkv: float32 [2048, 3, 2048], P('dp', None, 'mp')
- d_b_qkv: float32 [3, 2048], P(None, 'mp')
- d_w_out: float32 [2048, 2048], P('mp', 'dp')
- d_b_out: float32 [2048], replicated
- d_w_up: float32 [2048, 8192], P('dp', 'mp')
- d_b_up: float32 [8192], P('mp')
- d_w_down: float32 [8192, 2048], P('mp', 'dp')
- d_b_down: float32 [2048], replicated
The draws below stay inside these ranges and needn't reach their ends.
Inputs may be any that keep to these rules, and one draw needn't show every extreme that they name: `segments`: each sequence of 256 tokens holds exactly 2 documents, numbered from 0 in order, so segment numbers never fall and rise by one at each document start; the tokens at positions 124 to 131 of each sequence lie in one document.
All inputs are finite; a program needn't handle non-finite values.
Results may differ from the reference program's by a relative error of at most 0.011.
Values may be sent and summed in bfloat16 or wider, within the bound.
No kernel may reach another device: no remote copies, remote signals or barrier semaphores. Data moves between devices by JAX's collectives and lax.ppermute only.
A program may use at most 256 MiB of HBM per device.

```python
import math
import jax
import jax.numpy as jnp
from jax import lax

D = 2048
HEADS = 32
HEAD_DIM = 64
FF = 8192
ROT = 32
SEQ = 256
DOCS = 2
TOKENS = 16384


def draw_segments(key, part):
    key = jax.random.fold_in(key, 11)
    seq_count = TOKENS // SEQ
    slot = SEQ // DOCS
    token_index = jnp.arange(SEQ, dtype=jnp.int32)
    offsets = jax.random.randint(key, (seq_count, DOCS - 1), slot // 4, slot // 2).astype(jnp.int32)
    cuts = jnp.arange(1, DOCS, dtype=jnp.int32)[None, :] * slot + offsets
    crossed = (token_index[None, :, None] >= cuts[:, None, :]).astype(jnp.int32)
    return jnp.sum(crossed, axis=2).reshape(TOKENS).astype(jnp.int32)


def level_of(stream_key, extent, cuts, smallest, largest):
    loudness = 1.0
    for dim, parts in cuts:
        heights = jax.random.uniform(jax.random.fold_in(jax.random.fold_in(stream_key, 6), dim), (parts,), jnp.float32, smallest / len(cuts), largest / len(cuts))
        loudness = loudness * jnp.repeat(jnp.exp(heights), extent[dim] // parts).reshape((-1,) + (1,) * (len(extent) - 1 - dim))
    return loudness


def normal_values(stream_key, dims, spread, bound, split=(), held_as=jnp.bfloat16):
    loudness = level_of(stream_key, dims, split, -0.22, 0.18) if split else 1.0
    drawn = jax.random.normal(stream_key, dims, jnp.float32) * spread * loudness
    return jnp.minimum(jnp.maximum(drawn, -bound), bound).astype(held_as)


def setup_inputs(seed: int = 0) -> dict:
    streams_of = jax.random.split(jax.random.key(seed), 14)
    tokens = normal_values(streams_of[0], (TOKENS, D), 1.0, 6.0, ((0, 128),))
    layernorm_gain = jnp.clip(1.0 + 0.1 * jax.random.normal(streams_of[1], (D,), jnp.float32), 0.5, 1.5)
    layernorm_bias = normal_values(streams_of[2], (D,), 0.3, 1.75, (), jnp.float32)
    w_qkv = normal_values(streams_of[3], (D, 3, D), D ** -0.5, 0.125, ((0, 64), (2, 2)))
    b_qkv = normal_values(streams_of[4], (3, D), 0.5, 3.0, ((1, 2),), jnp.float32)
    w_out = normal_values(streams_of[5], (D, D), (D // 16) ** -0.5, 0.5, ((0, 2), (1, 64)))
    b_out = normal_values(streams_of[6], (D,), 0.3, 1.75, (), jnp.float32)
    w_up = normal_values(streams_of[7], (D, FF), D ** -0.5, 0.125, ((0, 64), (1, 2)))
    b_up = normal_values(streams_of[8], (FF,), 0.5, 3.0, ((0, 2),), jnp.float32)
    w_down = normal_values(streams_of[9], (FF, D), FF ** -0.5, 0.0625, ((0, 2), (1, 64)))
    b_down = normal_values(streams_of[10], (D,), 0.3, 1.75, (), jnp.float32)
    segments = draw_segments(jax.random.fold_in(streams_of[13], 71), 0)
    cotangent = normal_values(streams_of[12], (TOKENS, D), 1.0, 6.0, ((0, 128),))
    return dict(tokens=tokens, layernorm_gain=layernorm_gain, layernorm_bias=layernorm_bias, w_qkv=w_qkv, b_qkv=b_qkv, w_out=w_out, b_out=b_out, w_up=w_up, b_up=b_up, w_down=w_down, b_down=b_down, segments=segments, cotangent=cotangent)


@jax.custom_vjp
def low(v):
    return lax.optimization_barrier(v.astype(jnp.bfloat16)).astype(jnp.float32)

@jax.custom_vjp
def low_back(v):
    return v

def low_keep(v):
    return (low(v), None)

def low_pass(kept, grad):
    return (grad,)

def back_keep(v):
    return (v, None)

def back_low(kept, grad):
    return (low(grad),)
low.defvjp(low_keep, low_pass)
low_back.defvjp(back_keep, back_low)
epsilon = 1e-05
highest = lax.Precision.HIGHEST

def rotary_tables(segment_rows):
    length = segment_rows.shape[-1]
    token_index = jnp.arange(length, dtype=jnp.int32)
    same_doc = segment_rows[..., :, None] == segment_rows[..., None, :]
    doc_start = lax.optimization_barrier(jnp.min(jnp.where(same_doc, token_index[None, :], length), axis=-1))
    positions = (token_index - doc_start).astype(jnp.float32)
    inv_freq = 10000.0 ** (-(jnp.arange(ROT // 2, dtype=jnp.float32) * 2.0 / ROT))
    angles = positions[..., None] * inv_freq
    allowed = same_doc & (token_index[:, None] >= token_index[None, :])
    return (jnp.cos(angles)[..., None, :], jnp.sin(angles)[..., None, :], allowed)

def rotate_heads(tensor, cos_table, sin_table):
    half_rot = cos_table.shape[-1]
    first_half = tensor[..., :half_rot]
    second_half = tensor[..., half_rot:2 * half_rot]
    return jnp.concatenate([first_half * cos_table - second_half * sin_table, second_half * cos_table + first_half * sin_table, tensor[..., 2 * half_rot:]], axis=-1)

def block_forward(params, block_rows, block_segments):
    layernorm_gain, layernorm_bias, w_qkv, b_qkv, w_out, b_out, w_up, b_up, w_down, b_down = params
    row_mean = lax.optimization_barrier(jnp.mean(block_rows, axis=-1, keepdims=True))
    mean_removed = block_rows - row_mean
    variance = lax.optimization_barrier(jnp.mean(mean_removed * mean_removed, axis=-1, keepdims=True))
    normalized_rows = low(mean_removed * lax.rsqrt(variance + epsilon) * layernorm_gain + layernorm_bias)
    row_count = block_rows.shape[0]
    seq_count = block_segments.shape[0]
    length = block_segments.shape[1]
    linear = jnp.einsum('td,dce->tce', normalized_rows, w_qkv, precision=highest) + b_qkv
    linear = low_back(linear).reshape(seq_count, length, 3, HEADS, HEAD_DIM)
    cos_table, sin_table, allowed = rotary_tables(block_segments)
    score_scale = HEAD_DIM ** (-0.5)
    queries = low(rotate_heads(linear[:, :, 0], cos_table, sin_table) * score_scale)
    keys_rot = low(rotate_heads(linear[:, :, 1], cos_table, sin_table))
    values = low(linear[:, :, 2])
    scores = low_back(jnp.einsum('bqhe,bkhe->bhqk', queries, keys_rot, precision=highest))
    scores = jnp.where(allowed[:, None], scores, -1000000000.0)
    attn_probs = low(jax.nn.softmax(scores, axis=-1))
    attended = jnp.einsum('bhqk,bkhe->bqhe', attn_probs, values, precision=highest)
    attended = low_back(low(attended.reshape(row_count, HEADS * HEAD_DIM)))
    up_proj = low_back(jnp.dot(normalized_rows, w_up, precision=highest) + b_up)
    activated = low(jax.nn.gelu(up_proj, approximate=True))
    branches = jnp.dot(attended, w_out, precision=highest) + jnp.dot(activated, w_down, precision=highest)
    return block_rows + branches + b_out + b_down

def forward(tokens_f, segments, params):
    seq_count = TOKENS // SEQ
    per_block = math.gcd(max(4096 // SEQ, 1), seq_count)
    blocks = seq_count // per_block
    block_rows = tokens_f.reshape(blocks, per_block * SEQ, D)
    block_segments = segments.reshape(blocks, per_block, SEQ)
    checked = jax.checkpoint(block_forward)

    def run_block(block_item):
        return checked(params, block_item[0], block_item[1])
    outputs = lax.map(run_block, (block_rows, block_segments))
    return outputs.reshape(TOKENS, D)

def reference(tokens, layernorm_gain, layernorm_bias, w_qkv, b_qkv, w_out, b_out, w_up, b_up, w_down, b_down, segments, cotangent):
    floats = tuple((array.astype(jnp.float32) for array in (tokens, layernorm_gain, layernorm_bias, w_qkv, b_qkv, w_out, b_out, w_up, b_up, w_down, b_down)))

    def wrapped(*inputs):
        return forward(inputs[0], segments, inputs[1:])
    mixed, pullback = jax.vjp(wrapped, *floats)
    gradients = pullback(cotangent.astype(jnp.float32))
    return (mixed.astype(jnp.bfloat16), gradients[0], gradients[1], gradients[2], gradients[3], gradients[4], gradients[5], gradients[6], gradients[7], gradients[8], gradients[9], gradients[10])
```

```python
from functools import partial

import jax
import jax.numpy as jnp
from jax import lax
from jax.experimental import pallas as pl
from jax.experimental.pallas import tpu as pltpu
from jax.sharding import Mesh, PartitionSpec as P

HEAD_DIM = 64
ROT = 32
HALF = ROT // 2
LANES = 128
EPSILON = 1e-05

AXES = ("zl", "x", "y", "c", "mp")
SIZES = (2, 4, 4, 2, 2)
PLANE = ("x", "y")
PAIR = ("zl", "c")

BF16 = jnp.bfloat16
F32 = jnp.float32


def flip(value, *axes):
    count = 2 ** len(axes)
    return lax.ppermute(value, axes, [(i, count - 1 - i) for i in range(count)])


def hop(value, axis, bits):
    return lax.ppermute(value, axis, [(i, i ^ bits) for i in range(4)])


def gather_group(rows):
    half = jnp.concatenate([rows, flip(rows, "mp"), flip(rows, "zl"), flip(rows, "zl", "mp")], axis=0)
    return jnp.concatenate([half, flip(half, "c")], axis=0)


def scatter_group(partial_rows):
    rows = partial_rows.shape[0] // 8
    mine, theirs = partial_rows[: 4 * rows], partial_rows[4 * rows :]
    half = mine.astype(F32) + flip(theirs.astype(BF16), "c").astype(F32)
    low = half.astype(BF16)
    return (
        half[:rows]
        + flip(low[rows : 2 * rows], "mp").astype(F32)
        + flip(low[2 * rows : 3 * rows], "zl").astype(F32)
        + flip(low[3 * rows :], "zl", "mp").astype(F32)
    )


def sum_everywhere(vector):
    vector = vector + flip(vector, "c")
    vector = vector + flip(vector, "zl") + (flip(vector, "mp") + flip(vector, "zl", "mp"))
    for axis in PLANE:
        vector = (vector + hop(vector, axis, 2)) + (hop(vector, axis, 1) + hop(vector, axis, 3))
    return vector


def attention_kernel(
    linear_ref,
    grad_ref,
    cos_ref,
    low_ref,
    high_ref,
    segment_col,
    segment_row,
    index_col,
    index_row,
    attended_ref,
    grad_linear_ref,
    query_ref,
    key_ref,
    value_ref,
    grad_query_ref,
    grad_key_ref,
):
    width = grad_ref.shape[1]
    scale = HEAD_DIM ** (-0.5)

    def rotated(tile, lanes, sign):
        cos, low, high = cos_ref[...], low_ref[...], high_ref[...]
        ahead = pltpu.roll(tile, lanes - HALF, 1)
        behind = pltpu.roll(tile, HALF, 1)
        return tile * cos + (ahead * low + behind * high) * sign

    for start in range(0, width, LANES):
        lanes = slice(start, start + LANES)
        query_ref[:, lanes] = (rotated(linear_ref[:, lanes], LANES, 1.0) * scale).astype(BF16)
        keys = linear_ref[:, width + start : width + start + LANES]
        key_ref[:, lanes] = rotated(keys, LANES, 1.0).astype(BF16)
        value_ref[:, lanes] = linear_ref[:, 2 * width + start : 2 * width + start + LANES].astype(BF16)
    allowed = (segment_col[...] == segment_row[0]) & (index_col[...] >= index_row[0])
    for start in range(0, width, HEAD_DIM):
        lanes = slice(start, start + HEAD_DIM)
        query, key, value = query_ref[:, lanes], key_ref[:, lanes], value_ref[:, lanes]
        grad = grad_ref[:, lanes]
        scores = lax.dot_general(query, key, (((1,), (1,)), ((), ())), preferred_element_type=F32)
        scores = jnp.where(allowed, scores, -1000000000.0)
        expo = jnp.exp(scores - jnp.max(scores, axis=1, keepdims=True))
        probs = expo / jnp.sum(expo, axis=1, keepdims=True)
        low_probs = probs.astype(BF16)
        attended_ref[:, lanes] = jnp.dot(low_probs, value, preferred_element_type=F32).astype(BF16)
        grad_probs = lax.dot_general(grad, value, (((1,), (1,)), ((), ())), preferred_element_type=F32)
        grad_values = lax.dot_general(
            low_probs, grad, (((0,), (0,)), ((), ())), preferred_element_type=F32
        )
        weighted = probs * grad_probs
        delta = jnp.sum(weighted, axis=1, keepdims=True)
        grad_scores = (weighted - probs * delta).astype(BF16)
        grad_query_ref[:, lanes] = jnp.dot(grad_scores, key, preferred_element_type=F32) * scale
        grad_key_ref[:, lanes] = lax.dot_general(
            grad_scores, query, (((0,), (0,)), ((), ())), preferred_element_type=F32
        )
        grad_linear_ref[:, 2 * width + start : 2 * width + start + HEAD_DIM] = grad_values.astype(BF16)
    for start in range(0, width, LANES):
        lanes = slice(start, start + LANES)
        grad_linear_ref[:, lanes] = rotated(grad_query_ref[:, lanes], LANES, -1.0).astype(BF16)
        grad_linear_ref[:, width + start : width + start + LANES] = rotated(
            grad_key_ref[:, lanes], LANES, -1.0
        ).astype(BF16)


def attention(linear, grad_attended, tables, segments, indices, length):
    rows, width = grad_attended.shape
    count = rows // length
    blocks = lambda lanes: pl.BlockSpec((length, lanes), lambda i: (i, 0))
    rowwise = pl.BlockSpec((1, 1, length), lambda i: (i, 0, 0))
    return pl.pallas_call(
        attention_kernel,
        grid=(count,),
        in_specs=[
            blocks(3 * width),
            blocks(width),
            blocks(LANES),
            blocks(LANES),
            blocks(LANES),
            blocks(1),
            rowwise,
            blocks(1),
            rowwise,
        ],
        out_specs=[blocks(width), blocks(3 * width)],
        out_shape=[
            jax.ShapeDtypeStruct((rows, width), BF16),
            jax.ShapeDtypeStruct((rows, 3 * width), BF16),
        ],
        scratch_shapes=[pltpu.VMEM((length, width), BF16)] * 3
        + [pltpu.VMEM((length, width), F32)] * 2,
        compiler_params=pltpu.CompilerParams(vmem_limit_bytes=32 * 1024 * 1024),
        name="attention",
    )(
        linear,
        grad_attended,
        *tables,
        segments.reshape(rows, 1),
        segments.reshape(count, 1, length),
        indices.reshape(rows, 1),
        indices.reshape(count, 1, length),
    )


def gather_weights(shard):
    rows, columns = shard.shape
    whole = lax.all_gather(shard, PLANE, axis=0, tiled=False)
    whole = whole.reshape(16, 2, rows // 2, columns).transpose(1, 0, 2, 3)
    return whole.reshape(16 * rows, columns)


def scatter_weights(grads):
    rows, columns = grads.shape
    pieces = grads.astype(BF16).reshape(2, 16, rows // 32, columns).transpose(1, 0, 2, 3)
    mine = lax.psum_scatter(pieces.reshape(rows, columns), PLANE, scatter_dimension=0, tiled=True)
    return mine


def to_slices(shard, axis):
    return lax.all_to_all(shard, PAIR, axis, 0, tiled=True)


def from_slices(shard, axis):
    return lax.all_to_all(shard, PAIR, 0, axis, tiled=True)


def per_device(
    tokens,
    layernorm_gain,
    layernorm_bias,
    w_qkv,
    b_qkv,
    w_out,
    b_out,
    w_up,
    b_up,
    w_down,
    b_down,
    segments,
    cotangent,
):
    depth = tokens.shape[1]
    length = segments.shape[0]
    half_rows = tokens.shape[0]
    width = w_out.shape[0] // 4
    hidden = w_down.shape[0] // 4
    place = lax.axis_index("zl") * 2 + lax.axis_index("c")

    inputs_f = tokens.astype(F32)
    row_mean = jnp.mean(inputs_f, axis=-1, keepdims=True)
    mean_removed = inputs_f - row_mean
    variance = jnp.mean(mean_removed * mean_removed, axis=-1, keepdims=True)
    inverse_deviation = lax.rsqrt(variance + EPSILON)
    standardized_input = mean_removed * inverse_deviation
    normalized_rows = (standardized_input * layernorm_gain + layernorm_bias).astype(BF16)

    up_shard = to_slices(w_up, 1)
    down_shard = to_slices(w_down.T, 1)
    qkv_shard = to_slices(w_qkv, 2).reshape(-1, 3 * width)
    out_shard = to_slices(w_out.T, 1)

    sequence = gather_group(normalized_rows)
    cot_seq = gather_group(cotangent)

    mlp_weights = gather_weights(jnp.concatenate([up_shard, down_shard], axis=1))
    attention_weights = gather_weights(jnp.concatenate([qkv_shard, out_shard], axis=1))
    up_w, down_w = mlp_weights[:, :hidden], mlp_weights[:, hidden:]
    qkv_w, out_w = attention_weights[:, : 3 * width], attention_weights[:, 3 * width :]

    doc = flip_pair(segments).reshape(4, 2, half_rows)
    this_half = lax.axis_index("mp")
    doc = jnp.where(this_half == 0, doc, doc[:, ::-1]).reshape(4, length)
    halves = jnp.stack([this_half, 1 - this_half]) * half_rows
    index = (halves[:, None] + jnp.arange(half_rows, dtype=jnp.int32)).reshape(1, length)
    index = jnp.broadcast_to(index, (4, length)).astype(jnp.int32)
    same_doc = doc[:, :, None] == doc[:, None, :]
    doc_start = jnp.min(jnp.where(same_doc, index[:, None, :], length), axis=2)
    positions = (index - doc_start).astype(F32).reshape(-1)
    inv_freq = 10000.0 ** (-(jnp.arange(HALF, dtype=F32) * 2.0 / ROT))
    angles = positions[:, None] * inv_freq
    cos, sin = jnp.cos(angles), jnp.sin(angles)
    nothing = jnp.zeros_like(cos)
    rest = (positions.shape[0], HEAD_DIM - ROT)
    repeat = LANES // HEAD_DIM
    cos_table = jnp.tile(jnp.concatenate([cos, cos, jnp.ones(rest, F32)], axis=1), (1, repeat))
    low_table = jnp.tile(jnp.concatenate([-sin, nothing, jnp.zeros(rest, F32)], axis=1), (1, repeat))
    high_table = jnp.tile(jnp.concatenate([nothing, sin, jnp.zeros(rest, F32)], axis=1), (1, repeat))

    b_up_here = lax.dynamic_slice_in_dim(b_up, place * hidden, hidden)
    b_qkv_here = lax.dynamic_slice_in_dim(b_qkv, place * width, width, axis=1).reshape(-1)

    up_proj = jnp.dot(sequence, up_w, preferred_element_type=F32) + b_up_here
    activated, gelu_pull = jax.vjp(partial(jax.nn.gelu, approximate=True), up_proj)
    activated = activated.astype(BF16)
    grad_act = jnp.dot(cot_seq, down_w, preferred_element_type=F32)
    grad_up = gelu_pull(grad_act)[0].astype(BF16)
    grad_down_w = jnp.einsum("td,tf->df", cot_seq, activated, preferred_element_type=F32)
    grad_up_w = jnp.einsum("td,tf->df", sequence, grad_up, preferred_element_type=F32)
    mlp_grads = scatter_weights(jnp.concatenate([grad_up_w, grad_down_w], axis=1))

    linear = jnp.dot(sequence, qkv_w, preferred_element_type=F32) + b_qkv_here
    grad_attended = jnp.dot(cot_seq, out_w, preferred_element_type=F32).astype(BF16)
    attended, grad_linear = attention(
        linear, grad_attended, (cos_table, low_table, high_table), doc, index, length
    )
    grad_out_w = jnp.einsum("td,te->de", cot_seq, attended, preferred_element_type=F32)
    grad_qkv_w = jnp.einsum("td,te->de", sequence, grad_linear, preferred_element_type=F32)
    attention_grads = scatter_weights(jnp.concatenate([grad_qkv_w, grad_out_w], axis=1))

    branches = jnp.einsum("te,de->td", attended, out_w, preferred_element_type=F32) + jnp.einsum(
        "tf,df->td", activated, down_w, preferred_element_type=F32
    )
    mixed = (inputs_f + scatter_group(branches) + b_out + b_down).astype(BF16)
    grad_sequence = jnp.einsum(
        "te,de->td", grad_linear, qkv_w, preferred_element_type=F32
    ) + jnp.einsum("tf,df->td", grad_up, up_w, preferred_element_type=F32)
    normalized_gradient = scatter_group(grad_sequence)
    standardized_gradient = normalized_gradient * layernorm_gain
    grad_inputs = inverse_deviation * (
        standardized_gradient
        - jnp.mean(standardized_gradient, axis=-1, keepdims=True)
        - standardized_input
        * jnp.mean(standardized_gradient * standardized_input, axis=-1, keepdims=True)
    )
    cot_rows = cotangent.astype(F32)
    d_tokens = cot_rows + grad_inputs

    slices = jnp.concatenate(
        [
            jnp.sum(grad_linear.astype(F32), axis=0),
            jnp.sum(grad_up.astype(F32), axis=0),
        ]
    )
    slot = this_half * 4 + place
    spread = jnp.zeros((8,) + slices.shape, F32)
    spread = lax.dynamic_update_slice(spread, slices[None], (slot, 0))
    vector = jnp.concatenate(
        [
            spread.reshape(-1),
            jnp.sum(cot_rows, axis=0),
            jnp.sum(normalized_gradient * standardized_input, axis=0),
            jnp.sum(normalized_gradient, axis=0),
        ]
    )
    vector = sum_everywhere(vector.reshape(-1, LANES)).reshape(-1)
    spread, whole = vector[: spread.size].reshape(8, -1), vector[spread.size :].reshape(3, depth)
    spread = lax.dynamic_slice_in_dim(spread, this_half * 4, 4)
    grad_b_qkv = spread[:, : 3 * width].reshape(4, 3, width).transpose(1, 0, 2).reshape(3, 4 * width)
    grad_b_up = spread[:, 3 * width :].reshape(-1)

    grad_up_w = from_slices(mlp_grads[:, :hidden], 1).astype(F32)
    grad_down_w = from_slices(mlp_grads[:, hidden:], 1).astype(F32).T
    grad_qkv_w = from_slices(attention_grads[:, : 3 * width].reshape(-1, 3, width), 2).astype(F32)
    grad_out_w = from_slices(attention_grads[:, 3 * width :], 1).astype(F32).T
    return (
        mixed,
        d_tokens,
        whole[1],
        whole[2],
        grad_qkv_w,
        grad_b_qkv,
        grad_out_w,
        whole[0],
        grad_up_w,
        grad_b_up,
        grad_down_w,
        whole[0],
    )


def flip_pair(segments):
    half = jnp.stack([segments, flip(segments, "zl")])
    return jnp.concatenate([half, flip(half, "c")])


def solution(mesh):
    fine = Mesh(mesh.devices.reshape(SIZES), AXES)
    dp = ("zl", "x", "y", "c")
    in_specs = (
        P(AXES, None),
        P(),
        P(),
        P(dp, None, "mp"),
        P(None, "mp"),
        P("mp", dp),
        P(),
        P(dp, "mp"),
        P("mp"),
        P("mp", dp),
        P(),
        P(dp),
        P(AXES, None),
    )
    out_specs = (
        P(AXES, None),
        P(AXES, None),
        P(),
        P(),
        P(dp, None, "mp"),
        P(None, "mp"),
        P("mp", dp),
        P(),
        P(dp, "mp"),
        P("mp"),
        P("mp", dp),
        P(),
    )
    return jax.shard_map(
        per_device, mesh=fine, in_specs=in_specs, out_specs=out_specs, check_vma=False
    )
```

```python
import jax
import jax.numpy as jnp
from jax import lax
from jax.experimental import pallas as pl
from jax.experimental.pallas import tpu as pltpu
from jax.sharding import Mesh, PartitionSpec as P

HEAD_DIM = 64
ROT = 32
HALF = ROT // 2
LANES = 128
EPSILON = 1e-05

AXES = ("zl", "x", "y", "c", "mp")
SIZES = (2, 4, 4, 2, 2)
PLANE = ("x", "y")
PAIR = ("zl", "c")

BF16 = jnp.bfloat16
F32 = jnp.float32


def flip(value, *axes):
    count = 2 ** len(axes)
    return lax.ppermute(value, axes, [(i, count - 1 - i) for i in range(count)])


def hop(value, axis, bits):
    return lax.ppermute(value, axis, [(i, i ^ bits) for i in range(4)])


def scatter_group(partial_rows):
    rows = partial_rows.shape[0] // 8
    mine, theirs = partial_rows[: 4 * rows], partial_rows[4 * rows :]
    half = mine.astype(F32) + flip(theirs.astype(BF16), "c").astype(F32)
    low = half.astype(BF16)
    return (
        half[:rows]
        + flip(low[rows : 2 * rows], "mp").astype(F32)
        + flip(low[2 * rows : 3 * rows], "zl").astype(F32)
        + flip(low[3 * rows :], "zl", "mp").astype(F32)
    )


def sum_everywhere(vector):
    vector = vector + flip(vector, "c")
    vector = vector + flip(vector, "zl") + (flip(vector, "mp") + flip(vector, "zl", "mp"))
    for axis in PLANE:
        vector = (vector + hop(vector, axis, 2)) + (hop(vector, axis, 1) + hop(vector, axis, 3))
    return vector


def attention_kernel(
    linear_ref,
    grad_ref,
    cos_ref,
    low_ref,
    high_ref,
    segment_col,
    segment_row,
    index_col,
    index_row,
    attended_ref,
    grad_linear_ref,
    query_ref,
    key_ref,
    value_ref,
    grad_query_ref,
    grad_key_ref,
):
    width = grad_ref.shape[1]
    scale = HEAD_DIM ** (-0.5)

    def rotated(tile, lanes, sign):
        cos, low, high = cos_ref[...], low_ref[...], high_ref[...]
        ahead = pltpu.roll(tile, lanes - HALF, 1)
        behind = pltpu.roll(tile, HALF, 1)
        return tile * cos + (ahead * low + behind * high) * sign

    for start in range(0, width, LANES):
        lanes = slice(start, start + LANES)
        query_ref[:, lanes] = (rotated(linear_ref[:, lanes], LANES, 1.0) * scale).astype(BF16)
        keys = linear_ref[:, width + start : width + start + LANES]
        key_ref[:, lanes] = rotated(keys, LANES, 1.0).astype(BF16)
        value_ref[:, lanes] = linear_ref[:, 2 * width + start : 2 * width + start + LANES].astype(BF16)
    allowed = (segment_col[...] == segment_row[0]) & (index_col[...] >= index_row[0])
    for start in range(0, width, HEAD_DIM):
        lanes = slice(start, start + HEAD_DIM)
        query, key, value = query_ref[:, lanes], key_ref[:, lanes], value_ref[:, lanes]
        grad = grad_ref[:, lanes]
        scores = lax.dot_general(query, key, (((1,), (1,)), ((), ())), preferred_element_type=F32)
        scores = jnp.where(allowed, scores, -1000000000.0)
        expo = jnp.exp(scores - jnp.max(scores, axis=1, keepdims=True))
        probs = expo / jnp.sum(expo, axis=1, keepdims=True)
        low_probs = probs.astype(BF16)
        attended_ref[:, lanes] = jnp.dot(low_probs, value, preferred_element_type=F32).astype(BF16)
        grad_probs = lax.dot_general(grad, value, (((1,), (1,)), ((), ())), preferred_element_type=F32)
        grad_values = lax.dot_general(
            low_probs, grad, (((0,), (0,)), ((), ())), preferred_element_type=F32
        )
        weighted = probs * grad_probs
        delta = jnp.sum(weighted, axis=1, keepdims=True)
        grad_scores = (weighted - probs * delta).astype(BF16)
        grad_query_ref[:, lanes] = jnp.dot(grad_scores, key, preferred_element_type=F32) * scale
        grad_key_ref[:, lanes] = lax.dot_general(
            grad_scores, query, (((0,), (0,)), ((), ())), preferred_element_type=F32
        )
        grad_linear_ref[:, 2 * width + start : 2 * width + start + HEAD_DIM] = grad_values.astype(BF16)
    for start in range(0, width, LANES):
        lanes = slice(start, start + LANES)
        grad_linear_ref[:, lanes] = rotated(grad_query_ref[:, lanes], LANES, -1.0).astype(BF16)
        grad_linear_ref[:, width + start : width + start + LANES] = rotated(
            grad_key_ref[:, lanes], LANES, -1.0
        ).astype(BF16)


def attention(linear, grad_attended, tables, segments, indices, length):
    rows, width = grad_attended.shape
    count = rows // length
    blocks = lambda lanes: pl.BlockSpec((length, lanes), lambda i: (i, 0))
    rowwise = pl.BlockSpec((1, 1, length), lambda i: (i, 0, 0))
    return pl.pallas_call(
        attention_kernel,
        grid=(count,),
        in_specs=[
            blocks(3 * width),
            blocks(width),
            blocks(LANES),
            blocks(LANES),
            blocks(LANES),
            blocks(1),
            rowwise,
            blocks(1),
            rowwise,
        ],
        out_specs=[blocks(width), blocks(3 * width)],
        out_shape=[
            jax.ShapeDtypeStruct((rows, width), BF16),
            jax.ShapeDtypeStruct((rows, 3 * width), BF16),
        ],
        scratch_shapes=[pltpu.VMEM((length, width), BF16)] * 3
        + [pltpu.VMEM((length, width), F32)] * 2,
        compiler_params=pltpu.CompilerParams(vmem_limit_bytes=32 * 1024 * 1024),
        name="attention",
    )(
        linear,
        grad_attended,
        *tables,
        segments.reshape(rows, 1),
        segments.reshape(count, 1, length),
        indices.reshape(rows, 1),
        indices.reshape(count, 1, length),
    )


MIB = 1024 * 1024
ANY = pl.BlockSpec(memory_space=pl.ANY)
WHOLE = pl.BlockSpec(memory_space=pltpu.VMEM)
SCALARS = pl.BlockSpec(memory_space=pltpu.SMEM)


def like(shape, dtype=BF16):
    return jax.ShapeDtypeStruct(shape, dtype)


def params(mib):
    return pltpu.CompilerParams(vmem_limit_bytes=mib * MIB)


def cost(flops, moved):
    return pl.CostEstimate(flops=flops, bytes_accessed=moved, transcendentals=0)


def slot_of(coords, bits):
    return (coords[0] * 2 + coords[3]) ^ bits


def pack_kernel(coords, up_ref, down_ref, qkv_ref, out_ref, segment_ref, *parts):
    hidden, width = up_ref.shape[1] // 4, out_ref.shape[1] // 4
    rows = up_ref.shape[0]
    segments = segment_ref[...].astype(F32).astype(BF16)
    for bits in range(4):
        slot = slot_of(coords, bits)
        wide = pl.ds(pl.multiple_of(slot * hidden, hidden), hidden)
        narrow = pl.ds(pl.multiple_of(slot * width, width), width)
        mlp, heads = parts[2 * bits], parts[2 * bits + 1]
        mlp[:, :hidden] = up_ref[:, wide]
        mlp[:, hidden:] = down_ref[:, wide]
        for kind in range(3):
            heads[:rows, kind * width : (kind + 1) * width] = qkv_ref[kind, :, narrow]
        heads[:rows, 3 * width :] = out_ref[:, narrow]
        heads[rows:, :] = jnp.zeros((16, 4 * width), BF16)
        heads[rows:, : segments.shape[1]] = jnp.broadcast_to(segments, (16, segments.shape[1]))


def pack(coords, w_up, down_t, qkv_t, out_t, segments):
    rows, hidden, width = w_up.shape[0], w_up.shape[1] // 4, out_t.shape[1] // 4
    shapes = [like((rows, 2 * hidden)), like((rows + 16, 4 * width))] * 4
    return pl.pallas_call(
        pack_kernel,
        in_specs=[SCALARS] + [WHOLE] * 5,
        out_specs=[WHOLE] * 8,
        out_shape=shapes,
        compiler_params=params(16),
        name="pack",
    )(coords, w_up, down_t, qkv_t, out_t, segments.reshape(1, -1))


def order_kernel(coords, *refs):
    parts, outs = refs[:4], refs[4:]
    for bits in range(4):
        zl, c = coords[0] ^ (bits >> 1), coords[3] ^ (bits & 1)
        start = 0
        for out in outs:
            columns = out.shape[3]
            out[zl, c] = parts[bits][: out.shape[2], start : start + columns]
            start += columns


def order(coords, parts, columns, rows):
    return pl.pallas_call(
        order_kernel,
        in_specs=[SCALARS] + [WHOLE] * 4,
        out_specs=[WHOLE] * len(columns),
        out_shape=[like((2, 2, rows, count)) for count in columns],
        compiler_params=params(16),
        name="order",
    )(coords, *parts)


def join_kernel(*refs):
    parts, out, sem = refs[:-2], refs[-2], refs[-1]
    copies = []
    for i, part in enumerate(parts):
        copies.append(pltpu.make_async_copy(part, out.at[i], sem.at[i]))
        copies[-1].start()
    for copy in copies:
        copy.wait()


def join(*parts):
    return pl.pallas_call(
        join_kernel,
        in_specs=[ANY] * len(parts),
        out_specs=ANY,
        out_shape=like((len(parts),) + parts[0].shape),
        scratch_shapes=[pltpu.SemaphoreType.DMA((len(parts),))],
        compiler_params=params(16),
        name="join",
    )(*parts)


def gather_plane(shard, first, second):
    row = join(shard, hop(shard, first, 1), hop(shard, first, 2), hop(shard, first, 3))
    one, three = hop(row, second, 1), hop(row, second, 3)
    half = row.shape[0] // 2
    two_low, two_high = hop(three[:half], second, 1), hop(one[half:], second, 3)
    return row, one, two_low, two_high, three


def tokens_kernel(mine_ref, other_ref, rows_ref, columns_ref):
    @pl.when(pl.program_id(1) == 0)
    def _():
        rows_ref[0] = mine_ref[0, 0]
        columns_ref[0] = mine_ref[0, 0].T

    @pl.when(pl.program_id(1) == 1)
    def _():
        rows_ref[0] = other_ref[0, 0]
        columns_ref[0] = other_ref[0, 0].T


def gather_tokens(pair):
    near, far = flip(pair, "zl"), flip(pair, "zl", "mp")
    middle = join(flip(far[0], "zl"), flip(near[1], "zl", "mp"))
    mine = join(pair, middle, near, far)
    other = flip(mine, "c")
    _, _, rows, depth = mine.shape
    block = (1, 1, rows, depth)
    return pl.pallas_call(
        tokens_kernel,
        grid=(2, 2, 4),
        in_specs=[
            pl.BlockSpec(block, lambda w, c, z: (jnp.where(c == 0, z, 3), w, 0, 0)),
            pl.BlockSpec(block, lambda w, c, z: (jnp.where(c == 1, z, 0), w, 0, 0)),
        ],
        out_specs=[
            pl.BlockSpec((1, rows, depth), lambda w, c, z: (w, 4 * c + z, 0)),
            pl.BlockSpec((1, depth, rows), lambda w, c, z: (w, 0, 4 * c + z)),
        ],
        out_shape=[like((2, 8 * rows, depth)), like((2, depth, 8 * rows))],
        compiler_params=params(32),
        cost_estimate=cost(0, 8 * mine.size * 2),
        name="tokens",
    )(mine, other)


def mlp_kernel(coords, pair_ref, bias_ref, *refs):
    up_parts, down_parts = refs[:5], refs[5:10]
    hidden_ref, sums_ref, up_out, down_out = refs[10:14]
    rows_ref, up_ref, down_ref, sems = refs[14:]
    x, y = coords[1], coords[2]
    block = up_ref.shape[0] // 32

    def load(parts, target, sems, second_is_y):
        copies = []
        row, one, two_low, two_high, three = parts
        for second in range(4):
            for first in range(4):
                if second == 2:
                    source = two_low.at[first] if first < 2 else two_high.at[first - 2]
                else:
                    source = (row, one, None, three)[second].at[first]
                if second_is_y:
                    place = (x ^ first) * 4 + (y ^ second)
                else:
                    place = (x ^ second) * 4 + (y ^ first)
                for zl in range(2):
                    target_rows = pl.ds(pl.multiple_of((zl * 16 + place) * block, block), block)
                    sem = sems.at[len(copies)]
                    copies.append(pltpu.make_async_copy(source.at[zl], target.at[target_rows], sem))
        return copies

    first = [pltpu.make_async_copy(pair_ref.at[0], rows_ref.at[0], sems.at[0, 32])]
    first += load(up_parts, up_ref, sems.at[0], True)
    second = [pltpu.make_async_copy(pair_ref.at[1], rows_ref.at[1], sems.at[1, 32])]
    second += load(down_parts, down_ref, sems.at[1], False)
    for copy in first + second:
        copy.start()
    for copy in first:
        copy.wait()
    for copy in second:
        copy.wait()
    up_back = pltpu.make_async_copy(up_ref, up_out, sems.at[0, 33])
    down_back = pltpu.make_async_copy(down_ref, down_out, sems.at[1, 33])
    up_back.start()
    down_back.start()
    tile = 256
    slope = 0.7978845608028654

    def body(j, carry):
        lanes = pl.ds(pl.multiple_of(j * tile, tile), tile)
        up = jnp.dot(rows_ref[0], up_ref[:, lanes], preferred_element_type=F32) + bias_ref[:, lanes]
        square = up * up
        wave = jnp.tanh(slope * (up + 0.044715 * (square * up)))
        half = 0.5 * (1.0 + wave)
        hidden_ref[1, :, lanes] = (up * half).astype(BF16)
        rise = half + (0.5 * up) * (1.0 - wave * wave) * (slope * (1.0 + 0.134145 * square))
        grad = jnp.dot(rows_ref[1], down_ref[:, lanes], preferred_element_type=F32) * rise
        low = grad.astype(BF16)
        hidden_ref[0, :, lanes] = low
        sums_ref[:, lanes] = jnp.sum(low.astype(F32), axis=0, keepdims=True)
        return carry

    lax.fori_loop(0, up_ref.shape[1] // tile, body, 0)
    up_back.wait()
    down_back.wait()


def mlp(coords, pair, bias, up_parts, down_parts):
    rows, depth = pair.shape[1:]
    hidden = bias.shape[0]
    return pl.pallas_call(
        mlp_kernel,
        in_specs=[SCALARS, ANY, WHOLE] + [ANY] * 10,
        out_specs=[WHOLE, WHOLE, ANY, ANY],
        out_shape=[
            like((2, rows, hidden)),
            like((1, hidden), F32),
            like((depth, hidden)),
            like((depth, hidden)),
        ],
        scratch_shapes=[
            pltpu.VMEM((2, rows, depth), BF16),
            pltpu.VMEM((depth, hidden), BF16),
            pltpu.VMEM((depth, hidden), BF16),
            pltpu.SemaphoreType.DMA((2, 34)),
        ],
        compiler_params=params(48),
        cost_estimate=cost(4 * rows * depth * hidden, 24 * MIB),
        name="mlp",
    )(coords, pair, bias.reshape(1, -1), *up_parts, *down_parts)


def grads_kernel(left_ref, right_ref, out_ref):
    product = jnp.dot(left_ref[0], right_ref[0], preferred_element_type=F32).astype(BF16)
    out_ref[...] = product.reshape(out_ref.shape)


def weight_grads(pair_t, right, tile, which):
    _, depth, rows = pair_t.shape
    count, _, columns = right.shape
    tiles = columns // tile
    block = depth // 32
    return pl.pallas_call(
        grads_kernel,
        grid=(count, tiles, 2),
        in_specs=[
            pl.BlockSpec((1, depth // 2, rows), lambda i, j, zl: (which(i, j), zl, 0)),
            pl.BlockSpec((1, rows, tile), lambda i, j, zl: (i, 0, j)),
        ],
        out_specs=pl.BlockSpec((16, 1, block, tile), lambda i, j, zl: (0, zl, 0, i * tiles + j)),
        out_shape=like((16, 2, block, count * columns)),
        compiler_params=params(40),
        cost_estimate=cost(2 * depth * rows * count * columns, 2 * (pair_t.size + right.size * 2)),
        name="weight_grads",
    )(pair_t, right)


def project_kernel(pair_ref, bias_ref, weights_ref, linear_ref, grad_ref, order_ref):
    width = grad_ref.shape[1]
    columns = weights_ref[...].astype(BF16)
    columns = jnp.swapaxes(columns, 0, 1).reshape(order_ref.shape)
    order_ref[...] = columns

    @pl.when(pl.program_id(0) < 3)
    def _():
        linear_ref[...] = jnp.dot(pair_ref[0], columns, preferred_element_type=F32) + bias_ref[...]

    @pl.when(pl.program_id(0) == 3)
    def _():
        grad_ref[...] = jnp.dot(pair_ref[0], columns, preferred_element_type=F32).astype(BF16)


def project(pair, bias, weights):
    rows, depth = pair.shape[1:]
    block, width = depth // 32, weights.shape[3] // 4
    return pl.pallas_call(
        project_kernel,
        grid=(4,),
        in_specs=[
            pl.BlockSpec((1, rows, depth), lambda j: (j // 3, 0, 0)),
            pl.BlockSpec((1, width), lambda j: (0, jnp.minimum(j, 2))),
            pl.BlockSpec((16, 2, block, width), lambda j: (0, 0, 0, j)),
        ],
        out_specs=[
            pl.BlockSpec((rows, width), lambda j: (0, jnp.minimum(j, 2))),
            pl.BlockSpec((rows, width), lambda j: (0, 0)),
            pl.BlockSpec((depth, width), lambda j: (0, j)),
        ],
        out_shape=[
            like((rows, 3 * width), F32),
            like((rows, width)),
            like((depth, 4 * width)),
        ],
        compiler_params=params(40),
        cost_estimate=cost(8 * rows * depth * width, 16 * MIB),
        name="project",
    )(pair, bias.reshape(1, -1), weights)


def cut_kernel(coords, whole_ref, *outs):
    for bits in range(4):
        outs[bits][...] = whole_ref[slot_of(coords, bits)]


def cut(coords, whole):
    return pl.pallas_call(
        cut_kernel,
        in_specs=[SCALARS, WHOLE],
        out_specs=[WHOLE] * 4,
        out_shape=[like(whole.shape[1:])] * 4,
        compiler_params=params(16),
        name="cut",
    )(coords, whole)


def exchange(parts):
    return [parts[0], flip(parts[1], "c"), flip(parts[2], "zl"), flip(parts[3], "zl", "c")]


def unpack_mlp_kernel(coords, *refs):
    parts, (up_ref, down_ref) = refs[:4], refs[4:]
    hidden = up_ref.shape[1] // 4
    for bits in range(4):
        lanes = pl.ds(pl.multiple_of(slot_of(coords, bits) * hidden, hidden), hidden)
        up_ref[:, lanes] = parts[bits][:, :hidden].astype(F32)
        down_ref[:, lanes] = parts[bits][:, hidden:].astype(F32)


def unpack_heads_kernel(coords, *refs):
    parts, (qkv_ref, out_ref) = refs[:4], refs[4:]
    width = out_ref.shape[1] // 4
    for bits in range(4):
        lanes = pl.ds(pl.multiple_of(slot_of(coords, bits) * width, width), width)
        for kind in range(3):
            qkv_ref[kind, :, lanes] = parts[bits][:, kind * width : (kind + 1) * width].astype(F32)
        out_ref[:, lanes] = parts[bits][:, 3 * width :].astype(F32)


def unpack(coords, kernel, parts, shapes, name):
    return pl.pallas_call(
        kernel,
        in_specs=[SCALARS] + [WHOLE] * 4,
        out_specs=[WHOLE] * 2,
        out_shape=[like(shape, F32) for shape in shapes],
        compiler_params=params(16),
        name=name,
    )(coords, *parts)


def scatter_plane(grads):
    return lax.psum_scatter(grads.reshape(-1, grads.shape[3]), PLANE, scatter_dimension=0, tiled=True)


def per_device(
    tokens,
    layernorm_gain,
    layernorm_bias,
    w_qkv,
    b_qkv,
    w_out,
    b_out,
    w_up,
    b_up,
    w_down,
    b_down,
    segments,
    cotangent,
):
    depth = tokens.shape[1]
    length = segments.shape[0]
    half_rows = tokens.shape[0]
    width = w_out.shape[0] // 4
    hidden = w_down.shape[0] // 4
    rows = w_up.shape[0]
    coords = jnp.stack([lax.axis_index(axis) for axis in AXES]).astype(jnp.int32)
    place = coords[0] * 2 + coords[3]
    this_half = coords[4]

    packed = pack(coords, w_up, w_down.T, w_qkv.transpose(1, 0, 2), w_out.T, segments)
    mlp_parts, head_parts = exchange(packed[0::2]), exchange(packed[1::2])
    up_shard, down_shard = order(coords, mlp_parts, (hidden, hidden), rows)
    (head_shard,) = order(coords, head_parts, (4 * width,), rows)

    inputs_f = tokens.astype(F32)
    row_mean = jnp.mean(inputs_f, axis=-1, keepdims=True)
    mean_removed = inputs_f - row_mean
    variance = jnp.mean(mean_removed * mean_removed, axis=-1, keepdims=True)
    inverse_deviation = lax.rsqrt(variance + EPSILON)
    standardized_input = mean_removed * inverse_deviation
    normalized_rows = (standardized_input * layernorm_gain + layernorm_bias).astype(BF16)

    head_weights = lax.all_gather(head_shard.reshape(2, 2 * rows, 4 * width), PLANE, axis=0, tiled=False)
    head_weights = head_weights.reshape(16, 2, 2 * rows, 4 * width)
    pair, pair_t = gather_tokens(jnp.stack([normalized_rows, cotangent]))
    up_parts = gather_plane(up_shard.reshape(2, 2 * rows, hidden), "x", "y")
    down_parts = gather_plane(down_shard.reshape(2, 2 * rows, hidden), "y", "x")

    doc = jnp.stack([head_parts[k][rows, :length] for k in (0, 2, 1, 3)]).astype(jnp.int32)
    doc = doc.reshape(4, 2, half_rows)
    doc = jnp.where(this_half == 0, doc, doc[:, ::-1]).reshape(4, length)
    halves = jnp.stack([this_half, 1 - this_half]) * half_rows
    index = (halves[:, None] + jnp.arange(half_rows, dtype=jnp.int32)).reshape(1, length)
    index = jnp.broadcast_to(index, (4, length)).astype(jnp.int32)
    same_doc = doc[:, :, None] == doc[:, None, :]
    doc_start = jnp.min(jnp.where(same_doc, index[:, None, :], length), axis=2)
    positions = (index - doc_start).astype(F32).reshape(-1)
    inv_freq = 10000.0 ** (-(jnp.arange(HALF, dtype=F32) * 2.0 / ROT))
    angles = positions[:, None] * inv_freq
    cos, sin = jnp.cos(angles), jnp.sin(angles)
    nothing = jnp.zeros_like(cos)
    rest = (positions.shape[0], HEAD_DIM - ROT)
    repeat = LANES // HEAD_DIM
    cos_table = jnp.tile(jnp.concatenate([cos, cos, jnp.ones(rest, F32)], axis=1), (1, repeat))
    low_table = jnp.tile(jnp.concatenate([-sin, nothing, jnp.zeros(rest, F32)], axis=1), (1, repeat))
    high_table = jnp.tile(jnp.concatenate([nothing, sin, jnp.zeros(rest, F32)], axis=1), (1, repeat))

    b_up_here = lax.dynamic_slice_in_dim(b_up, place * hidden, hidden)
    b_qkv_here = lax.dynamic_slice_in_dim(b_qkv, place * width, width, axis=1).reshape(-1)

    hidden_pair, grad_b_up, up_w, down_w = mlp(coords, pair, b_up_here, up_parts, down_parts)
    mlp_grads = scatter_plane(weight_grads(pair_t, hidden_pair, hidden // 2, lambda i, j: i))

    linear, grad_attended, head_w = project(pair, b_qkv_here, head_weights)
    attended, grad_linear = attention(
        linear, grad_attended, (cos_table, low_table, high_table), doc, index, length
    )
    head_right = jnp.concatenate([grad_linear, attended], axis=1)[None]
    head_grads = scatter_plane(weight_grads(pair_t, head_right, width, lambda i, j: j // 3))

    out_w, qkv_w = head_w[:, 3 * width :], head_w[:, : 3 * width]
    branches = jnp.einsum("te,de->td", attended, out_w, preferred_element_type=F32) + jnp.einsum(
        "tf,df->td", hidden_pair[1], down_w, preferred_element_type=F32
    )
    mixed = (inputs_f + scatter_group(branches) + b_out + b_down).astype(BF16)
    grad_sequence = jnp.einsum(
        "te,de->td", grad_linear, qkv_w, preferred_element_type=F32
    ) + jnp.einsum("tf,df->td", hidden_pair[0], up_w, preferred_element_type=F32)
    normalized_gradient = scatter_group(grad_sequence)
    standardized_gradient = normalized_gradient * layernorm_gain
    grad_inputs = inverse_deviation * (
        standardized_gradient
        - jnp.mean(standardized_gradient, axis=-1, keepdims=True)
        - standardized_input
        * jnp.mean(standardized_gradient * standardized_input, axis=-1, keepdims=True)
    )
    cot_rows = cotangent.astype(F32)
    d_tokens = cot_rows + grad_inputs

    slices = jnp.concatenate([jnp.sum(grad_linear.astype(F32), axis=0), grad_b_up[0]])
    slot = this_half * 4 + place
    spread = jnp.zeros((8,) + slices.shape, F32)
    spread = lax.dynamic_update_slice(spread, slices[None], (slot, 0))
    vector = jnp.concatenate(
        [
            spread.reshape(-1),
            jnp.sum(cot_rows, axis=0),
            jnp.sum(normalized_gradient * standardized_input, axis=0),
            jnp.sum(normalized_gradient, axis=0),
        ]
    )
    vector = sum_everywhere(vector.reshape(-1, LANES)).reshape(-1)
    spread, whole = vector[: spread.size].reshape(8, -1), vector[spread.size :].reshape(3, depth)
    spread = lax.dynamic_slice_in_dim(spread, this_half * 4, 4)
    grad_b_qkv = spread[:, : 3 * width].reshape(4, 3, width).transpose(1, 0, 2).reshape(3, 4 * width)
    grad_b_up = spread[:, 3 * width :].reshape(-1)

    mlp_parts = exchange(cut(coords, mlp_grads.reshape(4, rows, 2 * hidden)))
    grad_up_w, grad_down_w = unpack(
        coords, unpack_mlp_kernel, mlp_parts, [w_up.shape, w_up.shape], "unpack_mlp"
    )
    head_parts = exchange(cut(coords, head_grads.reshape(4, rows, 4 * width)))
    shapes = [(3, rows, 4 * width), (rows, 4 * width)]
    grad_qkv_w, grad_out_w = unpack(coords, unpack_heads_kernel, head_parts, shapes, "unpack_heads")
    return (
        mixed,
        d_tokens,
        whole[1],
        whole[2],
        grad_qkv_w.transpose(1, 0, 2),
        grad_b_qkv,
        grad_out_w.T,
        whole[0],
        grad_up_w,
        grad_b_up,
        grad_down_w.T,
        whole[0],
    )


def solution(mesh):
    fine = Mesh(mesh.devices.reshape(SIZES), AXES)
    dp = ("zl", "x", "y", "c")
    in_specs = (
        P(AXES, None),
        P(),
        P(),
        P(dp, None, "mp"),
        P(None, "mp"),
        P("mp", dp),
        P(),
        P(dp, "mp"),
        P("mp"),
        P("mp", dp),
        P(),
        P(dp),
        P(AXES, None),
    )
    out_specs = (
        P(AXES, None),
        P(AXES, None),
        P(),
        P(),
        P(dp, None, "mp"),
        P(None, "mp"),
        P("mp", dp),
        P(),
        P(dp, "mp"),
        P("mp"),
        P("mp", dp),
        P(),
    )
    return jax.shard_map(
        per_device, mesh=fine, in_specs=in_specs, out_specs=out_specs, check_vma=False
    )
```

```python
import functools

import jax
import jax.numpy as jnp
from jax import lax
from jax.experimental import pallas as pl
from jax.experimental.pallas import tpu as pltpu
from jax.sharding import Mesh, PartitionSpec as P

HEAD_DIM = 64
ROT = 32
HALF = ROT // 2
LANES = 128
EPSILON = 1e-05

AXES = ("zl", "x", "y", "c", "mp")
SIZES = (2, 4, 4, 2, 2)
PLANE = ("x", "y")
PAIR = ("zl", "c")

BF16 = jnp.bfloat16
F32 = jnp.float32
MIB = 1024 * 1024
GIGA = 1000 * MIB


def flip(value, *axes):
    count = 2 ** len(axes)
    return lax.ppermute(value, axes, [(i, count - 1 - i) for i in range(count)])


def hop(value, axis, bits):
    return lax.ppermute(value, axis, [(i, i ^ bits) for i in range(4)])


def fold_kernel(mine_ref, theirs_ref, keep_ref, *sends):
    rows = keep_ref.shape[0]
    for i in range(4):
        block = slice(i * rows, (i + 1) * rows)
        total = mine_ref[block, :].astype(F32) + theirs_ref[block, :].astype(F32)
        if i == 0:
            keep_ref[...] = total
        else:
            sends[i - 1][...] = total.astype(BF16)


def scatter_group(mine, theirs):
    rows, depth = mine.shape[0] // 4, mine.shape[1]
    tile = depth // 4
    theirs = flip(theirs, "c")
    keep, *sends = pl.pallas_call(
        fold_kernel,
        grid=(4,),
        in_specs=[pl.BlockSpec((4 * rows, tile), lambda j: (0, j))] * 2,
        out_specs=[pl.BlockSpec((rows, tile), lambda j: (0, j))] * 4,
        out_shape=[like((rows, depth), F32)] + [like((rows, depth))] * 3,
        compiler_params=params(16),
        cost_estimate=cost(0, 13 * rows * depth),
        name="fold",
    )(mine, theirs)
    far = [flip(sends[0], "mp"), flip(sends[1], "zl"), flip(sends[2], "zl", "mp")]
    return keep + far[0].astype(F32) + (far[1].astype(F32) + far[2].astype(F32))


def sum_everywhere(vector):
    vector = vector + flip(vector, "c")
    vector = vector + flip(vector, "zl") + (flip(vector, "mp") + flip(vector, "zl", "mp"))
    for axis in PLANE:
        vector = (vector + hop(vector, axis, 2)) + (hop(vector, axis, 1) + hop(vector, axis, 3))
    return vector


def attention_kernel(
    linear_ref,
    grad_ref,
    cos_ref,
    low_ref,
    high_ref,
    segment_col,
    segment_row,
    index_col,
    index_row,
    right_ref,
    query_ref,
    key_ref,
    value_ref,
    grad_query_ref,
    grad_key_ref,
):
    width = grad_ref.shape[1]
    scale = HEAD_DIM ** (-0.5)

    def rotated(tile, lanes, sign):
        cos, low, high = cos_ref[...], low_ref[...], high_ref[...]
        ahead = pltpu.roll(tile, lanes - HALF, 1)
        behind = pltpu.roll(tile, HALF, 1)
        return tile * cos + (ahead * low + behind * high) * sign

    for start in range(0, width, LANES):
        lanes = slice(start, start + LANES)
        query_ref[:, lanes] = (rotated(linear_ref[:, lanes], LANES, 1.0) * scale).astype(BF16)
        keys = linear_ref[:, width + start : width + start + LANES]
        key_ref[:, lanes] = rotated(keys, LANES, 1.0).astype(BF16)
        value_ref[:, lanes] = linear_ref[:, 2 * width + start : 2 * width + start + LANES].astype(BF16)
    allowed = (segment_col[...] == segment_row[0]) & (index_col[...] >= index_row[0])
    for start in range(0, width, HEAD_DIM):
        lanes = slice(start, start + HEAD_DIM)
        query, key, value = query_ref[:, lanes], key_ref[:, lanes], value_ref[:, lanes]
        grad = grad_ref[:, lanes]
        scores = lax.dot_general(query, key, (((1,), (1,)), ((), ())), preferred_element_type=F32)
        scores = jnp.where(allowed, scores, -1000000000.0)
        expo = jnp.exp(scores - jnp.max(scores, axis=1, keepdims=True))
        probs = expo / jnp.sum(expo, axis=1, keepdims=True)
        low_probs = probs.astype(BF16)
        attended = jnp.dot(low_probs, value, preferred_element_type=F32)
        right_ref[:, 3 * width + start : 3 * width + start + HEAD_DIM] = attended.astype(BF16)
        grad_probs = lax.dot_general(grad, value, (((1,), (1,)), ((), ())), preferred_element_type=F32)
        grad_values = lax.dot_general(
            low_probs, grad, (((0,), (0,)), ((), ())), preferred_element_type=F32
        )
        weighted = probs * grad_probs
        delta = jnp.sum(weighted, axis=1, keepdims=True)
        grad_scores = (weighted - probs * delta).astype(BF16)
        grad_query_ref[:, lanes] = jnp.dot(grad_scores, key, preferred_element_type=F32) * scale
        grad_key_ref[:, lanes] = lax.dot_general(
            grad_scores, query, (((0,), (0,)), ((), ())), preferred_element_type=F32
        )
        right_ref[:, 2 * width + start : 2 * width + start + HEAD_DIM] = grad_values.astype(BF16)
    for start in range(0, width, LANES):
        lanes = slice(start, start + LANES)
        right_ref[:, lanes] = rotated(grad_query_ref[:, lanes], LANES, -1.0).astype(BF16)
        right_ref[:, width + start : width + start + LANES] = rotated(
            grad_key_ref[:, lanes], LANES, -1.0
        ).astype(BF16)


def attention(linear, grad_attended, tables, segments, indices, length):
    rows, width = grad_attended.shape
    count = rows // length
    blocks = lambda lanes: pl.BlockSpec((length, lanes), lambda i: (i, 0))
    rowwise = pl.BlockSpec((1, 1, length), lambda i: (i, 0, 0))
    return pl.pallas_call(
        attention_kernel,
        grid=(count,),
        in_specs=[
            blocks(3 * width),
            blocks(width),
            blocks(LANES),
            blocks(LANES),
            blocks(LANES),
            blocks(1),
            rowwise,
            blocks(1),
            rowwise,
        ],
        out_specs=blocks(4 * width),
        out_shape=jax.ShapeDtypeStruct((rows, 4 * width), BF16),
        scratch_shapes=[pltpu.VMEM((length, width), BF16)] * 3
        + [pltpu.VMEM((length, width), F32)] * 2,
        compiler_params=params(32),
        cost_estimate=cost(18 * GIGA, 8 * MIB),
        name="attention",
    )(
        linear,
        grad_attended,
        *tables,
        segments.reshape(rows, 1),
        segments.reshape(count, 1, length),
        indices.reshape(rows, 1),
        indices.reshape(count, 1, length),
    )


ANY = pl.BlockSpec(memory_space=pl.ANY)
WHOLE = pl.BlockSpec(memory_space=pltpu.VMEM)
SCALARS = pl.BlockSpec(memory_space=pltpu.SMEM)


def like(shape, dtype=BF16):
    return jax.ShapeDtypeStruct(shape, dtype)


def params(mib):
    return pltpu.CompilerParams(vmem_limit_bytes=mib * MIB)


def cost(flops, moved):
    return pl.CostEstimate(flops=flops, bytes_accessed=moved, transcendentals=0)


def slot_of(coords, bits):
    return (coords[0] * 2 + coords[3]) ^ bits


def pack_kernel(coords, up_ref, down_ref, qkv_ref, out_ref, segment_ref, *parts):
    hidden, width = up_ref.shape[1] // 4, out_ref.shape[1] // 4
    segments = segment_ref[...].astype(F32).astype(BF16)
    segments = jnp.broadcast_to(segments, (up_ref.shape[0], segments.shape[1]))
    for bits in range(4):
        slot = slot_of(coords, bits)
        wide = pl.ds(pl.multiple_of(slot * hidden, hidden), hidden)
        narrow = pl.ds(pl.multiple_of(slot * width, width), width)
        part = parts[bits]
        part[:, :hidden] = up_ref[:, wide]
        part[:, hidden : 2 * hidden] = down_ref[:, wide]
        for kind in range(3):
            start = 2 * hidden + kind * width
            part[:, start : start + width] = qkv_ref[kind, :, narrow]
        start = 2 * hidden + 3 * width
        part[:, start : start + width] = out_ref[:, narrow]
        part[:, start + width :] = segments


def pack(coords, w_up, down_t, qkv_t, out_t, segments):
    rows, hidden, width = w_up.shape[0], w_up.shape[1] // 4, out_t.shape[1] // 4
    return pl.pallas_call(
        pack_kernel,
        in_specs=[SCALARS] + [WHOLE] * 5,
        out_specs=[WHOLE] * 4,
        out_shape=[like((rows, 2 * hidden + 4 * width + segments.shape[0]))] * 4,
        compiler_params=params(16),
        name="pack",
    )(coords, w_up, down_t, qkv_t, out_t, segments.reshape(1, -1))


def order_kernel(coords, *refs):
    parts, outs = refs[:4], refs[4:]
    for bits in range(4):
        zl, c = coords[0] ^ (bits >> 1), coords[3] ^ (bits & 1)
        start = 0
        for out in outs:
            columns = out.shape[3]
            out[zl, c] = parts[bits][:, start : start + columns]
            start += columns


def order(coords, parts, columns):
    rows = parts[0].shape[0]
    outs = pl.pallas_call(
        order_kernel,
        in_specs=[SCALARS] + [WHOLE] * 4,
        out_specs=[WHOLE] * len(columns),
        out_shape=[like((2, 2, rows, count)) for count in columns],
        compiler_params=params(16),
        name="order",
    )(coords, *parts)
    return [out.reshape(2, 2 * rows, -1) for out in outs]


def join_kernel(*refs):
    parts, out, sem = refs[:-2], refs[-2], refs[-1]
    copies = []
    for i, part in enumerate(parts):
        copies.append(pltpu.make_async_copy(part, out.at[i], sem.at[i]))
        copies[-1].start()
    for copy in copies:
        copy.wait()


def join(*parts):
    return pl.pallas_call(
        join_kernel,
        in_specs=[ANY] * len(parts),
        out_specs=ANY,
        out_shape=like((len(parts),) + parts[0].shape),
        scratch_shapes=[pltpu.SemaphoreType.DMA((len(parts),))],
        compiler_params=params(16),
        name="join",
    )(*parts)


def place_kernel(entries, second_is_y, coords, *refs):
    parts, out, sems = refs[-2 - len(entries) : -2], refs[-2], refs[-1]
    x, y = coords[1], coords[2]
    copies = []
    for part, (second, start) in zip(parts, entries):
        for i in range(part.shape[0]):
            first = start + i
            if second_is_y:
                chip = (x ^ first) * 4 + (y ^ second)
            else:
                chip = (x ^ second) * 4 + (y ^ first)
            copies.append(pltpu.make_async_copy(part.at[i], out.at[:, chip], sems.at[len(copies)]))
            copies[-1].start()
    for copy in copies:
        copy.wait()


def place(coords, buffer, parts, entries, second):
    _, _, rows, columns = parts[0].shape
    count = sum(part.shape[0] for part in parts)
    buffers = [] if buffer is None else [buffer]
    return pl.pallas_call(
        functools.partial(place_kernel, entries, second == "y"),
        in_specs=[SCALARS] + [ANY] * (len(buffers) + len(parts)),
        out_specs=ANY,
        out_shape=like((2, 16, rows, columns)),
        scratch_shapes=[pltpu.SemaphoreType.DMA((count,))],
        input_output_aliases={1: 0} if buffers else {},
        compiler_params=params(16),
        cost_estimate=cost(0, 4 * count * rows * columns * 2),
        name="place",
    )(coords, *buffers, *parts)


def gather_line(shard, axis):
    return join(shard, hop(shard, axis, 1), hop(shard, axis, 2), hop(shard, axis, 3))


def gather_sides(row, axis):
    return hop(row, axis, 1), hop(row, axis, 3)


def gather_plane(coords, row, sides, second):
    one, three = sides
    buffer = place(coords, None, [row], [(0, 0)], second)
    half = row.shape[0] // 2
    two_low, two_high = hop(three[:half], second, 1), hop(one[half:], second, 3)
    buffer = place(coords, buffer, [one, three], [(1, 0), (3, 0)], second)
    buffer = place(coords, buffer, [two_low, two_high], [(2, 0), (2, half)], second)
    return buffer.reshape(-1, buffer.shape[3])


def tokens_kernel(mine_ref, other_ref, rows_ref, columns_ref):
    @pl.when(pl.program_id(1) == 0)
    def _():
        rows_ref[0] = mine_ref[0, 0]
        columns_ref[0] = mine_ref[0, 0].T

    @pl.when(pl.program_id(1) == 1)
    def _():
        rows_ref[0] = other_ref[0, 0]
        columns_ref[0] = other_ref[0, 0].T


def gather_tokens(*pairs):
    mine = join(*pairs)
    other = flip(mine, "c")
    _, _, rows, depth = mine.shape
    block = (1, 1, rows, depth)
    return pl.pallas_call(
        tokens_kernel,
        grid=(2, 2, 4),
        in_specs=[
            pl.BlockSpec(block, lambda w, c, z: (jnp.where(c == 0, z, 3), w, 0, 0)),
            pl.BlockSpec(block, lambda w, c, z: (jnp.where(c == 1, z, 0), w, 0, 0)),
        ],
        out_specs=[
            pl.BlockSpec((1, rows, depth), lambda w, c, z: (w, 4 * c + z, 0)),
            pl.BlockSpec((1, depth, rows), lambda w, c, z: (w, 0, 4 * c + z)),
        ],
        out_shape=[like((2, 8 * rows, depth)), like((2, depth, 8 * rows))],
        compiler_params=params(32),
        cost_estimate=cost(0, 8 * mine.size * 2),
        name="tokens",
    )(mine, other)


def mlp_kernel(pair_ref, bias_ref, up_ref, down_ref, hidden_ref, sums_ref):
    slope = 0.7978845608028654
    up = jnp.dot(pair_ref[0], up_ref[...], preferred_element_type=F32) + bias_ref[...]
    square = up * up
    wave = jnp.tanh(slope * (up + 0.044715 * (square * up)))
    half = 0.5 * (1.0 + wave)
    hidden_ref[1] = (up * half).astype(BF16)
    rise = half + (0.5 * up) * (1.0 - wave * wave) * (slope * (1.0 + 0.134145 * square))
    grad = jnp.dot(pair_ref[1], down_ref[...], preferred_element_type=F32) * rise
    low = grad.astype(BF16)
    hidden_ref[0] = low
    sums_ref[...] = jnp.sum(low.astype(F32), axis=0, keepdims=True)


def mlp(pair, bias, up_w, down_w):
    rows, depth = pair.shape[1:]
    hidden = bias.shape[0]
    tile = 256
    column = lambda j: (0, j)
    return pl.pallas_call(
        mlp_kernel,
        grid=(hidden // tile,),
        in_specs=[
            pl.BlockSpec((2, rows, depth), lambda j: (0, 0, 0), pipeline_mode=pl.Buffered(1)),
            pl.BlockSpec((1, tile), column),
            pl.BlockSpec((depth, tile), column),
            pl.BlockSpec((depth, tile), column),
        ],
        out_specs=[
            pl.BlockSpec((2, rows, tile), lambda j: (0, 0, j)),
            pl.BlockSpec((1, tile), column),
        ],
        out_shape=[like((2, rows, hidden)), like((1, hidden), F32)],
        compiler_params=params(32),
        cost_estimate=cost(4 * rows * depth * hidden, 20 * MIB),
        name="mlp",
    )(pair, bias.reshape(1, -1), up_w, down_w)


def grads_kernel(left_ref, right_ref, out_ref):
    product = jnp.dot(left_ref[0], right_ref[0], preferred_element_type=F32).astype(BF16)
    out_ref[...] = product.reshape(out_ref.shape)


def weight_grads(pair_t, right, tile, which):
    _, depth, rows = pair_t.shape
    count, _, columns = right.shape
    tiles = columns // tile
    block = depth // 32
    return pl.pallas_call(
        grads_kernel,
        grid=(count, tiles, 2),
        in_specs=[
            pl.BlockSpec((1, depth // 2, rows), lambda i, j, zl: (which(i, j), zl, 0)),
            pl.BlockSpec((1, rows, tile), lambda i, j, zl: (i, 0, j)),
        ],
        out_specs=pl.BlockSpec((16, 1, block, tile), lambda i, j, zl: (0, zl, 0, i * tiles + j)),
        out_shape=like((16, 2, block, count * columns)),
        compiler_params=params(40),
        cost_estimate=cost(2 * depth * rows * count * columns, 2 * (pair_t.size + right.size * 2)),
        name="weight_grads",
    )(pair_t, right)


def head_grads_kernel(coords, left_ref, right_ref, *refs):
    outs, product_ref = refs[:-1], refs[-1]
    zl, j = pl.program_id(0), pl.program_id(1)
    x, y = coords[1], coords[2]
    block, tile = product_ref.shape[1:]
    product = jnp.dot(left_ref[0], right_ref[...], preferred_element_type=F32).astype(BF16)
    product_ref[...] = product.reshape(product_ref.shape)
    for side in range(2):

        @pl.when(j // 2 == side)
        def _(side=side):
            lanes = pl.ds(pl.multiple_of((j % 2) * tile, tile), tile)
            for second in range(4):
                for first in range(4):
                    if side == 0:
                        chip = (x ^ first) * 4 + (y ^ second)
                    else:
                        chip = (x ^ second) * 4 + (y ^ first)
                    if second == 2:
                        out, i = outs[5 * side + 3 + first // 2], first % 2
                    else:
                        out, i = outs[5 * side + (0, 1, None, 2)[second]], first
                    out[i, zl, :, lanes] = product_ref[chip]


def head_grads(coords, pair_t, right):
    _, depth, rows = pair_t.shape
    columns = right.shape[1]
    tile, block = columns // 4, depth // 32
    full, half = like((4, 2, block, 2 * tile)), like((2, 2, block, 2 * tile))
    outs = pl.pallas_call(
        head_grads_kernel,
        grid=(2, 4),
        in_specs=[
            SCALARS,
            pl.BlockSpec((1, depth // 2, rows), lambda zl, j: (j // 3, zl, 0)),
            pl.BlockSpec((rows, tile), lambda zl, j: (0, j)),
        ],
        out_specs=[WHOLE] * 10,
        out_shape=[full, full, full, half, half] * 2,
        scratch_shapes=[pltpu.VMEM((16, block, tile), BF16)],
        compiler_params=params(32),
        cost_estimate=cost(2 * depth * rows * columns, 16 * MIB),
        name="head_grads",
    )(coords, pair_t, right)
    return outs[:5], outs[5:]


def bump_kernel(chunk_ref, part_ref, out_ref):
    out_ref[...] = (chunk_ref[...].astype(F32) + part_ref[...].astype(F32)).astype(BF16)


def bump(chunk, part, half):
    spec = pl.BlockSpec(part.shape, lambda i: (half, 0, 0, 0))
    return pl.pallas_call(
        bump_kernel,
        grid=(1,),
        in_specs=[spec, pl.BlockSpec(part.shape, lambda i: (0, 0, 0, 0))],
        out_specs=spec,
        out_shape=like(chunk.shape),
        input_output_aliases={0: 0},
        compiler_params=params(16),
        name="bump",
    )(chunk, part)


def near_kernel(own_ref, one_ref, three_ref, keep_ref, *sends):
    for i in range(4):
        total = own_ref[i].astype(F32) + (one_ref[i].astype(F32) + three_ref[i].astype(F32))
        if i == 0:
            keep_ref[...] = total
        else:
            sends[i - 1][...] = total.astype(BF16)


def scatter_blocks(chunks, first, second):
    own, one, three, two_low, two_high = chunks
    low, high = hop(two_low, second, 1), hop(two_high, second, 3)
    three = hop(bump(three, low, 0), second, 3)
    one = hop(bump(one, high, 1), second, 1)
    shape = own.shape[1:]
    keep, *sends = pl.pallas_call(
        near_kernel,
        in_specs=[WHOLE] * 3,
        out_specs=[WHOLE] * 4,
        out_shape=[like(shape, F32)] + [like(shape)] * 3,
        compiler_params=params(16),
        name="near",
    )(own, one, three)
    return [keep] + [hop(send, first, bits) for send, bits in zip(sends, (1, 2, 3))]


def cut_heads_kernel(coords, *refs):
    parts, outs = refs[:8], refs[8:]
    rows = outs[0].shape[0]
    half = outs[0].shape[1] // 2
    for bits in range(4):
        zl, c = coords[0] ^ (bits >> 1), coords[3] ^ (bits & 1)
        some = pl.ds(pl.multiple_of(c * rows, rows), rows)
        for side in range(2):
            keep, *others = parts[4 * side : 4 * side + 4]
            total = keep[zl, some, :]
            for other in others:
                total = total + other[zl, some, :].astype(F32)
            outs[bits][:, side * half : (side + 1) * half] = total.astype(BF16)


def cut_heads(coords, left, right, rows):
    return pl.pallas_call(
        cut_heads_kernel,
        in_specs=[SCALARS] + [WHOLE] * 8,
        out_specs=[WHOLE] * 4,
        out_shape=[like((rows, 2 * left[0].shape[2]))] * 4,
        compiler_params=params(16),
        name="cut_heads",
    )(coords, *left, *right)


def combine_kernel(products, *refs):
    mine_ref, theirs_ref = refs[2 * products : 2 * products + 2] if len(refs) == 2 * products + 2 else refs[-3:-1]
    contract = (((1,), (1,)), ((), ()))
    total = None
    for i in range(products):
        left, right = refs[2 * i], refs[2 * i + 1]
        left = left[0] if len(left.shape) == 3 else left[...]
        product = lax.dot_general(left, right[...], contract, preferred_element_type=F32)
        total = product if total is None else total + product
    half = mine_ref.shape[0]
    mine_ref[...] = total[:half].astype(BF16)
    theirs_ref[...] = total[half:].astype(BF16)
    if len(refs) > 2 * products + 2:
        rows_ref, sums_ref = refs[2 * products], refs[-1]
        sums_ref[0:1, :] = jnp.sum(total, axis=0, keepdims=True)
        sums_ref[1:2, :] = jnp.sum(total * rows_ref[0].astype(F32), axis=0, keepdims=True)


def combine(hidden_pair, side, mlp_w, right, head_parts, pair=None):
    _, rows, hidden = hidden_pair.shape
    depth = mlp_w.shape[0]
    tile = 256
    column = lambda i: (0, i)
    specs = [
        pl.BlockSpec((1, rows, hidden), lambda i: (side, 0, 0)),
        pl.BlockSpec((tile, hidden), lambda i: (i, 0)),
    ]
    arrays = [hidden_pair, mlp_w]
    total = hidden
    for start, weights, weights_start, columns in head_parts:
        left, where = start // columns, weights_start // columns
        specs.append(pl.BlockSpec((rows, columns), lambda i, left=left: (0, left)))
        specs.append(pl.BlockSpec((tile, columns), lambda i, where=where: (i, where)))
        arrays += [right, weights]
        total += columns
    out_specs = [pl.BlockSpec((rows // 2, tile), column)] * 2
    shapes = [like((rows // 2, depth))] * 2
    if pair is not None:
        specs.append(pl.BlockSpec((1, rows, tile), lambda i: (0, 0, i)))
        arrays.append(pair)
        out_specs.append(pl.BlockSpec((2, tile), column))
        shapes.append(like((2, depth), F32))
    return pl.pallas_call(
        functools.partial(combine_kernel, 1 + len(head_parts)),
        grid=(depth // tile,),
        in_specs=specs,
        out_specs=out_specs,
        out_shape=shapes,
        compiler_params=params(32),
        cost_estimate=cost(2 * rows * depth * total, 16 * MIB),
        name="combine",
    )(*arrays)


def project_kernel(pair_ref, bias_ref, first_ref, second_ref, linear_ref, grad_ref):
    step = pl.program_id(0)

    @pl.when(step < 2)
    def _():
        linear_ref[...] = jnp.dot(pair_ref[0], first_ref[...], preferred_element_type=F32) + bias_ref[...]

    @pl.when(step == 2)
    def _():
        linear_ref[...] = jnp.dot(pair_ref[0], second_ref[...], preferred_element_type=F32) + bias_ref[...]

    @pl.when(step == 3)
    def _():
        grad_ref[...] = jnp.dot(pair_ref[0], second_ref[...], preferred_element_type=F32).astype(BF16)


def project(pair, bias, first_w, second_w):
    rows, depth = pair.shape[1:]
    width = first_w.shape[1] // 2
    return pl.pallas_call(
        project_kernel,
        grid=(4,),
        in_specs=[
            pl.BlockSpec((1, rows, depth), lambda j: (j // 3, 0, 0)),
            pl.BlockSpec((1, width), lambda j: (0, jnp.minimum(j, 2))),
            pl.BlockSpec((depth, width), lambda j: (0, jnp.minimum(j, 1))),
            pl.BlockSpec((depth, width), lambda j: (0, jnp.maximum(j - 2, 0))),
        ],
        out_specs=[
            pl.BlockSpec((rows, width), lambda j: (0, jnp.minimum(j, 2))),
            pl.BlockSpec((rows, width), lambda j: (0, 0)),
        ],
        out_shape=[like((rows, 3 * width), F32), like((rows, width))],
        compiler_params=params(32),
        cost_estimate=cost(8 * rows * depth * width, 16 * MIB),
        name="project",
    )(pair, bias.reshape(1, -1), first_w, second_w)


def cut_kernel(coords, whole_ref, *outs):
    for bits in range(4):
        outs[bits][...] = whole_ref[slot_of(coords, bits)]


def cut(coords, whole):
    return pl.pallas_call(
        cut_kernel,
        in_specs=[SCALARS, WHOLE],
        out_specs=[WHOLE] * 4,
        out_shape=[like(whole.shape[1:])] * 4,
        compiler_params=params(16),
        name="cut",
    )(coords, whole)


def exchange(parts):
    return [parts[0], flip(parts[1], "c"), flip(parts[2], "zl"), flip(parts[3], "zl", "c")]


def unpack_mlp_kernel(coords, *refs):
    parts, (up_ref, down_ref) = refs[:4], refs[4:]
    hidden = up_ref.shape[1] // 4
    for bits in range(4):
        lanes = pl.ds(pl.multiple_of(slot_of(coords, bits) * hidden, hidden), hidden)
        up_ref[:, lanes] = parts[bits][:, :hidden].astype(F32)
        down_ref[:, lanes] = parts[bits][:, hidden:].astype(F32)


def unpack_heads_kernel(coords, *refs):
    parts, (qkv_ref, out_ref) = refs[:4], refs[4:]
    width = out_ref.shape[1] // 4
    for bits in range(4):
        lanes = pl.ds(pl.multiple_of(slot_of(coords, bits) * width, width), width)
        for kind in range(3):
            qkv_ref[kind, :, lanes] = parts[bits][:, kind * width : (kind + 1) * width].astype(F32)
        out_ref[:, lanes] = parts[bits][:, 3 * width :].astype(F32)


def unpack(coords, kernel, parts, shapes, name):
    return pl.pallas_call(
        kernel,
        in_specs=[SCALARS] + [WHOLE] * 4,
        out_specs=[WHOLE] * 2,
        out_shape=[like(shape, F32) for shape in shapes],
        compiler_params=params(16),
        name=name,
    )(coords, *parts)


def scatter_plane(grads):
    return lax.psum_scatter(grads.reshape(-1, grads.shape[3]), PLANE, scatter_dimension=0, tiled=True)


def per_device(
    tokens,
    layernorm_gain,
    layernorm_bias,
    w_qkv,
    b_qkv,
    w_out,
    b_out,
    w_up,
    b_up,
    w_down,
    b_down,
    segments,
    cotangent,
):
    depth = tokens.shape[1]
    length = segments.shape[0]
    half_rows = tokens.shape[0]
    width = w_out.shape[0] // 4
    hidden = w_down.shape[0] // 4
    rows = w_up.shape[0]
    coords = jnp.stack([lax.axis_index(axis) for axis in AXES]).astype(jnp.int32)
    place_here = coords[0] * 2 + coords[3]
    this_half = coords[4]

    parts = exchange(pack(coords, w_up, w_down.T, w_qkv.transpose(1, 0, 2), w_out.T, segments))
    up_shard, down_shard, first_shard, second_shard = order(
        coords, parts, (hidden, hidden, 2 * width, 2 * width)
    )

    inputs_f = tokens.astype(F32)
    row_mean = jnp.mean(inputs_f, axis=-1, keepdims=True)
    mean_removed = inputs_f - row_mean
    variance = jnp.mean(mean_removed * mean_removed, axis=-1, keepdims=True)
    inverse_deviation = lax.rsqrt(variance + EPSILON)
    standardized_input = mean_removed * inverse_deviation
    normalized_rows = (standardized_input * layernorm_gain + layernorm_bias).astype(BF16)

    pair = jnp.stack([normalized_rows, cotangent])
    up_shard, down_shard, pair = lax.optimization_barrier((up_shard, down_shard, pair))
    near, far = flip(pair, "zl"), flip(pair, "zl", "mp")
    up_row = gather_line(up_shard, "x")
    down_row = gather_line(down_shard, "y")
    up_row, down_row, pair = lax.optimization_barrier((up_row, down_row, pair))
    opposite = flip(pair, "mp")
    up_sides, down_sides = gather_sides(up_row, "y"), gather_sides(down_row, "x")
    up_sides, down_sides, opposite, near, far, first_shard, second_shard = lax.optimization_barrier(
        (up_sides, down_sides, opposite, near, far, first_shard, second_shard)
    )
    up_w = gather_plane(coords, up_row, up_sides, "y")
    down_w = gather_plane(coords, down_row, down_sides, "x")
    first_row = gather_line(first_shard, "x")
    second_row = gather_line(second_shard, "y")
    up_w, down_w, first_row, second_row = lax.optimization_barrier((up_w, down_w, first_row, second_row))
    first_sides, second_sides = gather_sides(first_row, "y"), gather_sides(second_row, "x")
    pair, pair_t = gather_tokens(pair, opposite, near, far)

    doc = jnp.stack([parts[k][0, -length:] for k in (0, 2, 1, 3)]).astype(jnp.int32)
    doc = doc.reshape(4, 2, half_rows)
    doc = jnp.where(this_half == 0, doc, doc[:, ::-1]).reshape(4, length)
    halves = jnp.stack([this_half, 1 - this_half]) * half_rows
    index = (halves[:, None] + jnp.arange(half_rows, dtype=jnp.int32)).reshape(1, length)
    index = jnp.broadcast_to(index, (4, length)).astype(jnp.int32)
    same_doc = doc[:, :, None] == doc[:, None, :]
    doc_start = jnp.min(jnp.where(same_doc, index[:, None, :], length), axis=2)
    positions = (index - doc_start).astype(F32).reshape(-1)
    inv_freq = 10000.0 ** (-(jnp.arange(HALF, dtype=F32) * 2.0 / ROT))
    angles = positions[:, None] * inv_freq
    cos, sin = jnp.cos(angles), jnp.sin(angles)
    nothing = jnp.zeros_like(cos)
    rest = (positions.shape[0], HEAD_DIM - ROT)
    repeat = LANES // HEAD_DIM
    cos_table = jnp.tile(jnp.concatenate([cos, cos, jnp.ones(rest, F32)], axis=1), (1, repeat))
    low_table = jnp.tile(jnp.concatenate([-sin, nothing, jnp.zeros(rest, F32)], axis=1), (1, repeat))
    high_table = jnp.tile(jnp.concatenate([nothing, sin, jnp.zeros(rest, F32)], axis=1), (1, repeat))

    b_up_here = lax.dynamic_slice_in_dim(b_up, place_here * hidden, hidden)
    b_qkv_here = lax.dynamic_slice_in_dim(b_qkv, place_here * width, width, axis=1).reshape(-1)

    hidden_pair, grad_b_up = mlp(pair, b_up_here, up_w, down_w)
    mlp_grads = scatter_plane(weight_grads(pair_t, hidden_pair, hidden // 2, lambda i, j: i))

    first_sides, second_sides, pair, hidden_pair = lax.optimization_barrier(
        (first_sides, second_sides, pair, hidden_pair)
    )
    first_w = gather_plane(coords, first_row, first_sides, "y")
    second_w = gather_plane(coords, second_row, second_sides, "x")
    linear, grad_attended = project(pair, b_qkv_here, first_w, second_w)
    right = attention(
        linear, grad_attended, (cos_table, low_table, high_table), doc, index, length
    )
    first_grads, second_grads = head_grads(coords, pair_t, right)
    first_grads, second_grads, hidden_pair = lax.optimization_barrier(
        (first_grads, second_grads, hidden_pair)
    )
    first_grads = scatter_blocks(first_grads, "x", "y")
    second_grads = scatter_blocks(second_grads, "y", "x")

    inner = [(0, first_w, 0, 2 * width), (2 * width, second_w, 0, width)]
    mine, theirs, sums = combine(hidden_pair, 0, up_w, right, inner, pair)
    normalized_gradient = scatter_group(mine, theirs)
    outer = [(3 * width, second_w, width, width)]
    branches = scatter_group(*combine(hidden_pair, 1, down_w, right, outer))
    mixed = (inputs_f + branches + b_out + b_down).astype(BF16)
    standardized_gradient = normalized_gradient * layernorm_gain
    grad_inputs = inverse_deviation * (
        standardized_gradient
        - jnp.mean(standardized_gradient, axis=-1, keepdims=True)
        - standardized_input
        * jnp.mean(standardized_gradient * standardized_input, axis=-1, keepdims=True)
    )
    cot_rows = cotangent.astype(F32)
    d_tokens = cot_rows + grad_inputs

    grad_b_heads = jnp.sum(right[:, : 3 * width].astype(F32), axis=0)
    slices = jnp.concatenate([grad_b_heads, grad_b_up[0]])
    slot = this_half * 4 + place_here
    spread = jnp.zeros((8,) + slices.shape, F32)
    spread = lax.dynamic_update_slice(spread, slices[None], (slot, 0))
    vector = jnp.concatenate([spread.reshape(-1), jnp.sum(cot_rows, axis=0), sums.reshape(-1)])
    vector = sum_everywhere(vector.reshape(-1, LANES)).reshape(-1)
    spread, whole = vector[: spread.size].reshape(8, -1), vector[spread.size :].reshape(3, depth)
    spread = lax.dynamic_slice_in_dim(spread, this_half * 4, 4)
    grad_b_qkv = spread[:, : 3 * width].reshape(4, 3, width).transpose(1, 0, 2).reshape(3, 4 * width)
    grad_b_up = spread[:, 3 * width :].reshape(-1)
    grad_gain = (whole[2] - layernorm_bias * whole[1]) / layernorm_gain

    mlp_parts = exchange(cut(coords, mlp_grads.reshape(4, rows, 2 * hidden)))
    grad_up_w, grad_down_w = unpack(
        coords, unpack_mlp_kernel, mlp_parts, [w_up.shape, w_up.shape], "unpack_mlp"
    )
    head_parts = exchange(cut_heads(coords, first_grads, second_grads, rows))
    shapes = [(3, rows, 4 * width), (rows, 4 * width)]
    grad_qkv_w, grad_out_w = unpack(coords, unpack_heads_kernel, head_parts, shapes, "unpack_heads")
    return (
        mixed,
        d_tokens,
        grad_gain,
        whole[1],
        grad_qkv_w.transpose(1, 0, 2),
        grad_b_qkv,
        grad_out_w.T,
        whole[0],
        grad_up_w,
        grad_b_up,
        grad_down_w.T,
        whole[0],
    )


def solution(mesh):
    fine = Mesh(mesh.devices.reshape(SIZES), AXES)
    dp = ("zl", "x", "y", "c")
    in_specs = (
        P(AXES, None),
        P(),
        P(),
        P(dp, None, "mp"),
        P(None, "mp"),
        P("mp", dp),
        P(),
        P(dp, "mp"),
        P("mp"),
        P("mp", dp),
        P(),
        P(dp),
        P(AXES, None),
    )
    out_specs = (
        P(AXES, None),
        P(AXES, None),
        P(),
        P(),
        P(dp, None, "mp"),
        P(None, "mp"),
        P("mp", dp),
        P(),
        P(dp, "mp"),
        P("mp"),
        P("mp", dp),
        P(),
    )
    return jax.shard_map(
        per_device, mesh=fine, in_specs=in_specs, out_specs=out_specs, check_vma=False
    )
```

```python
import functools

import jax
import jax.numpy as jnp
from jax import lax
from jax.experimental import pallas as pl
from jax.experimental.pallas import tpu as pltpu
from jax.sharding import Mesh, PartitionSpec as P

HEAD_DIM = 64
ROT = 32
HALF = ROT // 2
LANES = 128
EPSILON = 1e-05

AXES = ("zl", "x", "y", "c", "mp")
SIZES = (2, 4, 4, 2, 2)
PLANE = ("x", "y")
PAIR = ("zl", "c")

BF16 = jnp.bfloat16
F32 = jnp.float32
MIB = 1024 * 1024
GIGA = 1000 * MIB


def flip(value, *axes):
    count = 2 ** len(axes)
    return lax.ppermute(value, axes, [(i, count - 1 - i) for i in range(count)])


def hop(value, axis, bits):
    return lax.ppermute(value, axis, [(i, i ^ bits) for i in range(4)])


def fold_kernel(mine_ref, theirs_ref, keep_ref, *sends):
    rows = keep_ref.shape[0]
    for i in range(4):
        block = slice(i * rows, (i + 1) * rows)
        total = mine_ref[block, :].astype(F32) + theirs_ref[block, :].astype(F32)
        if i == 0:
            keep_ref[...] = total
        else:
            sends[i - 1][...] = total.astype(BF16)


def scatter_group(mine, theirs):
    rows, depth = mine.shape[0] // 4, mine.shape[1]
    tile = depth // 4
    theirs = flip(theirs, "c")
    keep, *sends = pl.pallas_call(
        fold_kernel,
        grid=(4,),
        in_specs=[pl.BlockSpec((4 * rows, tile), lambda j: (0, j))] * 2,
        out_specs=[pl.BlockSpec((rows, tile), lambda j: (0, j))] * 4,
        out_shape=[like((rows, depth), F32)] + [like((rows, depth))] * 3,
        compiler_params=params(16),
        cost_estimate=cost(0, 13 * rows * depth),
        name="fold",
    )(mine, theirs)
    return [keep, flip(sends[0], "mp"), flip(sends[1], "zl"), flip(sends[2], "zl", "mp")]


def sum_everywhere(vector):
    vector = vector + flip(vector, "c")
    vector = vector + flip(vector, "zl") + (flip(vector, "mp") + flip(vector, "zl", "mp"))
    for axis in PLANE:
        vector = (vector + hop(vector, axis, 2)) + (hop(vector, axis, 1) + hop(vector, axis, 3))
    return vector


def attention_kernel(
    linear_ref,
    grad_ref,
    cos_ref,
    low_ref,
    high_ref,
    segment_col,
    segment_row,
    index_col,
    index_row,
    right_ref,
    query_ref,
    key_ref,
    value_ref,
    grad_query_ref,
    grad_key_ref,
):
    width = grad_ref.shape[1]
    scale = HEAD_DIM ** (-0.5)

    def rotated(tile, lanes, sign):
        cos, low, high = cos_ref[...], low_ref[...], high_ref[...]
        ahead = pltpu.roll(tile, lanes - HALF, 1)
        behind = pltpu.roll(tile, HALF, 1)
        return tile * cos + (ahead * low + behind * high) * sign

    for start in range(0, width, LANES):
        lanes = slice(start, start + LANES)
        query_ref[:, lanes] = (rotated(linear_ref[:, lanes], LANES, 1.0) * scale).astype(BF16)
        keys = linear_ref[:, width + start : width + start + LANES]
        key_ref[:, lanes] = rotated(keys, LANES, 1.0).astype(BF16)
        value_ref[:, lanes] = linear_ref[:, 2 * width + start : 2 * width + start + LANES].astype(BF16)
    allowed = (segment_col[...] == segment_row[0]) & (index_col[...] >= index_row[0])
    for start in range(0, width, HEAD_DIM):
        lanes = slice(start, start + HEAD_DIM)
        query, key, value = query_ref[:, lanes], key_ref[:, lanes], value_ref[:, lanes]
        grad = grad_ref[:, lanes]
        scores = lax.dot_general(query, key, (((1,), (1,)), ((), ())), preferred_element_type=F32)
        scores = jnp.where(allowed, scores, -1000000000.0)
        expo = jnp.exp(scores - jnp.max(scores, axis=1, keepdims=True))
        probs = expo / jnp.sum(expo, axis=1, keepdims=True)
        low_probs = probs.astype(BF16)
        attended = jnp.dot(low_probs, value, preferred_element_type=F32)
        right_ref[:, 3 * width + start : 3 * width + start + HEAD_DIM] = attended.astype(BF16)
        grad_probs = lax.dot_general(grad, value, (((1,), (1,)), ((), ())), preferred_element_type=F32)
        grad_values = lax.dot_general(
            low_probs, grad, (((0,), (0,)), ((), ())), preferred_element_type=F32
        )
        weighted = probs * grad_probs
        delta = jnp.sum(weighted, axis=1, keepdims=True)
        grad_scores = (weighted - probs * delta).astype(BF16)
        grad_query_ref[:, lanes] = jnp.dot(grad_scores, key, preferred_element_type=F32) * scale
        grad_key_ref[:, lanes] = lax.dot_general(
            grad_scores, query, (((0,), (0,)), ((), ())), preferred_element_type=F32
        )
        right_ref[:, 2 * width + start : 2 * width + start + HEAD_DIM] = grad_values.astype(BF16)
    for start in range(0, width, LANES):
        lanes = slice(start, start + LANES)
        right_ref[:, lanes] = rotated(grad_query_ref[:, lanes], LANES, -1.0).astype(BF16)
        right_ref[:, width + start : width + start + LANES] = rotated(
            grad_key_ref[:, lanes], LANES, -1.0
        ).astype(BF16)


def attention(linear, grad_attended, tables, segments, indices, length):
    rows, width = grad_attended.shape
    count = rows // length
    blocks = lambda lanes: pl.BlockSpec((length, lanes), lambda i: (i, 0))
    rowwise = pl.BlockSpec((1, 1, length), lambda i: (i, 0, 0))
    return pl.pallas_call(
        attention_kernel,
        grid=(count,),
        in_specs=[
            blocks(3 * width),
            blocks(width),
            blocks(LANES),
            blocks(LANES),
            blocks(LANES),
            blocks(1),
            rowwise,
            blocks(1),
            rowwise,
        ],
        out_specs=blocks(4 * width),
        out_shape=jax.ShapeDtypeStruct((rows, 4 * width), BF16),
        scratch_shapes=[pltpu.VMEM((length, width), BF16)] * 3
        + [pltpu.VMEM((length, width), F32)] * 2,
        compiler_params=params(32),
        cost_estimate=cost(18 * GIGA, 8 * MIB),
        name="attention",
    )(
        linear,
        grad_attended,
        *tables,
        segments.reshape(rows, 1),
        segments.reshape(count, 1, length),
        indices.reshape(rows, 1),
        indices.reshape(count, 1, length),
    )


ANY = pl.BlockSpec(memory_space=pl.ANY)
WHOLE = pl.BlockSpec(memory_space=pltpu.VMEM)
SCALARS = pl.BlockSpec(memory_space=pltpu.SMEM)


def like(shape, dtype=BF16):
    return jax.ShapeDtypeStruct(shape, dtype)


def params(mib):
    return pltpu.CompilerParams(vmem_limit_bytes=mib * MIB)


def cost(flops, moved):
    return pl.CostEstimate(flops=flops, bytes_accessed=moved, transcendentals=0)


def slot_of(coords, bits):
    return (coords[0] * 2 + coords[3]) ^ bits


def pack_kernel(coords, up_ref, down_ref, qkv_ref, out_ref, segment_ref, *parts):
    hidden, width = up_ref.shape[1] // 4, out_ref.shape[1] // 4
    segments = segment_ref[...].astype(F32).astype(BF16)
    segments = jnp.broadcast_to(segments, (up_ref.shape[0], segments.shape[1]))
    for bits in range(4):
        slot = slot_of(coords, bits)
        wide = pl.ds(pl.multiple_of(slot * hidden, hidden), hidden)
        narrow = pl.ds(pl.multiple_of(slot * width, width), width)
        part = parts[bits]
        part[:, :hidden] = up_ref[:, wide]
        part[:, hidden : 2 * hidden] = down_ref[:, wide]
        for kind in range(3):
            start = 2 * hidden + kind * width
            part[:, start : start + width] = qkv_ref[kind, :, narrow]
        start = 2 * hidden + 3 * width
        part[:, start : start + width] = out_ref[:, narrow]
        part[:, start + width :] = segments


def pack(coords, w_up, down_t, qkv_t, out_t, segments):
    rows, hidden, width = w_up.shape[0], w_up.shape[1] // 4, out_t.shape[1] // 4
    return pl.pallas_call(
        pack_kernel,
        in_specs=[SCALARS] + [WHOLE] * 5,
        out_specs=[WHOLE] * 4,
        out_shape=[like((rows, 2 * hidden + 4 * width + segments.shape[0]))] * 4,
        compiler_params=params(16),
        name="pack",
    )(coords, w_up, down_t, qkv_t, out_t, segments.reshape(1, -1))


def order_kernel(coords, *refs):
    parts, outs = refs[:4], refs[4:]
    for bits in range(4):
        zl, c = coords[0] ^ (bits >> 1), coords[3] ^ (bits & 1)
        start = 0
        for out in outs:
            columns = out.shape[3]
            out[zl, c] = parts[bits][:, start : start + columns]
            start += columns


def order(coords, parts, columns):
    rows = parts[0].shape[0]
    outs = pl.pallas_call(
        order_kernel,
        in_specs=[SCALARS] + [WHOLE] * 4,
        out_specs=[WHOLE] * len(columns),
        out_shape=[like((2, 2, rows, count)) for count in columns],
        compiler_params=params(16),
        name="order",
    )(coords, *parts)
    return [out.reshape(2, 2 * rows, -1) for out in outs]


def join_kernel(*refs):
    parts, out, sem = refs[:-2], refs[-2], refs[-1]
    copies = []
    for i, part in enumerate(parts):
        copies.append(pltpu.make_async_copy(part, out.at[i], sem.at[i]))
        copies[-1].start()
    for copy in copies:
        copy.wait()


def join(*parts):
    return pl.pallas_call(
        join_kernel,
        in_specs=[ANY] * len(parts),
        out_specs=ANY,
        out_shape=like((len(parts),) + parts[0].shape),
        scratch_shapes=[pltpu.SemaphoreType.DMA((len(parts),))],
        compiler_params=params(16),
        name="join",
    )(*parts)


def place_kernel(entries, coords, *refs):
    parts, out, sems = refs[-2 - len(entries) : -2], refs[-2], refs[-1]
    copies = []
    for part, (y_bits, start) in zip(parts, entries):
        for i in range(part.shape[0]):
            chip = (coords[1] ^ (start + i)) * 4 + (coords[2] ^ y_bits)
            copies.append(pltpu.make_async_copy(part.at[i], out.at[chip], sems.at[len(copies)]))
            copies[-1].start()
    for copy in copies:
        copy.wait()


def place(coords, buffer, parts, entries):
    count = sum(part.shape[0] for part in parts)
    buffers = [] if buffer is None else [buffer]
    return pl.pallas_call(
        functools.partial(place_kernel, entries),
        in_specs=[SCALARS] + [ANY] * (len(buffers) + len(parts)),
        out_specs=ANY,
        out_shape=like((16,) + parts[0].shape[1:]),
        scratch_shapes=[pltpu.SemaphoreType.DMA((count,))],
        input_output_aliases={1: 0} if buffers else {},
        compiler_params=params(16),
        cost_estimate=cost(0, 4 * count * parts[0][0].size),
        name="place",
    )(coords, *buffers, *parts)


def gather_line(shard, axis):
    return join(shard, hop(shard, axis, 1), hop(shard, axis, 2), hop(shard, axis, 3))


def gather_plane(coords, shard):
    row = gather_line(shard, "x")
    one, three = hop(row, "y", 1), hop(row, "y", 3)
    half = row.shape[0] // 2
    two_low, two_high = hop(three[:half], "y", 1), hop(one[half:], "y", 3)
    buffer = place(coords, None, [row], [(0, 0)])
    buffer = place(coords, buffer, [one, three], [(1, 0), (3, 0)])
    buffer = place(coords, buffer, [two_low, two_high], [(2, 0), (2, half)])
    return buffer.reshape(-1, buffer.shape[3])


def tokens_kernel(mine_ref, other_ref, rows_ref, columns_ref):
    @pl.when(pl.program_id(1) == 0)
    def _():
        rows_ref[0] = mine_ref[0, 0]
        columns_ref[0] = mine_ref[0, 0].T

    @pl.when(pl.program_id(1) == 1)
    def _():
        rows_ref[0] = other_ref[0, 0]
        columns_ref[0] = other_ref[0, 0].T


def gather_tokens(*pairs):
    mine = join(*pairs)
    other = flip(mine, "c")
    _, _, rows, depth = mine.shape
    block = (1, 1, rows, depth)
    return pl.pallas_call(
        tokens_kernel,
        grid=(2, 2, 4),
        in_specs=[
            pl.BlockSpec(block, lambda w, c, z: (jnp.where(c == 0, z, 3), w, 0, 0)),
            pl.BlockSpec(block, lambda w, c, z: (jnp.where(c == 1, z, 0), w, 0, 0)),
        ],
        out_specs=[
            pl.BlockSpec((1, rows, depth), lambda w, c, z: (w, 4 * c + z, 0)),
            pl.BlockSpec((1, depth, rows), lambda w, c, z: (w, 0, 4 * c + z)),
        ],
        out_shape=[like((2, 8 * rows, depth)), like((2, depth, 8 * rows))],
        compiler_params=params(32),
        cost_estimate=cost(0, 8 * mine.size * 2),
        name="tokens",
    )(mine, other)


def mlp_kernel(pair_ref, bias_ref, up_ref, down_ref, hidden_ref, sums_ref):
    slope = 0.7978845608028654
    up = jnp.dot(pair_ref[0], up_ref[...], preferred_element_type=F32) + bias_ref[...]
    square = up * up
    wave = jnp.tanh(slope * (up + 0.044715 * (square * up)))
    half = 0.5 * (1.0 + wave)
    hidden_ref[1] = (up * half).astype(BF16)
    rise = half + (0.5 * up) * (1.0 - wave * wave) * (slope * (1.0 + 0.134145 * square))
    grad = jnp.dot(pair_ref[1], down_ref[...], preferred_element_type=F32) * rise
    low = grad.astype(BF16)
    hidden_ref[0] = low
    sums_ref[...] = jnp.sum(low.astype(F32), axis=0, keepdims=True)


def mlp(pair, bias, weights):
    rows, depth = pair.shape[1:]
    hidden = bias.shape[0]
    tile = 256
    tiles = hidden // tile
    column = lambda j: (0, j)
    return pl.pallas_call(
        mlp_kernel,
        grid=(tiles,),
        in_specs=[
            pl.BlockSpec((2, rows, depth), lambda j: (0, 0, 0), pipeline_mode=pl.Buffered(1)),
            pl.BlockSpec((1, tile), column),
            pl.BlockSpec((depth, tile), column),
            pl.BlockSpec((depth, tile), lambda j: (0, tiles + j)),
        ],
        out_specs=[
            pl.BlockSpec((2, rows, tile), lambda j: (0, 0, j)),
            pl.BlockSpec((1, tile), column),
        ],
        out_shape=[like((2, rows, hidden)), like((1, hidden), F32)],
        compiler_params=params(32),
        cost_estimate=cost(4 * rows * depth * hidden, 20 * MIB),
        name="mlp",
    )(pair, bias.reshape(1, -1), weights, weights)


def grads_kernel(left_ref, right_ref, out_ref):
    out_ref[...] = jnp.dot(left_ref[0], right_ref[0], preferred_element_type=F32).astype(BF16)


def weight_grads(pair_t, right, tile):
    _, depth, rows = pair_t.shape
    count, _, columns = right.shape
    tiles = columns // tile
    return pl.pallas_call(
        grads_kernel,
        grid=(count, tiles, 2),
        in_specs=[
            pl.BlockSpec((1, depth // 2, rows), lambda i, j, k: (i, k, 0)),
            pl.BlockSpec((1, rows, tile), lambda i, j, k: (i, 0, j)),
        ],
        out_specs=pl.BlockSpec((depth // 2, tile), lambda i, j, k: (k, i * tiles + j)),
        out_shape=like((depth, count * columns)),
        compiler_params=params(40),
        cost_estimate=cost(2 * depth * rows * count * columns, 2 * (pair_t.size + right.size * 2)),
        name="weight_grads",
    )(pair_t, right)


def head_grads_kernel(coords, left_ref, right_ref, *refs):
    outs, product_ref = refs[:-1], refs[-1]
    x, y = coords[1], coords[2]
    tile = product_ref.shape[3]
    lanes = pl.ds(pl.multiple_of(pl.program_id(0) * tile, tile), tile)
    product = jnp.dot(left_ref[0], right_ref[...], preferred_element_type=F32).astype(BF16)
    product_ref[...] = product.reshape(product_ref.shape)
    for y_bits in range(4):
        for x_bits in range(4):
            chip = (x ^ x_bits) * 4 + (y ^ y_bits)
            if y_bits == 2:
                out, i = outs[3 + x_bits // 2], x_bits % 2
            else:
                out, i = outs[(0, 1, None, 2)[y_bits]], x_bits
            out[i, :, :, lanes] = product_ref[chip]


def head_grads(coords, pair_t, right):
    _, depth, rows = pair_t.shape
    columns = right.shape[1]
    tile, block = columns // 4, depth // 32
    full, half = like((4, 2, block, columns)), like((2, 2, block, columns))
    return pl.pallas_call(
        head_grads_kernel,
        grid=(4,),
        in_specs=[
            SCALARS,
            pl.BlockSpec((1, depth, rows), lambda j: (j // 3, 0, 0)),
            pl.BlockSpec((rows, tile), lambda j: (0, j)),
        ],
        out_specs=[WHOLE] * 5,
        out_shape=[full, full, full, half, half],
        scratch_shapes=[pltpu.VMEM((16, 2, block, tile), BF16)],
        compiler_params=params(32),
        cost_estimate=cost(2 * depth * rows * columns, 16 * MIB),
        name="head_grads",
    )(coords, pair_t, right)


def bump_kernel(chunk_ref, part_ref, out_ref):
    out_ref[...] = (chunk_ref[...].astype(F32) + part_ref[...].astype(F32)).astype(BF16)


def bump(chunk, part, half):
    spec = pl.BlockSpec(part.shape, lambda i: (half, 0, 0, 0))
    return pl.pallas_call(
        bump_kernel,
        grid=(1,),
        in_specs=[spec, pl.BlockSpec(part.shape, lambda i: (0, 0, 0, 0))],
        out_specs=spec,
        out_shape=like(chunk.shape),
        input_output_aliases={0: 0},
        compiler_params=params(16),
        name="bump",
    )(chunk, part)


def near_kernel(own_ref, one_ref, three_ref, keep_ref, *sends):
    for i in range(4):
        total = own_ref[i].astype(F32) + (one_ref[i].astype(F32) + three_ref[i].astype(F32))
        if i == 0:
            keep_ref[...] = total
        else:
            sends[i - 1][...] = total.astype(BF16)


def scatter_blocks(chunks):
    own, one, three, two_low, two_high = chunks
    low, high = hop(two_low, "y", 1), hop(two_high, "y", 3)
    three = hop(bump(three, low, 0), "y", 3)
    one = hop(bump(one, high, 1), "y", 1)
    shape = own.shape[1:]
    keep, *sends = pl.pallas_call(
        near_kernel,
        in_specs=[WHOLE] * 3,
        out_specs=[WHOLE] * 4,
        out_shape=[like(shape, F32)] + [like(shape)] * 3,
        compiler_params=params(16),
        name="near",
    )(own, one, three)
    return [keep] + [hop(send, "x", bits) for send, bits in zip(sends, (1, 2, 3))]


def cut_kernel(coords, mlp_ref, *refs):
    heads, outs = refs[:4], refs[4:]
    rows, columns = outs[0].shape[0], mlp_ref.shape[1]
    for bits in range(4):
        start = pl.multiple_of(slot_of(coords, bits) * rows, rows)
        some = pl.ds(start, rows)
        outs[bits][:, :columns] = mlp_ref[some, :]
        total = heads[0][some, :]
        for head in heads[1:]:
            total = total + head[some, :].astype(F32)
        outs[bits][:, columns:] = total.astype(BF16)


def cut(coords, mlp_grads, heads):
    rows = mlp_grads.shape[0]
    heads = [head.reshape(rows, -1) for head in heads]
    columns = mlp_grads.shape[1] + heads[0].shape[1]
    return pl.pallas_call(
        cut_kernel,
        in_specs=[SCALARS] + [WHOLE] * 5,
        out_specs=[WHOLE] * 4,
        out_shape=[like((rows // 4, columns))] * 4,
        compiler_params=params(16),
        name="cut",
    )(coords, mlp_grads, *heads)


def combine_kernel(products, *refs):
    mine_ref, theirs_ref = refs[2 * products : 2 * products + 2] if len(refs) == 2 * products + 2 else refs[-3:-1]
    contract = (((1,), (1,)), ((), ()))
    total = None
    for i in range(products):
        left, right = refs[2 * i], refs[2 * i + 1]
        left = left[0] if len(left.shape) == 3 else left[...]
        product = lax.dot_general(left, right[...], contract, preferred_element_type=F32)
        total = product if total is None else total + product
    half = mine_ref.shape[0]
    mine_ref[...] = total[:half].astype(BF16)
    theirs_ref[...] = total[half:].astype(BF16)
    if len(refs) > 2 * products + 2:
        rows_ref, sums_ref = refs[2 * products], refs[-1]
        sums_ref[0:1, :] = jnp.sum(total, axis=0, keepdims=True)
        sums_ref[1:2, :] = jnp.sum(total * rows_ref[0].astype(F32), axis=0, keepdims=True)


def combine(hidden_pair, side, right, start, stop, mlp_w, head_w, pair=None):
    _, rows, hidden = hidden_pair.shape
    depth = mlp_w.shape[0]
    width, tile = stop - start, 256
    where = start // width
    column = lambda i: (0, i)
    specs = [
        pl.BlockSpec((1, rows, hidden), lambda i: (side, 0, 0)),
        pl.BlockSpec((tile, hidden), lambda i: (i, side)),
        pl.BlockSpec((rows, width), lambda i: (0, where)),
        pl.BlockSpec((tile, width), lambda i: (i, where)),
    ]
    arrays = [hidden_pair, mlp_w, right, head_w]
    out_specs = [pl.BlockSpec((rows // 2, tile), column)] * 2
    shapes = [like((rows // 2, depth))] * 2
    if pair is not None:
        specs.append(pl.BlockSpec((1, rows, tile), lambda i: (0, 0, i)))
        arrays.append(pair)
        out_specs.append(pl.BlockSpec((2, tile), column))
        shapes.append(like((2, depth), F32))
    return pl.pallas_call(
        functools.partial(combine_kernel, 2),
        grid=(depth // tile,),
        in_specs=specs,
        out_specs=out_specs,
        out_shape=shapes,
        compiler_params=params(32),
        cost_estimate=cost(2 * rows * depth * (hidden + width), 16 * MIB),
        name="combine",
    )(*arrays)


def project_kernel(pair_ref, bias_ref, weights_ref, linear_ref, grad_ref):
    product = jnp.dot(pair_ref[0], weights_ref[...], preferred_element_type=F32)

    @pl.when(pl.program_id(0) < 3)
    def _():
        linear_ref[...] = product + bias_ref[...]

    @pl.when(pl.program_id(0) == 3)
    def _():
        grad_ref[...] = product.astype(BF16)


def project(pair, bias, weights):
    rows, depth = pair.shape[1:]
    width = weights.shape[1] // 4
    return pl.pallas_call(
        project_kernel,
        grid=(4,),
        in_specs=[
            pl.BlockSpec((1, rows, depth), lambda j: (j // 3, 0, 0)),
            pl.BlockSpec((1, width), lambda j: (0, jnp.minimum(j, 2))),
            pl.BlockSpec((depth, width), lambda j: (0, j)),
        ],
        out_specs=[
            pl.BlockSpec((rows, width), lambda j: (0, jnp.minimum(j, 2))),
            pl.BlockSpec((rows, width), lambda j: (0, 0)),
        ],
        out_shape=[like((rows, 3 * width), F32), like((rows, width))],
        compiler_params=params(32),
        cost_estimate=cost(8 * rows * depth * width, 16 * MIB),
        name="project",
    )(pair, bias.reshape(1, -1), weights)


def exchange(parts):
    return [parts[0], flip(parts[1], "c"), flip(parts[2], "zl"), flip(parts[3], "zl", "c")]


def unpack_kernel(coords, *refs):
    parts, (up_ref, down_ref, qkv_ref, out_ref) = refs[:4], refs[4:]
    hidden, width = up_ref.shape[1] // 4, out_ref.shape[1] // 4
    for bits in range(4):
        slot = slot_of(coords, bits)
        wide = pl.ds(pl.multiple_of(slot * hidden, hidden), hidden)
        narrow = pl.ds(pl.multiple_of(slot * width, width), width)
        part = parts[bits]
        up_ref[:, wide] = part[:, :hidden].astype(F32)
        down_ref[:, wide] = part[:, hidden : 2 * hidden].astype(F32)
        for kind in range(3):
            start = 2 * hidden + kind * width
            qkv_ref[kind, :, narrow] = part[:, start : start + width].astype(F32)
        out_ref[:, narrow] = part[:, 2 * hidden + 3 * width :].astype(F32)


def unpack(coords, parts, hidden, width):
    rows = parts[0].shape[0]
    wide, narrow = (rows, 4 * hidden), (rows, 4 * width)
    return pl.pallas_call(
        unpack_kernel,
        in_specs=[SCALARS] + [WHOLE] * 4,
        out_specs=[WHOLE] * 4,
        out_shape=[like(shape, F32) for shape in (wide, wide, (3,) + narrow, narrow)],
        compiler_params=params(16),
        name="unpack",
    )(coords, *parts)


def turn(dest, value, back):
    block = value.shape[1] // 32
    for chip in range(16):
        for zl in range(2):
            natural, inside = (zl * 16 + chip) * block, (chip * 2 + zl) * block
            source, target = (inside, natural) if back else (natural, inside)
            dest[:, target : target + block] = value[:, source : source + block].astype(dest.dtype)


def standardize(tokens):
    rows = tokens.astype(F32)
    centered = rows - jnp.mean(rows, axis=1, keepdims=True)
    scale = lax.rsqrt(jnp.mean(centered * centered, axis=1, keepdims=True) + EPSILON)
    return rows, centered * scale, scale


def enter_kernel(tokens_ref, cot_ref, gain_ref, bias_ref, pair_ref, sums_ref):
    _, standard, _ = standardize(tokens_ref[...])
    turn(pair_ref.at[0], (standard * gain_ref[...] + bias_ref[...]).astype(BF16), False)
    turn(pair_ref.at[1], cot_ref[...], False)
    sums_ref[...] = jnp.sum(cot_ref[...].astype(F32), axis=0, keepdims=True)


def enter(tokens, cotangent, gain, bias):
    return pl.pallas_call(
        enter_kernel,
        in_specs=[WHOLE] * 4,
        out_specs=[WHOLE] * 2,
        out_shape=[like((2,) + tokens.shape), like((1, tokens.shape[1]), F32)],
        compiler_params=params(16),
        name="enter",
    )(tokens, cotangent, gain.reshape(1, -1), bias.reshape(1, -1))


def leave_kernel(tokens_ref, cot_ref, gain_ref, bias_ref, *refs):
    mixed_ref, grad_ref, branch_ref, normed_ref = refs[-4:]
    branch, normed = refs[:4], refs[4:8]
    total = branch[0][...]
    for part in branch[1:]:
        total = total + part[...].astype(F32)
    turn(branch_ref, total, True)
    total = normed[0][...]
    for part in normed[1:]:
        total = total + part[...].astype(F32)
    turn(normed_ref, total, True)
    rows, standard, scale = standardize(tokens_ref[...])
    mixed_ref[...] = (rows + branch_ref[...] + bias_ref[...]).astype(BF16)
    grad = normed_ref[...] * gain_ref[...]
    level = jnp.mean(grad, axis=1, keepdims=True)
    slope = jnp.mean(grad * standard, axis=1, keepdims=True)
    grad_ref[...] = cot_ref[...].astype(F32) + scale * (grad - level - standard * slope)


def leave(tokens, cotangent, gain, bias, branches, normed):
    shape = tokens.shape
    return pl.pallas_call(
        leave_kernel,
        in_specs=[WHOLE] * 12,
        out_specs=[WHOLE] * 2,
        out_shape=[like(shape), like(shape, F32)],
        scratch_shapes=[pltpu.VMEM(shape, F32)] * 2,
        compiler_params=params(24),
        name="leave",
    )(tokens, cotangent, gain.reshape(1, -1), bias.reshape(1, -1), *branches, *normed)


def scatter_plane(grads):
    return lax.psum_scatter(grads, PLANE, scatter_dimension=0, tiled=True)


def per_device(
    tokens,
    layernorm_gain,
    layernorm_bias,
    w_qkv,
    b_qkv,
    w_out,
    b_out,
    w_up,
    b_up,
    w_down,
    b_down,
    segments,
    cotangent,
):
    depth = tokens.shape[1]
    length = segments.shape[0]
    half_rows = tokens.shape[0]
    width = w_out.shape[0] // 4
    hidden = w_down.shape[0] // 4
    rows = w_up.shape[0]
    coords = jnp.stack([lax.axis_index(axis) for axis in AXES]).astype(jnp.int32)
    place_here = coords[0] * 2 + coords[3]
    this_half = coords[4]

    parts = exchange(pack(coords, w_up, w_down.T, w_qkv.transpose(1, 0, 2), w_out.T, segments))
    mlp_shard, head_shard = order(coords, parts, (2 * hidden, 4 * width))
    mlp_w = lax.all_gather(mlp_shard, PLANE, axis=0, tiled=False).reshape(depth, 2 * hidden)

    pair, grad_b_out = enter(tokens, cotangent, layernorm_gain, layernorm_bias)
    head_shard, pair = lax.optimization_barrier((head_shard, pair))
    near, far, opposite = flip(pair, "zl"), flip(pair, "zl", "mp"), flip(pair, "mp")
    head_w = gather_plane(coords, head_shard)
    pair, pair_t = gather_tokens(pair, opposite, near, far)

    doc = jnp.stack([parts[k][0, -length:] for k in (0, 2, 1, 3)]).astype(jnp.int32)
    doc = doc.reshape(4, 2, half_rows)
    doc = jnp.where(this_half == 0, doc, doc[:, ::-1]).reshape(4, length)
    halves = jnp.stack([this_half, 1 - this_half]) * half_rows
    index = (halves[:, None] + jnp.arange(half_rows, dtype=jnp.int32)).reshape(1, length)
    index = jnp.broadcast_to(index, (4, length)).astype(jnp.int32)
    same_doc = doc[:, :, None] == doc[:, None, :]
    doc_start = jnp.min(jnp.where(same_doc, index[:, None, :], length), axis=2)
    positions = (index - doc_start).astype(F32).reshape(-1)
    inv_freq = 10000.0 ** (-(jnp.arange(HALF, dtype=F32) * 2.0 / ROT))
    angles = positions[:, None] * inv_freq
    cos, sin = jnp.cos(angles), jnp.sin(angles)
    nothing = jnp.zeros_like(cos)
    rest = (positions.shape[0], HEAD_DIM - ROT)
    repeat = LANES // HEAD_DIM
    cos_table = jnp.tile(jnp.concatenate([cos, cos, jnp.ones(rest, F32)], axis=1), (1, repeat))
    low_table = jnp.tile(jnp.concatenate([-sin, nothing, jnp.zeros(rest, F32)], axis=1), (1, repeat))
    high_table = jnp.tile(jnp.concatenate([nothing, sin, jnp.zeros(rest, F32)], axis=1), (1, repeat))

    b_up_here = lax.dynamic_slice_in_dim(b_up, place_here * hidden, hidden)
    b_qkv_here = lax.dynamic_slice_in_dim(b_qkv, place_here * width, width, axis=1).reshape(-1)

    pair, head_w = lax.optimization_barrier((pair, head_w))
    hidden_pair, grad_b_up = mlp(pair, b_up_here, mlp_w)
    mlp_grads = scatter_plane(weight_grads(pair_t, hidden_pair, hidden // 2))

    pair, hidden_pair = lax.optimization_barrier((pair, hidden_pair))
    linear, grad_attended = project(pair, b_qkv_here, head_w)
    right = attention(
        linear, grad_attended, (cos_table, low_table, high_table), doc, index, length
    )
    heads, hidden_pair = lax.optimization_barrier((head_grads(coords, pair_t, right), hidden_pair))
    heads = scatter_blocks(heads)

    mine, theirs, sums = combine(hidden_pair, 0, right, 0, 3 * width, mlp_w, head_w, pair)
    normed = scatter_group(mine, theirs)
    branches = scatter_group(*combine(hidden_pair, 1, right, 3 * width, 4 * width, mlp_w, head_w))
    mixed, d_tokens = leave(
        tokens, cotangent, layernorm_gain, b_out + b_down, branches, normed
    )

    grad_b_heads = jnp.sum(right[:, : 3 * width].astype(F32), axis=0)
    slices = jnp.concatenate([grad_b_heads, grad_b_up[0]])
    slot = this_half * 4 + place_here
    spread = jnp.zeros((8,) + slices.shape, F32)
    spread = lax.dynamic_update_slice(spread, slices[None], (slot, 0))
    vector = jnp.concatenate([spread.reshape(-1), grad_b_out[0], sums.reshape(-1)])
    vector = sum_everywhere(vector.reshape(-1, LANES)).reshape(-1)
    spread, whole = vector[: spread.size].reshape(8, -1), vector[spread.size :].reshape(3, depth)
    spread = lax.dynamic_slice_in_dim(spread, this_half * 4, 4)
    grad_b_qkv = spread[:, : 3 * width].reshape(4, 3, width).transpose(1, 0, 2).reshape(3, 4 * width)
    grad_b_up = spread[:, 3 * width :].reshape(-1)
    sums = whole[1:].reshape(2, 16, 2, depth // 32).transpose(0, 2, 1, 3).reshape(2, depth)
    grad_gain = (sums[1] - layernorm_bias * sums[0]) / layernorm_gain

    parts = exchange(cut(coords, mlp_grads, heads))
    grad_up_w, grad_down_w, grad_qkv_w, grad_out_w = unpack(coords, parts, hidden, width)
    return (
        mixed,
        d_tokens,
        grad_gain,
        sums[0],
        grad_qkv_w.transpose(1, 0, 2),
        grad_b_qkv,
        grad_out_w.T,
        whole[0],
        grad_up_w,
        grad_b_up,
        grad_down_w.T,
        whole[0],
    )


def solution(mesh):
    fine = Mesh(mesh.devices.reshape(SIZES), AXES)
    dp = ("zl", "x", "y", "c")
    in_specs = (
        P(AXES, None),
        P(),
        P(),
        P(dp, None, "mp"),
        P(None, "mp"),
        P("mp", dp),
        P(),
        P(dp, "mp"),
        P("mp"),
        P("mp", dp),
        P(),
        P(dp),
        P(AXES, None),
    )
    out_specs = (
        P(AXES, None),
        P(AXES, None),
        P(),
        P(),
        P(dp, None, "mp"),
        P(None, "mp"),
        P("mp", dp),
        P(),
        P(dp, "mp"),
        P("mp"),
        P("mp", dp),
        P(),
    )
    return jax.shard_map(
        per_device, mesh=fine, in_specs=in_specs, out_specs=out_specs, check_vma=False
    )
```

```python
import functools

import jax
import jax.numpy as jnp
from jax import lax
from jax.experimental import pallas as pl
from jax.experimental.pallas import tpu as pltpu
from jax.sharding import Mesh, PartitionSpec as P

HEAD_DIM = 64
ROT = 32
HALF = ROT // 2
LANES = 128
EPSILON = 1e-05

AXES = ("zl", "x", "y", "c", "mp")
SIZES = (2, 4, 4, 2, 2)
PLANE = ("x", "y")
PAIR = ("zl", "c")

BF16 = jnp.bfloat16
F32 = jnp.float32
MIB = 1024 * 1024
GIGA = 1000 * MIB


def flip(value, *axes):
    count = 2 ** len(axes)
    return lax.ppermute(value, axes, [(i, count - 1 - i) for i in range(count)])


def hop(value, axis, bits):
    return lax.ppermute(value, axis, [(i, i ^ bits) for i in range(4)])


def fold_kernel(*refs):
    inputs, keep_ref, sends = refs[:4], refs[4], refs[5:]
    rows = keep_ref.shape[1]
    for which in range(2):
        mine_ref, theirs_ref = inputs[2 * which : 2 * which + 2]
        for i in range(4):
            block = slice(i * rows, (i + 1) * rows)
            total = mine_ref[block, :].astype(F32) + theirs_ref[block, :].astype(F32)
            if i == 0:
                keep_ref[which] = total
            else:
                sends[i - 1][which] = total.astype(BF16)


def fold(*sums):
    rows, depth = sums[0].shape[0] // 4, sums[0].shape[1]
    tile = depth // 4
    keep, *sends = pl.pallas_call(
        fold_kernel,
        grid=(4,),
        in_specs=[pl.BlockSpec((4 * rows, tile), lambda j: (0, j))] * 4,
        out_specs=[pl.BlockSpec((2, rows, tile), lambda j: (0, 0, j))] * 4,
        out_shape=[like((2, rows, depth), F32)] + [like((2, rows, depth))] * 3,
        compiler_params=params(16),
        cost_estimate=cost(0, 26 * rows * depth),
        name="fold",
    )(*sums)
    return keep, sends


def sum_along_z(vector):
    return vector + flip(vector, "zl") + (flip(vector, "mp") + flip(vector, "zl", "mp"))


def sum_plane(vector):
    for axis in PLANE:
        vector = (vector + hop(vector, axis, 2)) + (hop(vector, axis, 1) + hop(vector, axis, 3))
    return vector


def attention_kernel(
    linear_ref,
    grad_ref,
    cos_ref,
    low_ref,
    high_ref,
    segment_col,
    segment_row,
    index_col,
    index_row,
    right_ref,
    query_ref,
    key_ref,
    value_ref,
    grad_query_ref,
    grad_key_ref,
):
    width = grad_ref.shape[1]
    scale = HEAD_DIM ** (-0.5)

    def rotated(tile, lanes, sign):
        cos, low, high = cos_ref[...], low_ref[...], high_ref[...]
        ahead = pltpu.roll(tile, lanes - HALF, 1)
        behind = pltpu.roll(tile, HALF, 1)
        return tile * cos + (ahead * low + behind * high) * sign

    for start in range(0, width, LANES):
        lanes = slice(start, start + LANES)
        query_ref[:, lanes] = (rotated(linear_ref[:, lanes], LANES, 1.0) * scale).astype(BF16)
        keys = linear_ref[:, width + start : width + start + LANES]
        key_ref[:, lanes] = rotated(keys, LANES, 1.0).astype(BF16)
        value_ref[:, lanes] = linear_ref[:, 2 * width + start : 2 * width + start + LANES].astype(BF16)
    allowed = (segment_col[...] == segment_row[0]) & (index_col[...] >= index_row[0])
    for start in range(0, width, HEAD_DIM):
        lanes = slice(start, start + HEAD_DIM)
        query, key, value = query_ref[:, lanes], key_ref[:, lanes], value_ref[:, lanes]
        grad = grad_ref[:, lanes]
        scores = lax.dot_general(query, key, (((1,), (1,)), ((), ())), preferred_element_type=F32)
        scores = jnp.where(allowed, scores, -1000000000.0)
        expo = jnp.exp(scores - jnp.max(scores, axis=1, keepdims=True))
        probs = expo / jnp.sum(expo, axis=1, keepdims=True)
        low_probs = probs.astype(BF16)
        attended = jnp.dot(low_probs, value, preferred_element_type=F32)
        right_ref[:, 3 * width + start : 3 * width + start + HEAD_DIM] = attended.astype(BF16)
        grad_probs = lax.dot_general(grad, value, (((1,), (1,)), ((), ())), preferred_element_type=F32)
        grad_values = lax.dot_general(
            low_probs, grad, (((0,), (0,)), ((), ())), preferred_element_type=F32
        )
        weighted = probs * grad_probs
        delta = jnp.sum(weighted, axis=1, keepdims=True)
        grad_scores = (weighted - probs * delta).astype(BF16)
        grad_query_ref[:, lanes] = jnp.dot(grad_scores, key, preferred_element_type=F32) * scale
        grad_key_ref[:, lanes] = lax.dot_general(
            grad_scores, query, (((0,), (0,)), ((), ())), preferred_element_type=F32
        )
        right_ref[:, 2 * width + start : 2 * width + start + HEAD_DIM] = grad_values.astype(BF16)
    for start in range(0, width, LANES):
        lanes = slice(start, start + LANES)
        right_ref[:, lanes] = rotated(grad_query_ref[:, lanes], LANES, -1.0).astype(BF16)
        right_ref[:, width + start : width + start + LANES] = rotated(
            grad_key_ref[:, lanes], LANES, -1.0
        ).astype(BF16)


def attention(linear, grad_attended, tables, segments, indices, length):
    rows, width = grad_attended.shape
    count = rows // length
    blocks = lambda lanes: pl.BlockSpec((length, lanes), lambda i: (i, 0))
    rowwise = pl.BlockSpec((1, 1, length), lambda i: (i, 0, 0))
    return pl.pallas_call(
        attention_kernel,
        grid=(count,),
        in_specs=[
            blocks(3 * width),
            blocks(width),
            blocks(LANES),
            blocks(LANES),
            blocks(LANES),
            blocks(1),
            rowwise,
            blocks(1),
            rowwise,
        ],
        out_specs=blocks(4 * width),
        out_shape=jax.ShapeDtypeStruct((rows, 4 * width), BF16),
        scratch_shapes=[pltpu.VMEM((length, width), BF16)] * 3
        + [pltpu.VMEM((length, width), F32)] * 2,
        compiler_params=params(60),
        cost_estimate=cost(18 * GIGA, 8 * MIB),
        name="attention",
    )(
        linear,
        grad_attended,
        *tables,
        segments.reshape(rows, 1),
        segments.reshape(count, 1, length),
        indices.reshape(rows, 1),
        indices.reshape(count, 1, length),
    )


ANY = pl.BlockSpec(memory_space=pl.ANY)
WHOLE = pl.BlockSpec(memory_space=pltpu.VMEM)
SCALARS = pl.BlockSpec(memory_space=pltpu.SMEM)


def like(shape, dtype=BF16):
    return jax.ShapeDtypeStruct(shape, dtype)


def params(mib):
    return pltpu.CompilerParams(vmem_limit_bytes=mib * MIB)


def cost(flops, moved):
    return pl.CostEstimate(flops=flops, bytes_accessed=moved, transcendentals=0)


def slot_of(coords, bits):
    return (coords[0] * 2 + coords[3]) ^ bits


def pack_kernel(coords, up_ref, down_ref, qkv_ref, out_ref, segment_ref, *parts):
    hidden, width = up_ref.shape[1] // 4, out_ref.shape[1] // 4
    segments = segment_ref[...].astype(F32).astype(BF16)
    segments = jnp.broadcast_to(segments, (up_ref.shape[0], segments.shape[1]))
    for bits in range(4):
        slot = slot_of(coords, bits)
        wide = pl.ds(pl.multiple_of(slot * hidden, hidden), hidden)
        narrow = pl.ds(pl.multiple_of(slot * width, width), width)
        part = parts[bits]
        for kind in range(3):
            part[:, kind * width : (kind + 1) * width] = qkv_ref[kind, :, narrow]
        start = 4 * width
        part[:, start - width : start] = out_ref[:, narrow]
        part[:, start : start + hidden] = up_ref[:, wide]
        part[:, start + hidden : start + 2 * hidden] = down_ref[:, wide]
        part[:, start + 2 * hidden :] = segments


def pack(coords, w_up, down_t, qkv_t, out_t, segments):
    rows, hidden, width = w_up.shape[0], w_up.shape[1] // 4, out_t.shape[1] // 4
    return pl.pallas_call(
        pack_kernel,
        in_specs=[SCALARS] + [WHOLE] * 5,
        out_specs=[WHOLE] * 4,
        out_shape=[like((rows, 2 * hidden + 4 * width + segments.shape[0]))] * 4,
        compiler_params=params(16),
        name="pack",
    )(coords, w_up, down_t, qkv_t, out_t, segments.reshape(1, -1))


def order_kernel(coords, *refs):
    parts, out = refs[:4], refs[4]
    for bits in range(4):
        out[coords[0] ^ (bits >> 1), coords[3] ^ (bits & 1)] = parts[bits][:, : out.shape[3]]


def order(coords, parts, columns):
    rows = parts[0].shape[0]
    out = pl.pallas_call(
        order_kernel,
        in_specs=[SCALARS] + [WHOLE] * 4,
        out_specs=WHOLE,
        out_shape=like((2, 2, rows, columns)),
        compiler_params=params(16),
        name="order",
    )(coords, *parts)
    return out.reshape(4 * rows, columns)


def join_kernel(*refs):
    parts, out, sem = refs[:-2], refs[-2], refs[-1]
    copies = []
    for i, part in enumerate(parts):
        copies.append(pltpu.make_async_copy(part, out.at[i], sem.at[i]))
        copies[-1].start()
    for copy in copies:
        copy.wait()


def join(*parts):
    return pl.pallas_call(
        join_kernel,
        in_specs=[ANY] * len(parts),
        out_specs=ANY,
        out_shape=like((len(parts),) + parts[0].shape),
        scratch_shapes=[pltpu.SemaphoreType.DMA((len(parts),))],
        compiler_params=params(16),
        name="join",
    )(*parts)


def tokens_kernel(mine_ref, other_ref, rows_ref, columns_ref):
    @pl.when(pl.program_id(1) == 0)
    def _():
        rows_ref[0] = mine_ref[0, 0]
        columns_ref[0] = mine_ref[0, 0].T

    @pl.when(pl.program_id(1) == 1)
    def _():
        rows_ref[0] = other_ref[0, 0]
        columns_ref[0] = other_ref[0, 0].T


def gather_tokens(*pairs):
    mine = join(*pairs)
    other = flip(mine, "c")
    _, _, rows, depth = mine.shape
    block = (1, 1, rows, depth)
    return pl.pallas_call(
        tokens_kernel,
        grid=(2, 2, 4),
        in_specs=[
            pl.BlockSpec(block, lambda w, c, z: (jnp.where(c == 0, z, 3), w, 0, 0)),
            pl.BlockSpec(block, lambda w, c, z: (jnp.where(c == 1, z, 0), w, 0, 0)),
        ],
        out_specs=[
            pl.BlockSpec((1, rows, depth), lambda w, c, z: (w, 4 * c + z, 0)),
            pl.BlockSpec((1, depth, rows), lambda w, c, z: (w, 0, 4 * c + z)),
        ],
        out_shape=[like((2, 8 * rows, depth)), like((2, depth, 8 * rows))],
        compiler_params=params(32),
        cost_estimate=cost(0, 8 * mine.size * 2),
        name="tokens",
    )(mine, other)


def mlp_kernel(pair_ref, bias_ref, up_ref, down_ref, hidden_ref, sums_ref):
    slope = 0.7978845608028654
    up = jnp.dot(pair_ref[0], up_ref[...], preferred_element_type=F32) + bias_ref[...]
    square = up * up
    wave = jnp.tanh(slope * (up + 0.044715 * (square * up)))
    half = 0.5 * (1.0 + wave)
    hidden_ref[1] = (up * half).astype(BF16)
    rise = half + (0.5 * up) * (1.0 - wave * wave) * (slope * (1.0 + 0.134145 * square))
    grad = jnp.dot(pair_ref[1], down_ref[...], preferred_element_type=F32) * rise
    low = grad.astype(BF16)
    hidden_ref[0] = low
    sums_ref[...] = jnp.sum(low.astype(F32), axis=0, keepdims=True)


def mlp(pair, bias, weights):
    rows, depth = pair.shape[1:]
    hidden = bias.shape[0]
    tile = 256
    tiles = hidden // tile
    start = (weights.shape[1] - 2 * hidden) // tile
    column = lambda j: (0, j)
    return pl.pallas_call(
        mlp_kernel,
        grid=(tiles,),
        in_specs=[
            pl.BlockSpec((2, rows, depth), lambda j: (0, 0, 0), pipeline_mode=pl.Buffered(1)),
            pl.BlockSpec((1, tile), column),
            pl.BlockSpec((depth, tile), lambda j: (0, start + j)),
            pl.BlockSpec((depth, tile), lambda j: (0, start + tiles + j)),
        ],
        out_specs=[
            pl.BlockSpec((2, rows, tile), lambda j: (0, 0, j)),
            pl.BlockSpec((1, tile), column),
        ],
        out_shape=[like((2, rows, hidden)), like((1, hidden), F32)],
        compiler_params=params(60),
        cost_estimate=cost(4 * rows * depth * hidden, 20 * MIB),
        name="mlp",
    )(pair, bias.reshape(1, -1), weights, weights)


def grads_kernel(left_ref, right_ref, out_ref):
    out_ref[...] = jnp.dot(left_ref[0], right_ref[0], preferred_element_type=F32).astype(BF16)


def weight_grads(pair_t, right, tile):
    _, depth, rows = pair_t.shape
    count, _, columns = right.shape
    tiles = columns // tile
    return pl.pallas_call(
        grads_kernel,
        grid=(count, tiles, 2),
        in_specs=[
            pl.BlockSpec((1, depth // 2, rows), lambda i, j, k: (i, k, 0)),
            pl.BlockSpec((1, rows, tile), lambda i, j, k: (i, 0, j)),
        ],
        out_specs=pl.BlockSpec((depth // 2, tile), lambda i, j, k: (k, i * tiles + j)),
        out_shape=like((depth, count * columns)),
        compiler_params=params(60),
        cost_estimate=cost(2 * depth * rows * count * columns, 2 * (pair_t.size + right.size * 2)),
        name="weight_grads",
    )(pair_t, right)


def head_grads_kernel(coords, left_ref, right_ref, *refs):
    outs, product_ref = refs[:-1], refs[-1]
    x, y = coords[1], coords[2]
    tile = product_ref.shape[3]
    lanes = pl.ds(pl.multiple_of(pl.program_id(0) * tile, tile), tile)
    product = jnp.dot(left_ref[0], right_ref[...], preferred_element_type=F32).astype(BF16)
    product_ref[...] = product.reshape(product_ref.shape)
    for y_bits in range(4):
        for x_bits in range(4):
            chip = (x ^ x_bits) * 4 + (y ^ y_bits)
            if y_bits == 2:
                out, i = outs[3 + x_bits // 2], x_bits % 2
            else:
                out, i = outs[(0, 1, None, 2)[y_bits]], x_bits
            out[i, :, :, lanes] = product_ref[chip]


def head_grads(coords, pair_t, right):
    _, depth, rows = pair_t.shape
    columns = right.shape[1]
    tile, block = columns // 4, depth // 32
    full, half = like((4, 2, block, columns)), like((2, 2, block, columns))
    return pl.pallas_call(
        head_grads_kernel,
        grid=(4,),
        in_specs=[
            SCALARS,
            pl.BlockSpec((1, depth, rows), lambda j: (j // 3, 0, 0)),
            pl.BlockSpec((rows, tile), lambda j: (0, j)),
        ],
        out_specs=[WHOLE] * 5,
        out_shape=[full, full, full, half, half],
        scratch_shapes=[pltpu.VMEM((16, 2, block, tile), BF16)],
        compiler_params=params(60),
        cost_estimate=cost(2 * depth * rows * columns, 16 * MIB),
        name="head_grads",
    )(coords, pair_t, right)


def bump_kernel(chunk_ref, part_ref, out_ref):
    out_ref[...] = (chunk_ref[...].astype(F32) + part_ref[...].astype(F32)).astype(BF16)


def bump(chunk, part, half):
    spec = pl.BlockSpec(part.shape, lambda i: (half, 0, 0, 0))
    return pl.pallas_call(
        bump_kernel,
        grid=(1,),
        in_specs=[spec, pl.BlockSpec(part.shape, lambda i: (0, 0, 0, 0))],
        out_specs=spec,
        out_shape=like(chunk.shape),
        input_output_aliases={0: 0},
        compiler_params=params(16),
        name="bump",
    )(chunk, part)


def near_kernel(own_ref, one_ref, three_ref, keep_ref, *sends):
    for i in range(4):
        total = own_ref[i].astype(F32) + (one_ref[i].astype(F32) + three_ref[i].astype(F32))
        if i == 0:
            keep_ref[...] = total
        else:
            sends[i - 1][...] = total.astype(BF16)


def near_sums(own, one, three):
    shape = own.shape[1:]
    return pl.pallas_call(
        near_kernel,
        in_specs=[WHOLE] * 3,
        out_specs=[WHOLE] * 4,
        out_shape=[like(shape, F32)] + [like(shape)] * 3,
        compiler_params=params(16),
        name="near",
    )(own, one, three)


def cut_kernel(coords, mlp_ref, *refs):
    heads, outs = refs[:4], refs[4:]
    rows, columns = outs[0].shape[0], mlp_ref.shape[1]
    for bits in range(4):
        start = pl.multiple_of(slot_of(coords, bits) * rows, rows)
        some = pl.ds(start, rows)
        outs[bits][:, :columns] = mlp_ref[some, :]
        total = heads[0][some, :]
        for head in heads[1:]:
            total = total + head[some, :].astype(F32)
        outs[bits][:, columns:] = total.astype(BF16)


def cut(coords, mlp_grads, heads):
    rows = mlp_grads.shape[0]
    heads = [head.reshape(rows, -1) for head in heads]
    columns = mlp_grads.shape[1] + heads[0].shape[1]
    return pl.pallas_call(
        cut_kernel,
        in_specs=[SCALARS] + [WHOLE] * 5,
        out_specs=[WHOLE] * 4,
        out_shape=[like((rows // 4, columns))] * 4,
        compiler_params=params(16),
        name="cut",
    )(coords, mlp_grads, *heads)


def combine_kernel(products, *refs):
    mine_ref, theirs_ref = refs[2 * products : 2 * products + 2] if len(refs) == 2 * products + 2 else refs[-3:-1]
    contract = (((1,), (1,)), ((), ()))
    total = None
    for i in range(products):
        left, right = refs[2 * i], refs[2 * i + 1]
        left = left[0] if len(left.shape) == 3 else left[...]
        product = lax.dot_general(left, right[...], contract, preferred_element_type=F32)
        total = product if total is None else total + product
    half = mine_ref.shape[0]
    mine_ref[...] = total[:half].astype(BF16)
    theirs_ref[...] = total[half:].astype(BF16)
    if len(refs) > 2 * products + 2:
        rows_ref, sums_ref = refs[2 * products], refs[-1]
        sums_ref[0:1, :] = jnp.sum(total, axis=0, keepdims=True)
        sums_ref[1:2, :] = jnp.sum(total * rows_ref[0].astype(F32), axis=0, keepdims=True)


def combine(hidden_pair, side, right, weights, width, pair=None):
    _, rows, hidden = hidden_pair.shape
    depth, tile = weights.shape[0], 256
    where = 0 if side == 0 else right.shape[1] // width - 1
    first = right.shape[1] // hidden
    column = lambda i: (0, i)
    specs = [
        pl.BlockSpec((1, rows, hidden), lambda i: (side, 0, 0)),
        pl.BlockSpec((tile, hidden), lambda i: (i, first + side)),
        pl.BlockSpec((rows, width), lambda i: (0, where)),
        pl.BlockSpec((tile, width), lambda i: (i, where)),
    ]
    arrays = [hidden_pair, weights, right, weights]
    out_specs = [pl.BlockSpec((rows // 2, tile), column)] * 2
    shapes = [like((rows // 2, depth))] * 2
    if pair is not None:
        specs.append(pl.BlockSpec((1, rows, tile), lambda i: (0, 0, i)))
        arrays.append(pair)
        out_specs.append(pl.BlockSpec((2, tile), column))
        shapes.append(like((2, depth), F32))
    return pl.pallas_call(
        functools.partial(combine_kernel, 2),
        grid=(depth // tile,),
        in_specs=specs,
        out_specs=out_specs,
        out_shape=shapes,
        compiler_params=params(60),
        cost_estimate=cost(2 * rows * depth * (hidden + width), 16 * MIB),
        name="combine",
    )(*arrays)


def project_kernel(pair_ref, bias_ref, weights_ref, linear_ref, grad_ref):
    product = jnp.dot(pair_ref[0], weights_ref[...], preferred_element_type=F32)

    @pl.when(pl.program_id(0) < 3)
    def _():
        linear_ref[...] = product + bias_ref[...]

    @pl.when(pl.program_id(0) == 3)
    def _():
        grad_ref[...] = product.astype(BF16)


def project(pair, bias, weights):
    rows, depth = pair.shape[1:]
    width = bias.shape[0] // 3
    return pl.pallas_call(
        project_kernel,
        grid=(4,),
        in_specs=[
            pl.BlockSpec((1, rows, depth), lambda j: (j // 3, 0, 0)),
            pl.BlockSpec((1, width), lambda j: (0, jnp.minimum(j, 2))),
            pl.BlockSpec((depth, width), lambda j: (0, j)),
        ],
        out_specs=[
            pl.BlockSpec((rows, width), lambda j: (0, jnp.minimum(j, 2))),
            pl.BlockSpec((rows, width), lambda j: (0, 0)),
        ],
        out_shape=[like((rows, 3 * width), F32), like((rows, width))],
        compiler_params=params(60),
        cost_estimate=cost(8 * rows * depth * width, 16 * MIB),
        name="project",
    )(pair, bias.reshape(1, -1), weights)


def exchange(parts):
    return [parts[0], flip(parts[1], "c"), flip(parts[2], "zl"), flip(parts[3], "zl", "c")]


def unpack_kernel(coords, *refs):
    parts, (up_ref, down_ref, qkv_ref, out_ref) = refs[:4], refs[4:]
    hidden, width = up_ref.shape[1] // 4, out_ref.shape[1] // 4
    for bits in range(4):
        slot = slot_of(coords, bits)
        wide = pl.ds(pl.multiple_of(slot * hidden, hidden), hidden)
        narrow = pl.ds(pl.multiple_of(slot * width, width), width)
        part = parts[bits]
        up_ref[:, wide] = part[:, :hidden].astype(F32)
        down_ref[:, wide] = part[:, hidden : 2 * hidden].astype(F32)
        for kind in range(3):
            start = 2 * hidden + kind * width
            qkv_ref[kind, :, narrow] = part[:, start : start + width].astype(F32)
        out_ref[:, narrow] = part[:, 2 * hidden + 3 * width :].astype(F32)


def unpack(coords, parts, hidden, width):
    rows = parts[0].shape[0]
    wide, narrow = (rows, 4 * hidden), (rows, 4 * width)
    return pl.pallas_call(
        unpack_kernel,
        in_specs=[SCALARS] + [WHOLE] * 4,
        out_specs=[WHOLE] * 4,
        out_shape=[like(shape, F32) for shape in (wide, wide, (3,) + narrow, narrow)],
        compiler_params=params(16),
        name="unpack",
    )(coords, *parts)


def turn(dest, value, back):
    block = value.shape[1] // 32
    for chip in range(16):
        for zl in range(2):
            natural, inside = (zl * 16 + chip) * block, (chip * 2 + zl) * block
            source, target = (inside, natural) if back else (natural, inside)
            dest[:, target : target + block] = value[:, source : source + block].astype(dest.dtype)


def standardize(tokens):
    rows = tokens.astype(F32)
    centered = rows - jnp.mean(rows, axis=1, keepdims=True)
    scale = lax.rsqrt(jnp.mean(centered * centered, axis=1, keepdims=True) + EPSILON)
    return rows, centered * scale, scale


def enter_kernel(tokens_ref, cot_ref, gain_ref, bias_ref, pair_ref, sums_ref):
    _, standard, _ = standardize(tokens_ref[...])
    turn(pair_ref.at[0], (standard * gain_ref[...] + bias_ref[...]).astype(BF16), False)
    turn(pair_ref.at[1], cot_ref[...], False)
    sums_ref[...] = jnp.sum(cot_ref[...].astype(F32), axis=0, keepdims=True)


def enter(tokens, cotangent, gain, bias):
    return pl.pallas_call(
        enter_kernel,
        in_specs=[WHOLE] * 4,
        out_specs=[WHOLE] * 2,
        out_shape=[like((2,) + tokens.shape), like((1, tokens.shape[1]), F32)],
        compiler_params=params(16),
        name="enter",
    )(tokens, cotangent, gain.reshape(1, -1), bias.reshape(1, -1))


def leave_kernel(tokens_ref, cot_ref, gain_ref, bias_ref, *refs):
    mixed_ref, grad_ref, branch_ref, normed_ref = refs[-4:]
    for which, target in ((0, normed_ref), (1, branch_ref)):
        total = refs[0][which]
        for part in refs[1:4]:
            total = total + part[which].astype(F32)
        turn(target, total, True)
    rows, standard, scale = standardize(tokens_ref[...])
    mixed_ref[...] = (rows + branch_ref[...] + bias_ref[...]).astype(BF16)
    grad = normed_ref[...] * gain_ref[...]
    level = jnp.mean(grad, axis=1, keepdims=True)
    slope = jnp.mean(grad * standard, axis=1, keepdims=True)
    grad_ref[...] = cot_ref[...].astype(F32) + scale * (grad - level - standard * slope)


def leave(tokens, cotangent, gain, bias, sums):
    shape = tokens.shape
    return pl.pallas_call(
        leave_kernel,
        in_specs=[WHOLE] * 8,
        out_specs=[WHOLE] * 2,
        out_shape=[like(shape), like(shape, F32)],
        scratch_shapes=[pltpu.VMEM(shape, F32)] * 2,
        compiler_params=params(24),
        name="leave",
    )(tokens, cotangent, gain.reshape(1, -1), bias.reshape(1, -1), *sums)


def scatter_plane(grads):
    return lax.psum_scatter(grads, PLANE, scatter_dimension=0, tiled=True)


def per_device(
    tokens,
    layernorm_gain,
    layernorm_bias,
    w_qkv,
    b_qkv,
    w_out,
    b_out,
    w_up,
    b_up,
    w_down,
    b_down,
    segments,
    cotangent,
):
    depth = tokens.shape[1]
    length = segments.shape[0]
    half_rows = tokens.shape[0]
    width = w_out.shape[0] // 4
    hidden = w_down.shape[0] // 4
    rows = w_up.shape[0]
    coords = jnp.stack([lax.axis_index(axis) for axis in AXES]).astype(jnp.int32)
    place_here = coords[0] * 2 + coords[3]
    this_half = coords[4]

    parts = exchange(pack(coords, w_up, w_down.T, w_qkv.transpose(1, 0, 2), w_out.T, segments))
    shard = order(coords, parts, 2 * hidden + 4 * width)
    weights = lax.all_gather(shard, PLANE, axis=0, tiled=True)

    pair, grad_b_out = enter(tokens, cotangent, layernorm_gain, layernorm_bias)
    _, pair = lax.optimization_barrier((shard, pair))
    near, far, opposite = flip(pair, "zl"), flip(pair, "zl", "mp"), flip(pair, "mp")
    pair, pair_t = gather_tokens(pair, opposite, near, far)

    doc = jnp.stack([parts[k][0, -length:] for k in (0, 2, 1, 3)]).astype(jnp.int32)
    doc = doc.reshape(4, 2, half_rows)
    doc = jnp.where(this_half == 0, doc, doc[:, ::-1]).reshape(4, length)
    halves = jnp.stack([this_half, 1 - this_half]) * half_rows
    index = (halves[:, None] + jnp.arange(half_rows, dtype=jnp.int32)).reshape(1, length)
    index = jnp.broadcast_to(index, (4, length)).astype(jnp.int32)
    same_doc = doc[:, :, None] == doc[:, None, :]
    doc_start = jnp.min(jnp.where(same_doc, index[:, None, :], length), axis=2)
    positions = (index - doc_start).astype(F32).reshape(-1)
    inv_freq = 10000.0 ** (-(jnp.arange(HALF, dtype=F32) * 2.0 / ROT))
    angles = positions[:, None] * inv_freq
    cos, sin = jnp.cos(angles), jnp.sin(angles)
    nothing = jnp.zeros_like(cos)
    rest = (positions.shape[0], HEAD_DIM - ROT)
    repeat = LANES // HEAD_DIM
    cos_table = jnp.tile(jnp.concatenate([cos, cos, jnp.ones(rest, F32)], axis=1), (1, repeat))
    low_table = jnp.tile(jnp.concatenate([-sin, nothing, jnp.zeros(rest, F32)], axis=1), (1, repeat))
    high_table = jnp.tile(jnp.concatenate([nothing, sin, jnp.zeros(rest, F32)], axis=1), (1, repeat))

    b_up_here = lax.dynamic_slice_in_dim(b_up, place_here * hidden, hidden)
    b_qkv_here = lax.dynamic_slice_in_dim(b_qkv, place_here * width, width, axis=1).reshape(-1)

    tables = (cos_table, low_table, high_table, doc, index)
    pair, tables = lax.optimization_barrier((pair, tables))
    hidden_pair, grad_b_up = mlp(pair, b_up_here, weights)
    mlp_grads = scatter_plane(weight_grads(pair_t, hidden_pair, hidden // 2))

    pair, hidden_pair = lax.optimization_barrier((pair, hidden_pair))
    linear, grad_attended = project(pair, b_qkv_here, weights)
    right = attention(linear, grad_attended, tables[:3], *tables[3:], length)

    chunks = head_grads(coords, pair_t, right)
    chunks, hidden_pair = lax.optimization_barrier((chunks, hidden_pair))
    own, one, three, two_low, two_high = chunks
    low, high = hop(two_low, "y", 1), hop(two_high, "y", 3)
    normed, normed_theirs, sums = combine(hidden_pair, 0, right, weights, 3 * width, pair)
    normed_theirs = flip(normed_theirs, "c")
    branch, branch_theirs = combine(hidden_pair, 1, right, weights, width)

    grad_b_heads = jnp.sum(right[:, : 3 * width].astype(F32), axis=0)
    slices = jnp.concatenate([grad_b_heads, grad_b_up[0]])
    slot = this_half * 4 + place_here
    spread = jnp.zeros((8,) + slices.shape, F32)
    spread = lax.dynamic_update_slice(spread, slices[None], (slot, 0))
    vector = jnp.concatenate([spread.reshape(-1), grad_b_out[0], sums.reshape(-1)])
    vector = vector.reshape(-1, LANES)
    vector = vector + flip(vector, "c")

    low, high, normed_theirs, branch, branch_theirs, vector = lax.optimization_barrier(
        (low, high, normed_theirs, branch, branch_theirs, vector)
    )
    branch_theirs = flip(branch_theirs, "c")
    one, three = hop(bump(one, high, 1), "y", 1), hop(bump(three, low, 0), "y", 3)
    keep, sends = fold(normed, normed_theirs, branch, branch_theirs)
    along_z = [flip(sends[1], "zl"), flip(sends[2], "zl", "mp"), flip(sends[0], "mp")]
    one, three, keep, vector = lax.optimization_barrier((one, three, keep, vector))
    heads = near_sums(own, one, three)
    heads = [heads[0]] + [hop(part, "x", bits) for part, bits in zip(heads[1:], (1, 2, 3))]
    parts, vector = lax.optimization_barrier((cut(coords, mlp_grads, heads), vector))
    parts = exchange(parts)
    vector = sum_plane(sum_along_z(vector)).reshape(-1)
    mixed, d_tokens = leave(
        tokens, cotangent, layernorm_gain, b_out + b_down, [keep] + along_z
    )
    spread, whole = vector[: spread.size].reshape(8, -1), vector[spread.size :].reshape(3, depth)
    spread = lax.dynamic_slice_in_dim(spread, this_half * 4, 4)
    grad_b_qkv = spread[:, : 3 * width].reshape(4, 3, width).transpose(1, 0, 2).reshape(3, 4 * width)
    grad_b_up = spread[:, 3 * width :].reshape(-1)
    sums = whole[1:].reshape(2, 16, 2, depth // 32).transpose(0, 2, 1, 3).reshape(2, depth)
    grad_gain = (sums[1] - layernorm_bias * sums[0]) / layernorm_gain

    grad_up_w, grad_down_w, grad_qkv_w, grad_out_w = unpack(coords, parts, hidden, width)
    return (
        mixed,
        d_tokens,
        grad_gain,
        sums[0],
        grad_qkv_w.transpose(1, 0, 2),
        grad_b_qkv,
        grad_out_w.T,
        whole[0],
        grad_up_w,
        grad_b_up,
        grad_down_w.T,
        whole[0],
    )


def solution(mesh):
    fine = Mesh(mesh.devices.reshape(SIZES), AXES)
    dp = ("zl", "x", "y", "c")
    in_specs = (
        P(AXES, None),
        P(),
        P(),
        P(dp, None, "mp"),
        P(None, "mp"),
        P("mp", dp),
        P(),
        P(dp, "mp"),
        P("mp"),
        P("mp", dp),
        P(),
        P(dp),
        P(AXES, None),
    )
    out_specs = (
        P(AXES, None),
        P(AXES, None),
        P(),
        P(),
        P(dp, None, "mp"),
        P(None, "mp"),
        P("mp", dp),
        P(),
        P(dp, "mp"),
        P("mp"),
        P("mp", dp),
        P(),
    )
    return jax.shard_map(
        per_device, mesh=fine, in_specs=in_specs, out_specs=out_specs, check_vma=False
    )
```

```python
import functools

import jax
import jax.numpy as jnp
from jax import lax
from jax.experimental import pallas as pl
from jax.experimental.pallas import tpu as pltpu
from jax.sharding import Mesh, PartitionSpec as P

HEAD_DIM = 64
ROT = 32
HALF = ROT // 2
LANES = 128
EPSILON = 1e-05

AXES = ("zl", "x", "y", "c", "mp")
SIZES = (2, 4, 4, 2, 2)
PLANE = ("x", "y")
PAIR = ("zl", "c")

BF16 = jnp.bfloat16
F32 = jnp.float32
MIB = 1024 * 1024
GIGA = 1000 * MIB
ANY = pl.BlockSpec(memory_space=pl.ANY)
WHOLE = pl.BlockSpec(memory_space=pltpu.VMEM)
SCALARS = pl.BlockSpec(memory_space=pltpu.SMEM)


def flip(value, *axes):
    count = 2 ** len(axes)
    return lax.ppermute(value, axes, [(i, count - 1 - i) for i in range(count)])


def hop(value, axis, bits):
    return lax.ppermute(value, axis, [(i, i ^ bits) for i in range(4)])


def fold_kernel(*refs):
    inputs, keep_ref, sends = refs[:4], refs[4], refs[5:]
    rows = keep_ref.shape[1]

    def add(mine_ref, theirs_ref):
        for which in range(2):
            for i in range(4):
                block = slice(i * rows, (i + 1) * rows)
                total = mine_ref[which, block, :].astype(F32) + theirs_ref[which, block, :].astype(F32)
                if i == 0:
                    keep_ref[which] = total
                else:
                    sends[i - 1][which] = total.astype(BF16)

    pl.when(pl.program_id(0) < 2)(lambda: add(inputs[0], inputs[1]))
    pl.when(pl.program_id(0) >= 2)(lambda: add(inputs[2], inputs[3]))


def fold(*halves):
    _, rows, half = halves[0].shape
    rows, tile = rows // 4, half // 2
    low = pl.BlockSpec((2, 4 * rows, tile), lambda j: (0, 0, jnp.minimum(j, 1)))
    high = pl.BlockSpec((2, 4 * rows, tile), lambda j: (0, 0, jnp.maximum(j - 2, 0)))
    keep, *sends = pl.pallas_call(
        fold_kernel,
        grid=(4,),
        in_specs=[low, low, high, high],
        out_specs=[pl.BlockSpec((2, rows, tile), lambda j: (0, 0, j))] * 4,
        out_shape=[like((2, rows, 2 * half), F32)] + [like((2, rows, 2 * half))] * 3,
        compiler_params=params(16),
        cost_estimate=cost(0, 52 * rows * half),
        name="fold",
    )(*halves)
    return keep, sends


def heads_kernel(
    pair_ref,
    weights_ref,
    bias_ref,
    trig_ref,
    segment_col,
    segment_row,
    index_col,
    index_row,
    right_ref,
    linear_ref,
    query_ref,
    key_ref,
    value_ref,
    grad_ref,
    grad_query_ref,
    grad_key_ref,
    attended_ref,
):
    width = grad_ref.shape[1]
    length = grad_ref.shape[0]
    scale = HEAD_DIM ** (-0.5)
    linear_ref[...] = (
        jnp.dot(pair_ref[0], weights_ref[:, : 3 * width], preferred_element_type=F32)
        + bias_ref[...]
    )
    grad_ref[...] = jnp.dot(
        pair_ref[1], weights_ref[:, 3 * width :], preferred_element_type=F32
    ).astype(BF16)

    def rotated(tile, sign):
        ahead = pltpu.roll(tile, LANES - HALF, 1)
        behind = pltpu.roll(tile, HALF, 1)
        turned = ahead * trig_ref[:, LANES : 2 * LANES] + behind * trig_ref[:, 2 * LANES :]
        return tile * trig_ref[:, :LANES] + turned * sign

    for start in range(0, width, LANES):
        lanes = slice(start, start + LANES)
        query_ref[:, lanes] = (rotated(linear_ref[:, lanes], 1.0) * scale).astype(BF16)
        keys = linear_ref[:, width + start : width + start + LANES]
        key_ref[:, lanes] = rotated(keys, 1.0).astype(BF16)
        value_ref[:, lanes] = linear_ref[:, 2 * width + start : 2 * width + start + LANES].astype(BF16)
    allowed = (segment_row[0] == segment_col[...]) & (index_row[0] >= index_col[...])
    both = (((1,), (1,)), ((), ()))
    value_t, key_t = value_ref[...].T, key_ref[...].T
    for start in range(0, width, HEAD_DIM):
        lanes = slice(start, start + HEAD_DIM)
        query, key, value = query_ref[:, lanes], key_ref[:, lanes], value_ref[:, lanes]
        grad = grad_ref[:, lanes]
        scores = lax.dot_general(key, query, both, preferred_element_type=F32)
        scores = jnp.where(allowed, scores, -1000000000.0)
        expo = jnp.exp(scores - jnp.max(scores, axis=0, keepdims=True))
        probs = expo * (1.0 / jnp.sum(expo, axis=0, keepdims=True))
        low_probs = probs.astype(BF16)
        attended_ref[lanes, :] = jnp.dot(value_t[lanes], low_probs, preferred_element_type=F32)
        grad_probs = lax.dot_general(value, grad, both, preferred_element_type=F32)
        grad_values = jnp.dot(low_probs, grad, preferred_element_type=F32)
        weighted = probs * grad_probs
        delta = jnp.sum(weighted, axis=0, keepdims=True)
        grad_scores = (weighted - probs * delta).astype(BF16)
        grad_query_ref[lanes, :] = jnp.dot(key_t[lanes], grad_scores, preferred_element_type=F32) * scale
        grad_key_ref[:, lanes] = jnp.dot(grad_scores, query, preferred_element_type=F32)
        right_ref[:, 2 * width + start : 2 * width + start + HEAD_DIM] = grad_values.astype(BF16)
    right_ref[:, 3 * width :] = attended_ref[...].T.astype(BF16)
    linear_ref[:, :width] = grad_query_ref[...].T
    for start in range(0, width, LANES):
        lanes = slice(start, start + LANES)
        right_ref[:, lanes] = rotated(linear_ref[:, lanes], -1.0).astype(BF16)
        right_ref[:, width + start : width + start + LANES] = rotated(
            grad_key_ref[:, lanes], -1.0
        ).astype(BF16)


def heads(pair, weights, bias, tables, length):
    _, rows, depth = pair.shape
    width = bias.shape[0] // 3
    blocks = lambda lanes: pl.BlockSpec((length, lanes), lambda i: (i, 0))
    rowwise = pl.BlockSpec((1, 1, length), lambda i: (i, 0, 0))
    return pl.pallas_call(
        heads_kernel,
        grid=(rows // length,),
        in_specs=[
            pl.BlockSpec((2, length, depth), lambda i: (0, i, 0)),
            pl.BlockSpec((depth, 4 * width), lambda i: (0, 0), pipeline_mode=pl.Buffered(1)),
            pl.BlockSpec((1, 3 * width), lambda i: (0, 0)),
            blocks(3 * LANES),
            blocks(1),
            rowwise,
            blocks(1),
            rowwise,
        ],
        out_specs=blocks(4 * width),
        out_shape=like((rows, 4 * width)),
        scratch_shapes=[pltpu.VMEM((length, 3 * width), F32)]
        + [pltpu.VMEM((length, width), BF16)] * 4
        + [
            pltpu.VMEM((width, length), F32),
            pltpu.VMEM((length, width), F32),
            pltpu.VMEM((width, length), F32),
        ],
        compiler_params=params(32),
        cost_estimate=cost(26 * GIGA, 10 * MIB),
        name="heads",
    )(pair, weights, bias.reshape(1, -1), *tables)


def tables_kernel(cos_ref, sin_ref, *refs):
    inputs, outputs = refs[:4], refs[5:]
    trig_ref = refs[4]
    cos, sin = cos_ref[...], sin_ref[...]
    trig_ref[...] = jnp.zeros_like(trig_ref)
    for start in range(0, LANES, HEAD_DIM):
        rest = (cos.shape[0], HEAD_DIM - ROT)
        trig_ref[:, start : start + HALF] = cos
        trig_ref[:, start + HALF : start + ROT] = cos
        trig_ref[:, start + ROT : start + HEAD_DIM] = jnp.ones(rest, F32)
        trig_ref[:, LANES + start : LANES + start + HALF] = -sin
        trig_ref[:, 2 * LANES + start + HALF : 2 * LANES + start + ROT] = sin
    for source, target in zip(inputs, outputs):
        target[...] = source[...]


def rotary_tables(doc, index):
    count, length = doc.shape
    rows = count * length
    same_doc = doc[:, :, None] == doc[:, None, :]
    doc_start = jnp.min(jnp.where(same_doc, index[:, None, :], length), axis=2)
    positions = (index - doc_start).astype(F32).reshape(-1)
    inv_freq = 10000.0 ** (-(jnp.arange(HALF, dtype=F32) * 2.0 / ROT))
    angles = positions[:, None] * inv_freq
    column, row = (rows, 1), (count, 1, length)
    shapes = [column, row, column, row]
    passed = [value.reshape(shape) for value, shape in zip((doc, doc, index, index), shapes)]
    return pl.pallas_call(
        tables_kernel,
        in_specs=[WHOLE] * 6,
        out_specs=[WHOLE] * 5,
        out_shape=[like((rows, 3 * LANES), F32)] + [like(shape, jnp.int32) for shape in shapes],
        compiler_params=params(16),
        name="tables",
    )(jnp.cos(angles), jnp.sin(angles), *passed)


def like(shape, dtype=BF16):
    return jax.ShapeDtypeStruct(shape, dtype)


def params(mib):
    return pltpu.CompilerParams(vmem_limit_bytes=mib * MIB)


def cost(flops, moved):
    return pl.CostEstimate(flops=flops, bytes_accessed=moved, transcendentals=0)


def slot_of(coords, bits):
    return (coords[0] * 2 + coords[3]) ^ bits


def pack_kernel(coords, up_ref, down_ref, qkv_ref, out_ref, segment_ref, *refs):
    parts, sems = refs[:4], refs[4]
    hidden, width = up_ref.shape[1] // 4, out_ref.shape[1] // 4
    copies = []

    def copy(source, target):
        copies.append(pltpu.make_async_copy(source, target, sems.at[len(copies)]))
        copies[-1].start()

    for bits in (1, 2, 3, 0):
        slot = slot_of(coords, bits)
        wide = pl.ds(pl.multiple_of(slot * hidden, hidden), hidden)
        narrow = pl.ds(pl.multiple_of(slot * width, width), width)
        part = parts[bits]
        for kind in range(3):
            copy(qkv_ref.at[kind, :, narrow], part.at[:, pl.ds(kind * width, width)])
        copy(out_ref.at[:, narrow], part.at[:, pl.ds(3 * width, width)])
        copy(up_ref.at[:, wide], part.at[:, pl.ds(4 * width, hidden)])
        copy(down_ref.at[:, wide], part.at[:, pl.ds(4 * width + hidden, hidden)])
    segments = segment_ref[...].astype(F32).astype(BF16)
    segments = jnp.broadcast_to(segments, (up_ref.shape[0], segments.shape[1]))
    for part in parts:
        part[:, 4 * width + 2 * hidden :] = segments
    for each in copies:
        each.wait()


def pack(coords, w_up, down_t, qkv_t, out_t, segments):
    rows, hidden, width = w_up.shape[0], w_up.shape[1] // 4, out_t.shape[1] // 4
    return pl.pallas_call(
        pack_kernel,
        in_specs=[SCALARS] + [ANY] * 4 + [WHOLE],
        out_specs=[WHOLE] * 4,
        out_shape=[like((rows, 2 * hidden + 4 * width + segments.shape[0]))] * 4,
        scratch_shapes=[pltpu.SemaphoreType.DMA((24,))],
        compiler_params=params(60),
        name="pack",
    )(coords, w_up, down_t, qkv_t, out_t, segments.reshape(1, -1))


def order_kernel(coords, *refs):
    parts, out = refs[:4], refs[4]
    for bits in range(4):
        out[coords[0] ^ (bits >> 1), coords[3] ^ (bits & 1)] = parts[bits][:, : out.shape[3]]


def order(coords, parts, columns):
    rows = parts[0].shape[0]
    out = pl.pallas_call(
        order_kernel,
        in_specs=[SCALARS] + [WHOLE] * 4,
        out_specs=WHOLE,
        out_shape=like((2, 2, rows, columns)),
        compiler_params=params(16),
        name="order",
    )(coords, *parts)
    return out.reshape(4 * rows, columns)


def join_kernel(*refs):
    parts, out, sem = refs[:-2], refs[-2], refs[-1]
    copies = []
    for i, part in enumerate(parts):
        copies.append(pltpu.make_async_copy(part, out.at[i], sem.at[i]))
        copies[-1].start()
    for copy in copies:
        copy.wait()


def join(*parts):
    return pl.pallas_call(
        join_kernel,
        in_specs=[ANY] * len(parts),
        out_specs=ANY,
        out_shape=like((len(parts),) + parts[0].shape),
        scratch_shapes=[pltpu.SemaphoreType.DMA((len(parts),))],
        compiler_params=params(16),
        name="join",
    )(*parts)


def tokens_kernel(mine_ref, other_ref, rows_ref, columns_ref):
    @pl.when(pl.program_id(1) == 0)
    def _():
        rows_ref[0] = mine_ref[0, 0]
        columns_ref[0] = mine_ref[0, 0].T

    @pl.when(pl.program_id(1) == 1)
    def _():
        rows_ref[0] = other_ref[0, 0]
        columns_ref[0] = other_ref[0, 0].T


def gather_tokens(*pairs):
    mine = join(*pairs)
    other = flip(mine, "c")
    _, _, rows, depth = mine.shape
    block = (1, 1, rows, depth)
    return pl.pallas_call(
        tokens_kernel,
        grid=(2, 2, 4),
        in_specs=[
            pl.BlockSpec(block, lambda w, c, z: (jnp.where(c == 0, z, 3), w, 0, 0)),
            pl.BlockSpec(block, lambda w, c, z: (jnp.where(c == 1, z, 0), w, 0, 0)),
        ],
        out_specs=[
            pl.BlockSpec((1, rows, depth), lambda w, c, z: (w, 4 * c + z, 0)),
            pl.BlockSpec((1, depth, rows), lambda w, c, z: (w, 0, 4 * c + z)),
        ],
        out_shape=[like((2, 8 * rows, depth)), like((2, depth, 8 * rows))],
        compiler_params=params(32),
        cost_estimate=cost(0, 8 * mine.size * 2),
        name="tokens",
    )(mine, other)


def across(columns):
    ones = jnp.ones((8, columns.shape[1]), F32)
    contract = (((1,), (1,)), ((), ()))
    return lax.dot_general(
        ones, columns, contract, precision=lax.Precision.HIGHEST, preferred_element_type=F32
    )[:1]


def lane_sums(value):
    total = value[:, :LANES]
    for start in range(LANES, value.shape[1], LANES):
        total = total + value[:, start : start + LANES]
    return total


def mlp_kernel(pair_hbm, pair_t_hbm, bias_ref, up_ref, down_ref, *refs):
    hidden_ref, grads_ref, bias_sums_ref, sums_ref, product_ref, level_ref, pair_ref, pair_t_ref, sems = refs
    step, tile = pl.program_id(0), up_ref.shape[1]
    slope = 0.7978845608028654
    loads = [
        pltpu.make_async_copy(source.at[i], target.at[i], sems.at[k, i])
        for k, (source, target) in enumerate(((pair_hbm, pair_ref), (pair_t_hbm, pair_t_ref)))
        for i in range(2)
    ]

    def begin():
        for load in loads:
            load.start()

    def wait(*which):
        def body():
            for i in which:
                loads[i].wait()

        pl.when(step == 0)(body)

    pl.when(step == 0)(begin)
    wait(0)
    up = jnp.dot(pair_ref[0], up_ref[...], preferred_element_type=F32) + bias_ref[...]
    square = up * up
    wave = jnp.tanh(up * (slope + (slope * 0.044715) * square))
    half = 0.5 + 0.5 * wave
    activated = (up * half).astype(BF16)
    hidden_ref[1] = activated
    rise = half + up * (1.0 - wave * wave) * (0.5 * slope + (1.5 * slope * 0.044715) * square)
    wait(1)
    grad = jnp.dot(pair_ref[1], down_ref[...], preferred_element_type=F32) * rise
    low = grad.astype(BF16)
    hidden_ref[0] = low
    wait(2, 3)
    bias_sums = jnp.sum(low.astype(F32), axis=0, keepdims=True)
    bias_sums_ref[...] = bias_sums
    grads_ref[:, tile:] = jnp.dot(pair_t_ref[1], activated, preferred_element_type=F32).astype(BF16)
    grads = jnp.dot(pair_t_ref[0], low, preferred_element_type=F32)
    grads_ref[:, :tile] = grads.astype(BF16)
    weights = up_ref[...].astype(F32)
    products, levels = lane_sums(weights * grads), lane_sums(weights * bias_sums)

    @pl.when(step == 0)
    def _():
        product_ref[...] = products
        level_ref[...] = levels

    @pl.when(step > 0)
    def _():
        product_ref[...] += products
        level_ref[...] += levels

    @pl.when(step == pl.num_programs(0) - 1)
    def _():
        sums_ref[0:1, :] = across(level_ref[...])
        sums_ref[1:2, :] = across(product_ref[...])


def mlp(pair, pair_t, bias, weights, tile):
    rows, depth = pair.shape[1:]
    hidden = bias.shape[0]
    tiles = hidden // tile
    start = (weights.shape[1] - 2 * hidden) // tile
    column = lambda j: (0, j)
    return pl.pallas_call(
        mlp_kernel,
        grid=(tiles,),
        in_specs=[
            ANY,
            ANY,
            pl.BlockSpec((1, tile), column),
            pl.BlockSpec((depth, tile), lambda j: (0, start + j)),
            pl.BlockSpec((depth, tile), lambda j: (0, start + tiles + j)),
        ],
        out_specs=[
            pl.BlockSpec((2, rows, tile), lambda j: (0, 0, j)),
            pl.BlockSpec((depth, 2 * tile), column),
            pl.BlockSpec((1, tile), column),
            pl.BlockSpec((2, depth), lambda j: (0, 0)),
        ],
        out_shape=[
            like((2, rows, hidden)),
            like((depth, 2 * hidden)),
            like((1, hidden), F32),
            like((2, depth), F32),
        ],
        scratch_shapes=[pltpu.VMEM((depth, LANES), F32)] * 2
        + [
            pltpu.VMEM((2, rows, depth), BF16),
            pltpu.VMEM((2, depth, rows), BF16),
            pltpu.SemaphoreType.DMA((2, 2)),
        ],
        compiler_params=params(48),
        cost_estimate=cost(8 * rows * depth * hidden, 40 * MIB),
        name="mlp",
    )(pair, pair_t, bias.reshape(1, -1), weights, weights)


def split(rows):
    high = rows.astype(BF16)
    return high, (rows - high.astype(F32)).astype(BF16)


def whole(rows):
    count = rows.shape[0] // 2
    return rows[:count].astype(F32) + rows[count:].astype(F32)


def head_grads_kernel(
    coords, left_ref, right_ref, weights_ref, gain_ref, bias_ref, mlp_sums_ref, up_sums_ref, cot_ref, *refs
):
    outs, (product_ref, turned_ref, rows_ref, product_sums, level_sums) = refs[:5], refs[5:]
    x, y = coords[1], coords[2]
    step, tile = pl.program_id(0), right_ref.shape[1]
    block = product_ref.shape[1]
    lanes = pl.ds(pl.multiple_of(step * tile, tile), tile)
    product = jnp.dot(left_ref[step // 3], right_ref[...], preferred_element_type=F32)
    product_ref[...] = product.astype(BF16).reshape(product_ref.shape)
    targets = []
    for y_bits in range(4):
        for x_bits in range(4):
            out, i = outs[(0, 1, None, 2)[y_bits] or 0], x_bits
            if y_bits == 2:
                out, i = outs[3 + x_bits // 2], x_bits % 2
            chip = (x ^ x_bits) * 4 + (y ^ y_bits)
            out[i, :block, lanes] = product_ref[chip]
            targets.append(out.at[i])

    @pl.when(step == 0)
    def _():
        product_sums[...] = jnp.zeros_like(product_sums)
        level_sums[...] = jnp.zeros_like(level_sums)
        rows_ref[...] = jnp.zeros_like(rows_ref)

    @pl.when(step < 3)
    def _():
        sums = jnp.sum(right_ref[...].astype(F32), axis=0, keepdims=True)
        rows_ref[7:8, lanes] = sums
        weights = weights_ref[...].astype(F32)
        product_sums[...] += lane_sums(weights * product)
        level_sums[...] += lane_sums(weights * sums)

    @pl.when(step == 3)
    def _():
        wide = rows_ref.shape[1]
        level = mlp_sums_ref[0:1, :] + across(level_sums[...])
        product = mlp_sums_ref[1:2, :] + across(product_sums[...])
        turn(turned_ref, jnp.concatenate([product, level], axis=0), True)
        level = turned_ref[1:2, :]
        by_gain = (turned_ref[0:1, :] - bias_ref[...] * level) / gain_ref[...]
        for i, row in enumerate((by_gain, level, cot_ref[...])):
            rows_ref[2 * i : 2 * i + 1, :] = row[:, :wide]
            rows_ref[2 * i + 1 : 2 * i + 2, :] = row[:, wide:]
        rows_ref[6:7, :] = up_sums_ref[...]
        high, low = split(rows_ref[...])
        both = jnp.concatenate([high.astype(F32), low.astype(F32)], axis=0).astype(BF16)
        for target in targets:
            target[block:, :] = both


def head_grads(coords, pair_t, right, weights, gain, bias, mlp_sums, up_sums, cot_sums):
    _, depth, rows = pair_t.shape
    columns = right.shape[1]
    tile, block = columns // 4, depth // 16
    full, half = like((4, block + 16, columns)), like((2, block + 16, columns))
    first = lambda j: (0, jnp.minimum(j, 2))
    return pl.pallas_call(
        head_grads_kernel,
        grid=(4,),
        in_specs=[
            SCALARS,
            WHOLE,
            pl.BlockSpec((rows, tile), lambda j: (0, j)),
            pl.BlockSpec((depth, tile), first),
        ]
        + [WHOLE] * 5,
        out_specs=[WHOLE] * 5,
        out_shape=[full, full, full, half, half],
        scratch_shapes=[
            pltpu.VMEM((16, block, tile), BF16),
            pltpu.VMEM((2, depth), F32),
            pltpu.VMEM((8, columns), F32),
            pltpu.VMEM((depth, LANES), F32),
            pltpu.VMEM((depth, LANES), F32),
        ],
        compiler_params=params(28),
        cost_estimate=cost(2 * depth * rows * columns, 16 * MIB),
        name="head_grads",
    )(coords, pair_t, right, weights, gain.reshape(1, -1), bias.reshape(1, -1), mlp_sums, up_sums, cot_sums)


def put(target, data, rows):
    block = data.shape[0]
    target[:block, :] = data.astype(BF16)
    high, low = split(rows)
    target[block:, :] = jnp.concatenate([high.astype(F32), low.astype(F32)], axis=0).astype(BF16)


def bump_kernel(chunk_ref, part_ref, out_ref):
    block = chunk_ref.shape[1] - 16
    for i in range(2):
        data = chunk_ref[i, :block].astype(F32) + part_ref[i, :block].astype(F32)
        put(out_ref.at[i], data, whole(chunk_ref[i, block:]) + whole(part_ref[i, block:]))


def bump(chunk, part, half):
    spec = pl.BlockSpec(part.shape, lambda i: (half, 0, 0))
    return pl.pallas_call(
        bump_kernel,
        grid=(1,),
        in_specs=[spec, pl.BlockSpec(part.shape, lambda i: (0, 0, 0))],
        out_specs=spec,
        out_shape=like(chunk.shape),
        input_output_aliases={0: 0},
        compiler_params=params(16),
        name="bump",
    )(chunk, part)


def near_kernel(own_ref, one_ref, three_ref, keep_ref, *sends):
    block = own_ref.shape[1] - 16
    for i in range(4):
        data = own_ref[i, :block].astype(F32)
        data = data + (one_ref[i, :block].astype(F32) + three_ref[i, :block].astype(F32))
        rows = whole(own_ref[i, block:]) + (whole(one_ref[i, block:]) + whole(three_ref[i, block:]))
        if i == 0:
            keep_ref[:block, :] = data
            keep_ref[block:, :] = rows
        else:
            put(sends[i - 1], data, rows)


def near_sums(own, one, three):
    rows, columns = own.shape[1:]
    return pl.pallas_call(
        near_kernel,
        in_specs=[WHOLE] * 3,
        out_specs=[WHOLE] * 4,
        out_shape=[like((rows - 8, columns), F32)] + [like((rows, columns))] * 3,
        compiler_params=params(16),
        name="near",
    )(own, one, three)


def cut_kernel(coords, mlp_ref, *refs):
    blocks, outs = refs[:4], refs[4:]
    rows, columns = outs[0].shape[0], mlp_ref.shape[1]
    block, wide = 4 * rows, blocks[0].shape[1]
    vectors = blocks[0][block:, :]
    for other in blocks[1:]:
        vectors = vectors + whole(other[block:, :])
    high, low = split(vectors)
    vectors = jnp.concatenate([high.astype(F32), low.astype(F32)], axis=0).astype(BF16)
    for bits in range(4):
        some = pl.ds(pl.multiple_of(slot_of(coords, bits) * rows, rows), rows)
        out = outs[bits]
        out[:, :columns] = mlp_ref[some, :]
        total = blocks[0][some, :]
        for other in blocks[1:]:
            total = total + other[some, :].astype(F32)
        out[:, columns : columns + wide] = total.astype(BF16)
        out[:16, columns + wide :] = vectors[:, : wide // 2]
        out[16:, columns + wide :] = vectors[:, wide // 2 :]


def cut(coords, mlp_grads, blocks):
    rows, columns = mlp_grads.shape[0] // 4, mlp_grads.shape[1]
    wide = blocks[0].shape[1]
    return pl.pallas_call(
        cut_kernel,
        in_specs=[SCALARS] + [WHOLE] * 5,
        out_specs=[WHOLE] * 4,
        out_shape=[like((rows, columns + wide + wide // 2))] * 4,
        compiler_params=params(16),
        name="cut",
    )(coords, mlp_grads, *blocks)


def combine_kernel(hidden_ref, right_ref, weights_ref, mine_ref, theirs_ref):
    contract = (((1,), (1,)), ((), ()))
    hidden, columns = hidden_ref.shape[2], right_ref.shape[1]
    inner = columns * 3 // 4
    half = mine_ref.shape[1]

    def product(left, start):
        weights = weights_ref[:, start : start + left.shape[1]]
        return lax.dot_general(left, weights, contract, preferred_element_type=F32)

    total = product(hidden_ref[0], columns) + product(right_ref[:, :inner], 0)
    mine_ref[0] = total[:half].astype(BF16)
    theirs_ref[0] = total[half:].astype(BF16)
    total = product(hidden_ref[1], columns + hidden) + product(right_ref[:, inner:], inner)
    mine_ref[1] = total[:half].astype(BF16)
    theirs_ref[1] = total[half:].astype(BF16)


def combine(hidden_pair, right, weights, part):
    _, rows, hidden = hidden_pair.shape
    depth, columns = weights.shape
    tile = depth // 4
    block = pl.BlockSpec((2, rows // 2, tile), lambda i: (0, 0, i))
    return pl.pallas_call(
        combine_kernel,
        grid=(2,),
        in_specs=[
            WHOLE,
            WHOLE,
            pl.BlockSpec((tile, columns), lambda i: (2 * part + i, 0)),
        ],
        out_specs=[block] * 2,
        out_shape=[like((2, rows // 2, depth // 2))] * 2,
        compiler_params=params(40),
        cost_estimate=cost(rows * depth * columns, 16 * MIB),
        name="combine",
    )(hidden_pair, right, weights)


def exchange(parts):
    return [parts[0], flip(parts[1], "c"), flip(parts[2], "zl"), flip(parts[3], "zl", "c")]


def unpack_kernel(coords, *refs):
    parts, (up_ref, down_ref, qkv_ref, out_ref, rows_ref, up_sums_ref, qkv_sums_ref) = refs[:4], refs[4:]
    hidden, width = up_ref.shape[1] // 4, out_ref.shape[1] // 4
    tile = hidden // 4
    for bits in range(4):
        slot = slot_of(coords, bits)
        wide = pl.ds(pl.multiple_of(slot * hidden, hidden), hidden)
        narrow = pl.ds(pl.multiple_of(slot * width, width), width)
        part = parts[bits]
        for j in range(4):
            some = pl.ds(pl.multiple_of(slot * hidden + j * tile, tile), tile)
            up_ref[:, some] = part[:, 2 * j * tile : (2 * j + 1) * tile].astype(F32)
            down_ref[:, some] = part[:, (2 * j + 1) * tile : (2 * j + 2) * tile].astype(F32)
        start = 2 * hidden
        for kind in range(3):
            qkv_ref[kind, :, narrow] = part[:, start + kind * width : start + (kind + 1) * width].astype(F32)
        out_ref[:, narrow] = part[:, start + 3 * width : start + 4 * width].astype(F32)
        start += 4 * width
        vectors = jnp.concatenate([whole(part[:16, start:]), whole(part[16:, start:])], axis=1)
        rows_ref[...] = vectors if bits == 0 else rows_ref[...] + vectors
        up_sums_ref[:, wide] = vectors[6:7, :]
        for kind in range(3):
            qkv_sums_ref[kind : kind + 1, narrow] = vectors[7:8, kind * width : (kind + 1) * width]


def unpack(coords, parts, hidden, width):
    rows = parts[0].shape[0]
    wide, narrow = (rows, 4 * hidden), (rows, 4 * width)
    shapes = [wide, wide, (3,) + narrow, narrow, (8, 4 * width), (1, 4 * hidden), (3, 4 * width)]
    return pl.pallas_call(
        unpack_kernel,
        in_specs=[SCALARS] + [WHOLE] * 4,
        out_specs=[WHOLE] * 7,
        out_shape=[like(shape, F32) for shape in shapes],
        compiler_params=params(16),
        name="unpack",
    )(coords, *parts)


def turn(dest, value, back):
    block = value.shape[1] // 32
    for chip in range(16):
        for zl in range(2):
            natural, inside = (zl * 16 + chip) * block, (chip * 2 + zl) * block
            source, target = (inside, natural) if back else (natural, inside)
            dest[:, target : target + block] = value[:, source : source + block].astype(dest.dtype)


def standardize(tokens):
    rows = tokens.astype(F32)
    centered = rows - jnp.mean(rows, axis=1, keepdims=True)
    scale = lax.rsqrt(jnp.mean(centered * centered, axis=1, keepdims=True) + EPSILON)
    return rows, centered * scale, scale


def enter_kernel(tokens_ref, cot_ref, gain_ref, bias_ref, pair_ref, sums_ref):
    _, standard, _ = standardize(tokens_ref[...])
    turn(pair_ref.at[0], (standard * gain_ref[...] + bias_ref[...]).astype(BF16), False)
    turn(pair_ref.at[1], cot_ref[...], False)
    sums_ref[...] = jnp.sum(cot_ref[...].astype(F32), axis=0, keepdims=True)


def enter(tokens, cotangent, gain, bias):
    return pl.pallas_call(
        enter_kernel,
        in_specs=[WHOLE] * 4,
        out_specs=[WHOLE] * 2,
        out_shape=[like((2,) + tokens.shape), like((1, tokens.shape[1]), F32)],
        compiler_params=params(16),
        name="enter",
    )(tokens, cotangent, gain.reshape(1, -1), bias.reshape(1, -1))


def leave_kernel(tokens_ref, cot_ref, gain_ref, bias_ref, *refs):
    mixed_ref, grad_ref, branch_ref, normed_ref = refs[-4:]
    for which, target in ((0, normed_ref), (1, branch_ref)):
        total = refs[0][which]
        for part in refs[1:4]:
            total = total + part[which].astype(F32)
        turn(target, total, True)
    rows, standard, scale = standardize(tokens_ref[...])
    mixed_ref[...] = (rows + branch_ref[...] + bias_ref[...]).astype(BF16)
    grad = normed_ref[...] * gain_ref[...]
    level = jnp.mean(grad, axis=1, keepdims=True)
    slope = jnp.mean(grad * standard, axis=1, keepdims=True)
    grad_ref[...] = cot_ref[...].astype(F32) + scale * (grad - level - standard * slope)


def leave(tokens, cotangent, gain, bias, sums):
    shape = tokens.shape
    return pl.pallas_call(
        leave_kernel,
        in_specs=[WHOLE] * 8,
        out_specs=[WHOLE] * 2,
        out_shape=[like(shape), like(shape, F32)],
        scratch_shapes=[pltpu.VMEM(shape, F32)] * 2,
        compiler_params=params(24),
        name="leave",
    )(tokens, cotangent, gain.reshape(1, -1), bias.reshape(1, -1), *sums)


def scatter_plane(grads):
    return lax.psum_scatter(grads, PLANE, scatter_dimension=0, tiled=True)


def per_device(
    tokens,
    layernorm_gain,
    layernorm_bias,
    w_qkv,
    b_qkv,
    w_out,
    b_out,
    w_up,
    b_up,
    w_down,
    b_down,
    segments,
    cotangent,
):
    depth = tokens.shape[1]
    length = segments.shape[0]
    half_rows = tokens.shape[0]
    width = w_out.shape[0] // 4
    hidden = w_down.shape[0] // 4
    rows = w_up.shape[0]
    coords = jnp.stack([lax.axis_index(axis) for axis in AXES]).astype(jnp.int32)
    place_here = coords[0] * 2 + coords[3]
    this_half = coords[4]

    parts = exchange(pack(coords, w_up, w_down.T, w_qkv.transpose(1, 0, 2), w_out.T, segments))
    shard = order(coords, parts, 2 * hidden + 4 * width)
    weights = lax.all_gather(shard, PLANE, axis=0, tiled=True)

    pair, cot_sums = enter(tokens, cotangent, layernorm_gain, layernorm_bias)
    _, pair = lax.optimization_barrier((shard, pair))
    near, far, opposite = flip(pair, "zl"), flip(pair, "zl", "mp"), flip(pair, "mp")
    pair, pair_t = gather_tokens(pair, opposite, near, far)

    doc = jnp.stack([parts[k][0, -length:] for k in (0, 2, 1, 3)]).astype(jnp.int32)
    doc = doc.reshape(4, 2, half_rows)
    doc = jnp.where(this_half == 0, doc, doc[:, ::-1]).reshape(4, length)
    halves = jnp.stack([this_half, 1 - this_half]) * half_rows
    index = (halves[:, None] + jnp.arange(half_rows, dtype=jnp.int32)).reshape(1, length)
    index = jnp.broadcast_to(index, (4, length)).astype(jnp.int32)
    b_up_here = lax.dynamic_slice_in_dim(b_up, place_here * hidden, hidden)
    b_qkv_here = lax.dynamic_slice_in_dim(b_qkv, place_here * width, width, axis=1).reshape(-1)

    tables = rotary_tables(doc, index)

    pair, pair_t, tables = lax.optimization_barrier((pair, pair_t, tables))
    hidden_pair, mlp_grads, up_sums, mlp_sums = mlp(pair, pair_t, b_up_here, weights, hidden // 4)
    mlp_grads = scatter_plane(mlp_grads)

    pair, pair_t, hidden_pair = lax.optimization_barrier((pair, pair_t, hidden_pair))
    right = heads(pair, weights, b_qkv_here, tables, length)

    chunks = head_grads(
        coords, pair_t, right, weights, layernorm_gain, layernorm_bias, mlp_sums, up_sums, cot_sums
    )
    chunks, hidden_pair = lax.optimization_barrier((chunks, hidden_pair))
    own, one, three, two_low, two_high = chunks
    low, high = hop(two_low, "y", 1), hop(two_high, "y", 3)
    first, first_theirs = combine(hidden_pair, right, weights, 0)
    first_theirs = flip(first_theirs, "c")
    first, hidden_pair = lax.optimization_barrier((first, hidden_pair))
    second, second_theirs = combine(hidden_pair, right, weights, 1)

    low, high, first_theirs, second, second_theirs = lax.optimization_barrier(
        (low, high, first_theirs, second, second_theirs)
    )
    second_theirs = flip(second_theirs, "c")
    one, three = hop(bump(one, high, 1), "y", 1), hop(bump(three, low, 0), "y", 3)
    keep, sends = fold(first, first_theirs, second, second_theirs)
    near, far = flip(sends[1], "zl"), flip(sends[2], "zl", "mp")
    one, three, near, far, keep, opposite = lax.optimization_barrier(
        (one, three, near, far, keep, sends[0])
    )
    along_z = [near, far, flip(opposite, "mp")]
    blocks = near_sums(own, one, three)
    blocks = [blocks[0]] + [hop(part, "x", bits) for part, bits in zip(blocks[1:], (1, 2, 3))]
    parts = exchange(cut(coords, mlp_grads, blocks))
    mixed, d_tokens = leave(
        tokens, cotangent, layernorm_gain, b_out + b_down, [keep] + along_z
    )
    grad_up_w, grad_down_w, grad_qkv_w, grad_out_w, vectors, grad_b_up, grad_b_qkv = unpack(
        coords, parts, hidden, width
    )
    vectors = (vectors + flip(vectors, "mp"))[:6].reshape(3, depth)
    return (
        mixed,
        d_tokens,
        vectors[0],
        vectors[1],
        grad_qkv_w.transpose(1, 0, 2),
        grad_b_qkv,
        grad_out_w.T,
        vectors[2],
        grad_up_w,
        grad_b_up[0],
        grad_down_w.T,
        vectors[2],
    )


def solution(mesh):
    fine = Mesh(mesh.devices.reshape(SIZES), AXES)
    dp = ("zl", "x", "y", "c")
    in_specs = (
        P(AXES, None),
        P(),
        P(),
        P(dp, None, "mp"),
        P(None, "mp"),
        P("mp", dp),
        P(),
        P(dp, "mp"),
        P("mp"),
        P("mp", dp),
        P(),
        P(dp),
        P(AXES, None),
    )
    out_specs = (
        P(AXES, None),
        P(AXES, None),
        P(),
        P(),
        P(dp, None, "mp"),
        P(None, "mp"),
        P("mp", dp),
        P(),
        P(dp, "mp"),
        P("mp"),
        P("mp", dp),
        P(),
    )
    return jax.shard_map(
        per_device, mesh=fine, in_specs=in_specs, out_specs=out_specs, check_vma=False
    )
```

```python
import functools

import jax
import jax.numpy as jnp
from jax import lax
from jax.experimental import pallas as pl
from jax.experimental.pallas import tpu as pltpu
from jax.sharding import Mesh, PartitionSpec as P

HEAD_DIM = 64
ROT = 32
HALF = ROT // 2
LANES = 128
EPSILON = 1e-05

AXES = ("zl", "x", "y", "c", "mp")
SIZES = (2, 4, 4, 2, 2)
PLANE = ("x", "y")
PAIR = ("zl", "c")

BF16 = jnp.bfloat16
F32 = jnp.float32
MIB = 1024 * 1024
GIGA = 1000 * MIB
ANY = pl.BlockSpec(memory_space=pl.ANY)
WHOLE = pl.BlockSpec(memory_space=pltpu.VMEM)
SCALARS = pl.BlockSpec(memory_space=pltpu.SMEM)


def flip(value, *axes):
    count = 2 ** len(axes)
    return lax.ppermute(value, axes, [(i, count - 1 - i) for i in range(count)])


def hop(value, axis, bits):
    return lax.ppermute(value, axis, [(i, i ^ bits) for i in range(4)])


def fold_kernel(mine_ref, theirs_ref, keep_ref, *sends):
    rows = keep_ref.shape[1]
    for which in range(2):
        for i in range(4):
            block = slice(i * rows, (i + 1) * rows)
            total = mine_ref[which, block, :].astype(F32) + theirs_ref[which, block, :].astype(F32)
            if i == 0:
                keep_ref[which] = total
            else:
                sends[i - 1][which] = total.astype(BF16)


def fold(mine, theirs):
    _, rows, depth = mine.shape
    rows, tile = rows // 4, depth // 4
    keep, *sends = pl.pallas_call(
        fold_kernel,
        grid=(4,),
        in_specs=[pl.BlockSpec((2, 4 * rows, tile), lambda j: (0, 0, j))] * 2,
        out_specs=[pl.BlockSpec((2, rows, tile), lambda j: (0, 0, j))] * 4,
        out_shape=[like((2, rows, depth), F32)] + [like((2, rows, depth))] * 3,
        compiler_params=params(16),
        cost_estimate=cost(0, 26 * rows * depth),
        name="fold",
    )(mine, theirs)
    return keep, sends


def heads_kernel(
    pair_ref,
    weights_ref,
    bias_ref,
    trig_ref,
    segment_col,
    segment_row,
    index_col,
    index_row,
    right_ref,
    linear_ref,
    query_ref,
    key_ref,
    value_ref,
    grad_ref,
    grad_query_ref,
    grad_key_ref,
    attended_ref,
):
    width = grad_ref.shape[1]
    length = grad_ref.shape[0]
    scale = HEAD_DIM ** (-0.5)
    linear_ref[...] = (
        jnp.dot(pair_ref[0], weights_ref[:, : 3 * width], preferred_element_type=F32)
        + bias_ref[...]
    )
    grad_ref[...] = jnp.dot(
        pair_ref[1], weights_ref[:, 3 * width :], preferred_element_type=F32
    ).astype(BF16)

    def rotated(tile, sign):
        ahead = pltpu.roll(tile, LANES - HALF, 1)
        behind = pltpu.roll(tile, HALF, 1)
        turned = ahead * trig_ref[:, LANES : 2 * LANES] + behind * trig_ref[:, 2 * LANES :]
        return tile * trig_ref[:, :LANES] + turned * sign

    for start in range(0, width, LANES):
        lanes = slice(start, start + LANES)
        query_ref[:, lanes] = (rotated(linear_ref[:, lanes], 1.0) * scale).astype(BF16)
        keys = linear_ref[:, width + start : width + start + LANES]
        key_ref[:, lanes] = rotated(keys, 1.0).astype(BF16)
        value_ref[:, lanes] = linear_ref[:, 2 * width + start : 2 * width + start + LANES].astype(BF16)
    allowed = (segment_row[0] == segment_col[...]) & (index_row[0] >= index_col[...])
    both = (((1,), (1,)), ((), ()))
    value_t, key_t = value_ref[...].T, key_ref[...].T
    for start in range(0, width, HEAD_DIM):
        lanes = slice(start, start + HEAD_DIM)
        query, key, value = query_ref[:, lanes], key_ref[:, lanes], value_ref[:, lanes]
        grad = grad_ref[:, lanes]
        scores = lax.dot_general(key, query, both, preferred_element_type=F32)
        scores = jnp.where(allowed, scores, -1000000000.0)
        expo = jnp.exp(scores - jnp.max(scores, axis=0, keepdims=True))
        probs = expo * (1.0 / jnp.sum(expo, axis=0, keepdims=True))
        low_probs = probs.astype(BF16)
        attended_ref[lanes, :] = jnp.dot(value_t[lanes], low_probs, preferred_element_type=F32)
        grad_probs = lax.dot_general(value, grad, both, preferred_element_type=F32)
        grad_values = jnp.dot(low_probs, grad, preferred_element_type=F32)
        weighted = probs * grad_probs
        delta = jnp.sum(weighted, axis=0, keepdims=True)
        grad_scores = (weighted - probs * delta).astype(BF16)
        grad_query_ref[lanes, :] = jnp.dot(key_t[lanes], grad_scores, preferred_element_type=F32) * scale
        grad_key_ref[:, lanes] = jnp.dot(grad_scores, query, preferred_element_type=F32)
        right_ref[:, 2 * width + start : 2 * width + start + HEAD_DIM] = grad_values.astype(BF16)
    right_ref[:, 3 * width :] = attended_ref[...].T.astype(BF16)
    linear_ref[:, :width] = grad_query_ref[...].T
    for start in range(0, width, LANES):
        lanes = slice(start, start + LANES)
        right_ref[:, lanes] = rotated(linear_ref[:, lanes], -1.0).astype(BF16)
        right_ref[:, width + start : width + start + LANES] = rotated(
            grad_key_ref[:, lanes], -1.0
        ).astype(BF16)


def heads(pair, weights, bias, tables, length):
    _, rows, depth = pair.shape
    width = bias.shape[0] // 3
    blocks = lambda lanes: pl.BlockSpec((length, lanes), lambda i: (i, 0))
    rowwise = pl.BlockSpec((1, 1, length), lambda i: (i, 0, 0))
    return pl.pallas_call(
        heads_kernel,
        grid=(rows // length,),
        in_specs=[
            pl.BlockSpec((2, length, depth), lambda i: (0, i, 0)),
            pl.BlockSpec((depth, 4 * width), lambda i: (0, 0), pipeline_mode=pl.Buffered(1)),
            pl.BlockSpec((1, 3 * width), lambda i: (0, 0)),
            blocks(3 * LANES),
            blocks(1),
            rowwise,
            blocks(1),
            rowwise,
        ],
        out_specs=blocks(4 * width),
        out_shape=like((rows, 4 * width)),
        scratch_shapes=[pltpu.VMEM((length, 3 * width), F32)]
        + [pltpu.VMEM((length, width), BF16)] * 4
        + [
            pltpu.VMEM((width, length), F32),
            pltpu.VMEM((length, width), F32),
            pltpu.VMEM((width, length), F32),
        ],
        compiler_params=params(32),
        cost_estimate=cost(26 * GIGA, 10 * MIB),
        name="heads",
    )(pair, weights, bias.reshape(1, -1), *tables)


def tables_kernel(cos_ref, sin_ref, *refs):
    inputs, outputs = refs[:4], refs[5:]
    trig_ref = refs[4]
    cos, sin = cos_ref[...], sin_ref[...]
    trig_ref[...] = jnp.zeros_like(trig_ref)
    for start in range(0, LANES, HEAD_DIM):
        rest = (cos.shape[0], HEAD_DIM - ROT)
        trig_ref[:, start : start + HALF] = cos
        trig_ref[:, start + HALF : start + ROT] = cos
        trig_ref[:, start + ROT : start + HEAD_DIM] = jnp.ones(rest, F32)
        trig_ref[:, LANES + start : LANES + start + HALF] = -sin
        trig_ref[:, 2 * LANES + start + HALF : 2 * LANES + start + ROT] = sin
    for source, target in zip(inputs, outputs):
        target[...] = source[...]


def rotary_tables(doc, index):
    count, length = doc.shape
    rows = count * length
    same_doc = doc[:, :, None] == doc[:, None, :]
    doc_start = jnp.min(jnp.where(same_doc, index[:, None, :], length), axis=2)
    positions = (index - doc_start).astype(F32).reshape(-1)
    inv_freq = 10000.0 ** (-(jnp.arange(HALF, dtype=F32) * 2.0 / ROT))
    angles = positions[:, None] * inv_freq
    column, row = (rows, 1), (count, 1, length)
    shapes = [column, row, column, row]
    passed = [value.reshape(shape) for value, shape in zip((doc, doc, index, index), shapes)]
    return pl.pallas_call(
        tables_kernel,
        in_specs=[WHOLE] * 6,
        out_specs=[WHOLE] * 5,
        out_shape=[like((rows, 3 * LANES), F32)] + [like(shape, jnp.int32) for shape in shapes],
        compiler_params=params(16),
        name="tables",
    )(jnp.cos(angles), jnp.sin(angles), *passed)


def like(shape, dtype=BF16):
    return jax.ShapeDtypeStruct(shape, dtype)


def params(mib):
    return pltpu.CompilerParams(vmem_limit_bytes=mib * MIB)


def cost(flops, moved):
    return pl.CostEstimate(flops=flops, bytes_accessed=moved, transcendentals=0)


def slot_of(coords, bits):
    return (coords[0] * 2 + coords[3]) ^ bits


def pack_kernel(coords, up_ref, down_ref, qkv_ref, out_ref, segment_ref, *refs):
    parts, sems = refs[:4], refs[4]
    hidden, width = up_ref.shape[1] // 4, out_ref.shape[1] // 4
    copies = []

    def copy(source, target):
        copies.append(pltpu.make_async_copy(source, target, sems.at[len(copies)]))
        copies[-1].start()

    for bits in (1, 2, 3, 0):
        slot = slot_of(coords, bits)
        wide = pl.ds(pl.multiple_of(slot * hidden, hidden), hidden)
        narrow = pl.ds(pl.multiple_of(slot * width, width), width)
        part = parts[bits]
        for kind in range(3):
            copy(qkv_ref.at[kind, :, narrow], part.at[:, pl.ds(kind * width, width)])
        copy(out_ref.at[:, narrow], part.at[:, pl.ds(3 * width, width)])
        copy(up_ref.at[:, wide], part.at[:, pl.ds(4 * width, hidden)])
        copy(down_ref.at[:, wide], part.at[:, pl.ds(4 * width + hidden, hidden)])
    segments = segment_ref[...].astype(F32).astype(BF16)
    segments = jnp.broadcast_to(segments, (up_ref.shape[0], segments.shape[1]))
    for part in parts:
        part[:, 4 * width + 2 * hidden :] = segments
    for each in copies:
        each.wait()


def pack(coords, w_up, down_t, qkv_t, out_t, segments):
    rows, hidden, width = w_up.shape[0], w_up.shape[1] // 4, out_t.shape[1] // 4
    return pl.pallas_call(
        pack_kernel,
        in_specs=[SCALARS] + [ANY] * 4 + [WHOLE],
        out_specs=[WHOLE] * 4,
        out_shape=[like((rows, 2 * hidden + 4 * width + segments.shape[0]))] * 4,
        scratch_shapes=[pltpu.SemaphoreType.DMA((24,))],
        compiler_params=params(60),
        name="pack",
    )(coords, w_up, down_t, qkv_t, out_t, segments.reshape(1, -1))


def order_kernel(coords, *refs):
    parts, out = refs[:4], refs[4]
    for bits in range(4):
        out[coords[0] ^ (bits >> 1), coords[3] ^ (bits & 1)] = parts[bits][:, : out.shape[3]]


def order(coords, parts, columns):
    rows = parts[0].shape[0]
    out = pl.pallas_call(
        order_kernel,
        in_specs=[SCALARS] + [WHOLE] * 4,
        out_specs=WHOLE,
        out_shape=like((2, 2, rows, columns)),
        compiler_params=params(16),
        name="order",
    )(coords, *parts)
    return out.reshape(4 * rows, columns)


def join_kernel(*refs):
    parts, out, sem = refs[:-2], refs[-2], refs[-1]
    copies = []
    for i, part in enumerate(parts):
        copies.append(pltpu.make_async_copy(part, out.at[i], sem.at[i]))
        copies[-1].start()
    for copy in copies:
        copy.wait()


def join(*parts):
    return pl.pallas_call(
        join_kernel,
        in_specs=[ANY] * len(parts),
        out_specs=ANY,
        out_shape=like((len(parts),) + parts[0].shape),
        scratch_shapes=[pltpu.SemaphoreType.DMA((len(parts),))],
        compiler_params=params(16),
        name="join",
    )(*parts)


def tokens_kernel(mine_ref, other_ref, rows_ref, columns_ref):
    @pl.when(pl.program_id(1) == 0)
    def _():
        rows_ref[0] = mine_ref[0, 0]
        columns_ref[0] = mine_ref[0, 0].T

    @pl.when(pl.program_id(1) == 1)
    def _():
        rows_ref[0] = other_ref[0, 0]
        columns_ref[0] = other_ref[0, 0].T


def gather_tokens(*pairs):
    mine = join(*pairs)
    other = flip(mine, "c")
    _, _, rows, depth = mine.shape
    block = (1, 1, rows, depth)
    return pl.pallas_call(
        tokens_kernel,
        grid=(2, 2, 4),
        in_specs=[
            pl.BlockSpec(block, lambda w, c, z: (jnp.where(c == 0, z, 3), w, 0, 0)),
            pl.BlockSpec(block, lambda w, c, z: (jnp.where(c == 1, z, 0), w, 0, 0)),
        ],
        out_specs=[
            pl.BlockSpec((1, rows, depth), lambda w, c, z: (w, 4 * c + z, 0)),
            pl.BlockSpec((1, depth, rows), lambda w, c, z: (w, 0, 4 * c + z)),
        ],
        out_shape=[like((2, 8 * rows, depth)), like((2, depth, 8 * rows))],
        compiler_params=params(12),
        cost_estimate=cost(0, 8 * mine.size * 2),
        name="tokens",
    )(mine, other)


def across(columns):
    ones = jnp.ones((8, columns.shape[1]), F32)
    contract = (((1,), (1,)), ((), ()))
    return lax.dot_general(
        ones, columns, contract, precision=lax.Precision.HIGHEST, preferred_element_type=F32
    )[:1]


def lane_sums(value):
    total = value[:, :LANES]
    for start in range(LANES, value.shape[1], LANES):
        total = total + value[:, start : start + LANES]
    return total


def hidden_kernel(pair_ref, bias_ref, up_ref, down_ref, hidden_ref, sums_ref):
    slope = 0.7978845608028654
    up = jnp.dot(pair_ref[0], up_ref[...], preferred_element_type=F32) + bias_ref[...]
    square = up * up
    wave = jnp.tanh(up * (slope + (slope * 0.044715) * square))
    half = 0.5 + 0.5 * wave
    hidden_ref[1] = (up * half).astype(BF16)
    rise = half + up * (1.0 - wave * wave) * (0.5 * slope + (1.5 * slope * 0.044715) * square)
    grad = jnp.dot(pair_ref[1], down_ref[...], preferred_element_type=F32) * rise
    low = grad.astype(BF16)
    hidden_ref[0] = low
    sums_ref[...] = jnp.sum(low.astype(F32), axis=0, keepdims=True)


def hidden_units(pair, bias, weights):
    rows, depth = pair.shape[1:]
    hidden = bias.shape[0]
    tile = hidden // 4
    start = (weights.shape[1] - 2 * hidden) // tile
    column = lambda j: (0, j)
    return pl.pallas_call(
        hidden_kernel,
        grid=(4,),
        in_specs=[
            WHOLE,
            pl.BlockSpec((1, tile), column),
            pl.BlockSpec((depth, tile), lambda j: (0, start + j)),
            pl.BlockSpec((depth, tile), lambda j: (0, start + 4 + j)),
        ],
        out_specs=[pl.BlockSpec((2, rows, tile), lambda j: (0, 0, j)), pl.BlockSpec((1, tile), column)],
        out_shape=[like((2, rows, hidden)), like((1, hidden), F32)],
        compiler_params=params(40),
        cost_estimate=cost(4 * rows * depth * hidden, 20 * MIB),
        name="hidden",
    )(pair, bias.reshape(1, -1), weights, weights)


def mlp_grads_kernel(pair_t_ref, hidden_ref, bias_sums_ref, weights_ref, grads_ref, sums_ref, product_ref, level_ref):
    step, tile = pl.program_id(0), weights_ref.shape[1]
    grads = jnp.dot(pair_t_ref[0], hidden_ref[0], preferred_element_type=F32)
    grads_ref[:, :tile] = grads.astype(BF16)
    weights = weights_ref[...].astype(F32)
    products, levels = lane_sums(weights * grads), lane_sums(weights * bias_sums_ref[...])
    product_ref[...] = jnp.where(step == 0, products, product_ref[...] + products)
    level_ref[...] = jnp.where(step == 0, levels, level_ref[...] + levels)
    grads_ref[:, tile:] = jnp.dot(pair_t_ref[1], hidden_ref[1], preferred_element_type=F32).astype(BF16)

    @pl.when(step == pl.num_programs(0) - 1)
    def _():
        sums_ref[0:1, :] = across(level_ref[...])
        sums_ref[1:2, :] = across(product_ref[...])


def mlp_weight_grads(pair_t, hidden_pair, bias_sums, weights):
    _, depth, rows = pair_t.shape
    hidden = hidden_pair.shape[2]
    tile = hidden // 4
    start = (weights.shape[1] - 2 * hidden) // tile
    column = lambda j: (0, j)
    return pl.pallas_call(
        mlp_grads_kernel,
        grid=(4,),
        in_specs=[
            WHOLE,
            pl.BlockSpec((2, rows, tile), lambda j: (0, 0, j)),
            pl.BlockSpec((1, tile), column),
            pl.BlockSpec((depth, tile), lambda j: (0, start + j)),
        ],
        out_specs=[pl.BlockSpec((depth, 2 * tile), column), pl.BlockSpec((2, depth), lambda j: (0, 0))],
        out_shape=[like((depth, 2 * hidden)), like((2, depth), F32)],
        scratch_shapes=[pltpu.VMEM((depth, LANES), F32)] * 2,
        compiler_params=params(40),
        cost_estimate=cost(4 * rows * depth * hidden, 20 * MIB),
        name="mlp_grads",
    )(pair_t, hidden_pair, bias_sums, weights)


def split(rows):
    high = rows.astype(BF16)
    return high, (rows - high.astype(F32)).astype(BF16)


def whole(rows):
    count = rows.shape[0] // 2
    return rows[:count].astype(F32) + rows[count:].astype(F32)


def head_grads_kernel(
    coords, left_ref, right_ref, weights_ref, gain_ref, bias_ref, mlp_sums_ref, up_sums_ref, cot_ref, *refs
):
    outs, (product_ref, turned_ref, rows_ref, product_sums, level_sums) = refs[:5], refs[5:]
    x, y = coords[1], coords[2]
    step, tile = pl.program_id(0), right_ref.shape[1]
    block = product_ref.shape[1]
    lanes = pl.ds(pl.multiple_of(step * tile, tile), tile)
    product = jnp.dot(left_ref[step // 3], right_ref[...], preferred_element_type=F32)
    product_ref[...] = product.astype(BF16).reshape(product_ref.shape)
    targets = []
    for y_bits in range(4):
        for x_bits in range(4):
            out, i = outs[(0, 1, None, 2)[y_bits] or 0], x_bits
            if y_bits == 2:
                out, i = outs[3 + x_bits // 2], x_bits % 2
            chip = (x ^ x_bits) * 4 + (y ^ y_bits)
            out[i, :block, lanes] = product_ref[chip]
            targets.append(out.at[i])

    sums = jnp.sum(right_ref[...].astype(F32), axis=0, keepdims=True)
    weights = weights_ref[...].astype(F32)
    fresh, inner = step == 0, jnp.where(step < 3, 1.0, 0.0)
    products, levels = lane_sums(weights * product) * inner, lane_sums(weights * sums) * inner
    product_sums[...] = jnp.where(fresh, products, product_sums[...] + products)
    level_sums[...] = jnp.where(fresh, levels, level_sums[...] + levels)
    rows_ref[7:8, lanes] = sums * inner

    @pl.when(step == 3)
    def _():
        wide = rows_ref.shape[1]
        level = mlp_sums_ref[0:1, :] + across(level_sums[...])
        product = mlp_sums_ref[1:2, :] + across(product_sums[...])
        turn(turned_ref, jnp.concatenate([product, level], axis=0), True)
        level = turned_ref[1:2, :]
        by_gain = (turned_ref[0:1, :] - bias_ref[...] * level) / gain_ref[...]
        for i, row in enumerate((by_gain, level, cot_ref[...])):
            rows_ref[2 * i : 2 * i + 1, :] = row[:, :wide]
            rows_ref[2 * i + 1 : 2 * i + 2, :] = row[:, wide:]
        rows_ref[6:7, :] = up_sums_ref[...]
        high, low = split(rows_ref[...])
        both = jnp.concatenate([high.astype(F32), low.astype(F32)], axis=0).astype(BF16)
        for target in targets:
            target[block:, :] = both


def head_grads(coords, pair_t, right, weights, gain, bias, mlp_sums, up_sums, cot_sums):
    _, depth, rows = pair_t.shape
    columns = right.shape[1]
    tile, block = columns // 4, depth // 16
    full, half = like((4, block + 16, columns)), like((2, block + 16, columns))
    first = lambda j: (0, jnp.minimum(j, 2))
    return pl.pallas_call(
        head_grads_kernel,
        grid=(4,),
        in_specs=[
            SCALARS,
            WHOLE,
            pl.BlockSpec((rows, tile), lambda j: (0, j)),
            pl.BlockSpec((depth, tile), first),
        ]
        + [WHOLE] * 5,
        out_specs=[WHOLE] * 5,
        out_shape=[full, full, full, half, half],
        scratch_shapes=[
            pltpu.VMEM((16, block, tile), BF16),
            pltpu.VMEM((2, depth), F32),
            pltpu.VMEM((8, columns), F32),
            pltpu.VMEM((depth, LANES), F32),
            pltpu.VMEM((depth, LANES), F32),
        ],
        compiler_params=params(28),
        cost_estimate=cost(2 * depth * rows * columns, 16 * MIB),
        name="head_grads",
    )(coords, pair_t, right, weights, gain.reshape(1, -1), bias.reshape(1, -1), mlp_sums, up_sums, cot_sums)


def put(target, data, rows):
    block = data.shape[0]
    target[:block, :] = data.astype(BF16)
    high, low = split(rows)
    target[block:, :] = jnp.concatenate([high.astype(F32), low.astype(F32)], axis=0).astype(BF16)


def bump_kernel(chunk_ref, part_ref, out_ref):
    block = chunk_ref.shape[1] - 16
    for i in range(2):
        data = chunk_ref[i, :block].astype(F32) + part_ref[i, :block].astype(F32)
        put(out_ref.at[i], data, whole(chunk_ref[i, block:]) + whole(part_ref[i, block:]))


def bump(chunk, part, half):
    spec = pl.BlockSpec(part.shape, lambda i: (half, 0, 0))
    return pl.pallas_call(
        bump_kernel,
        grid=(1,),
        in_specs=[spec, pl.BlockSpec(part.shape, lambda i: (0, 0, 0))],
        out_specs=spec,
        out_shape=like(chunk.shape),
        input_output_aliases={0: 0},
        compiler_params=params(16),
        name="bump",
    )(chunk, part)


def near_kernel(own_ref, one_ref, three_ref, keep_ref, *sends):
    block = own_ref.shape[1] - 16
    for i in range(4):
        data = own_ref[i, :block].astype(F32)
        data = data + (one_ref[i, :block].astype(F32) + three_ref[i, :block].astype(F32))
        rows = whole(own_ref[i, block:]) + (whole(one_ref[i, block:]) + whole(three_ref[i, block:]))
        if i == 0:
            keep_ref[:block, :] = data
            keep_ref[block:, :] = rows
        else:
            put(sends[i - 1], data, rows)


def near_sums(own, one, three):
    rows, columns = own.shape[1:]
    return pl.pallas_call(
        near_kernel,
        in_specs=[WHOLE] * 3,
        out_specs=[WHOLE] * 4,
        out_shape=[like((rows - 8, columns), F32)] + [like((rows, columns))] * 3,
        compiler_params=params(16),
        name="near",
    )(own, one, three)


def cut_kernel(coords, *refs):
    sources, outs, targets, sems = refs[:5], refs[5:9], refs[9:14], refs[14]
    copies = []
    for i, (source, target) in enumerate(zip(sources, targets)):
        copies.append(pltpu.make_async_copy(source, target, sems.at[i]))
        copies[-1].start()
    for copy in copies:
        copy.wait()
    mlp_ref, blocks = targets[0], targets[1:]
    rows, columns = outs[0].shape[0], mlp_ref.shape[1]
    block, wide = 4 * rows, blocks[0].shape[1]
    vectors = blocks[0][block:, :]
    for other in blocks[1:]:
        vectors = vectors + whole(other[block:, :])
    high, low = split(vectors)
    vectors = jnp.concatenate([high.astype(F32), low.astype(F32)], axis=0).astype(BF16)
    for bits in range(4):
        some = pl.ds(pl.multiple_of(slot_of(coords, bits) * rows, rows), rows)
        out = outs[bits]
        out[:, :columns] = mlp_ref[some, :]
        total = blocks[0][some, :]
        for other in blocks[1:]:
            total = total + other[some, :].astype(F32)
        out[:, columns : columns + wide] = total.astype(BF16)
        out[:16, columns + wide :] = vectors[:, : wide // 2]
        out[16:, columns + wide :] = vectors[:, wide // 2 :]


def cut(coords, mlp_grads, blocks):
    rows, columns = mlp_grads.shape[0] // 4, mlp_grads.shape[1]
    wide = blocks[0].shape[1]
    arrays = [mlp_grads, *blocks]
    return pl.pallas_call(
        cut_kernel,
        in_specs=[SCALARS] + [ANY] * 5,
        out_specs=[WHOLE] * 4,
        out_shape=[like((rows, columns + wide + wide // 2))] * 4,
        scratch_shapes=[pltpu.VMEM(array.shape, array.dtype) for array in arrays]
        + [pltpu.SemaphoreType.DMA((5,))],
        compiler_params=params(16),
        name="cut",
    )(coords, *arrays)


def combine_kernel(hidden_ref, right_ref, weights_ref, mine_ref, theirs_ref):
    contract = (((1,), (1,)), ((), ()))
    hidden, columns = hidden_ref.shape[2], right_ref.shape[1]
    inner = columns * 3 // 4
    half = mine_ref.shape[1]

    def product(left, start):
        weights = weights_ref[:, start : start + left.shape[1]]
        return lax.dot_general(left, weights, contract, preferred_element_type=F32)

    total = product(hidden_ref[0], columns) + product(right_ref[:, :inner], 0)
    mine_ref[0] = total[:half].astype(BF16)
    theirs_ref[0] = total[half:].astype(BF16)
    total = product(hidden_ref[1], columns + hidden) + product(right_ref[:, inner:], inner)
    mine_ref[1] = total[:half].astype(BF16)
    theirs_ref[1] = total[half:].astype(BF16)


def combine(hidden_pair, right, weights):
    _, rows, hidden = hidden_pair.shape
    depth, columns = weights.shape
    tile = depth // 4
    block = pl.BlockSpec((2, rows // 2, tile), lambda i: (0, 0, i))
    return pl.pallas_call(
        combine_kernel,
        grid=(4,),
        in_specs=[WHOLE, WHOLE, pl.BlockSpec((tile, columns), lambda i: (i, 0))],
        out_specs=[block] * 2,
        out_shape=[like((2, rows // 2, depth))] * 2,
        compiler_params=params(40),
        cost_estimate=cost(2 * rows * depth * columns, 16 * MIB),
        name="combine",
    )(hidden_pair, right, weights)


def exchange(parts):
    return [parts[0], flip(parts[1], "c"), flip(parts[2], "zl"), flip(parts[3], "zl", "c")]


def unpack_kernel(coords, *refs):
    parts, (up_ref, down_ref, qkv_ref, out_ref, rows_ref, up_sums_ref, qkv_sums_ref) = refs[:4], refs[4:]
    hidden, width = up_ref.shape[1] // 4, out_ref.shape[1] // 4
    tile = hidden // 4
    for bits in range(4):
        slot = slot_of(coords, bits)
        wide = pl.ds(pl.multiple_of(slot * hidden, hidden), hidden)
        narrow = pl.ds(pl.multiple_of(slot * width, width), width)
        part = parts[bits]
        for j in range(4):
            some = pl.ds(pl.multiple_of(slot * hidden + j * tile, tile), tile)
            up_ref[:, some] = part[:, 2 * j * tile : (2 * j + 1) * tile].astype(F32)
            down_ref[:, some] = part[:, (2 * j + 1) * tile : (2 * j + 2) * tile].astype(F32)
        start = 2 * hidden
        for kind in range(3):
            qkv_ref[kind, :, narrow] = part[:, start + kind * width : start + (kind + 1) * width].astype(F32)
        out_ref[:, narrow] = part[:, start + 3 * width : start + 4 * width].astype(F32)
        start += 4 * width
        vectors = jnp.concatenate([whole(part[:16, start:]), whole(part[16:, start:])], axis=1)
        rows_ref[...] = vectors if bits == 0 else rows_ref[...] + vectors
        up_sums_ref[:, wide] = vectors[6:7, :]
        for kind in range(3):
            qkv_sums_ref[kind : kind + 1, narrow] = vectors[7:8, kind * width : (kind + 1) * width]


def unpack(coords, parts, hidden, width):
    rows = parts[0].shape[0]
    wide, narrow = (rows, 4 * hidden), (rows, 4 * width)
    shapes = [wide, wide, (3,) + narrow, narrow, (8, 4 * width), (1, 4 * hidden), (3, 4 * width)]
    return pl.pallas_call(
        unpack_kernel,
        in_specs=[SCALARS] + [WHOLE] * 4,
        out_specs=[WHOLE] * 7,
        out_shape=[like(shape, F32) for shape in shapes],
        compiler_params=params(16),
        name="unpack",
    )(coords, *parts)


def turn(dest, value, back):
    block = value.shape[1] // 32
    for chip in range(16):
        for zl in range(2):
            natural, inside = (zl * 16 + chip) * block, (chip * 2 + zl) * block
            source, target = (inside, natural) if back else (natural, inside)
            dest[:, target : target + block] = value[:, source : source + block].astype(dest.dtype)


def standardize(tokens):
    rows = tokens.astype(F32)
    centered = rows - jnp.mean(rows, axis=1, keepdims=True)
    scale = lax.rsqrt(jnp.mean(centered * centered, axis=1, keepdims=True) + EPSILON)
    return rows, centered * scale, scale


def enter_kernel(tokens_ref, cot_ref, gain_ref, bias_ref, pair_ref, sums_ref):
    _, standard, _ = standardize(tokens_ref[...])
    turn(pair_ref.at[0], (standard * gain_ref[...] + bias_ref[...]).astype(BF16), False)
    turn(pair_ref.at[1], cot_ref[...], False)
    sums_ref[...] = jnp.sum(cot_ref[...].astype(F32), axis=0, keepdims=True)


def enter(tokens, cotangent, gain, bias):
    return pl.pallas_call(
        enter_kernel,
        in_specs=[WHOLE] * 4,
        out_specs=[WHOLE] * 2,
        out_shape=[like((2,) + tokens.shape), like((1, tokens.shape[1]), F32)],
        compiler_params=params(16),
        name="enter",
    )(tokens, cotangent, gain.reshape(1, -1), bias.reshape(1, -1))


def leave_kernel(tokens_ref, cot_ref, gain_ref, bias_ref, *refs):
    mixed_ref, grad_ref, branch_ref, normed_ref = refs[-4:]
    for which, target in ((0, normed_ref), (1, branch_ref)):
        total = refs[0][which]
        for part in refs[1:4]:
            total = total + part[which].astype(F32)
        turn(target, total, True)
    rows, standard, scale = standardize(tokens_ref[...])
    mixed_ref[...] = (rows + branch_ref[...] + bias_ref[...]).astype(BF16)
    grad = normed_ref[...] * gain_ref[...]
    level = jnp.mean(grad, axis=1, keepdims=True)
    slope = jnp.mean(grad * standard, axis=1, keepdims=True)
    grad_ref[...] = cot_ref[...].astype(F32) + scale * (grad - level - standard * slope)


def leave(tokens, cotangent, gain, bias, sums):
    shape = tokens.shape
    return pl.pallas_call(
        leave_kernel,
        in_specs=[WHOLE] * 8,
        out_specs=[WHOLE] * 2,
        out_shape=[like(shape), like(shape, F32)],
        scratch_shapes=[pltpu.VMEM(shape, F32)] * 2,
        compiler_params=params(24),
        name="leave",
    )(tokens, cotangent, gain.reshape(1, -1), bias.reshape(1, -1), *sums)


def scatter_plane(grads):
    return lax.psum_scatter(grads, PLANE, scatter_dimension=0, tiled=True)


def per_device(
    tokens,
    layernorm_gain,
    layernorm_bias,
    w_qkv,
    b_qkv,
    w_out,
    b_out,
    w_up,
    b_up,
    w_down,
    b_down,
    segments,
    cotangent,
):
    depth = tokens.shape[1]
    length = segments.shape[0]
    half_rows = tokens.shape[0]
    width = w_out.shape[0] // 4
    hidden = w_down.shape[0] // 4
    rows = w_up.shape[0]
    coords = jnp.stack([lax.axis_index(axis) for axis in AXES]).astype(jnp.int32)
    place_here = coords[0] * 2 + coords[3]
    this_half = coords[4]

    parts = exchange(pack(coords, w_up, w_down.T, w_qkv.transpose(1, 0, 2), w_out.T, segments))
    shard = order(coords, parts, 2 * hidden + 4 * width)
    weights = lax.all_gather(shard, PLANE, axis=0, tiled=True)

    pair, cot_sums = enter(tokens, cotangent, layernorm_gain, layernorm_bias)
    _, pair = lax.optimization_barrier((shard, pair))
    near, far, opposite = flip(pair, "zl"), flip(pair, "zl", "mp"), flip(pair, "mp")
    pair, pair_t = gather_tokens(pair, opposite, near, far)

    doc = jnp.stack([parts[k][0, -length:] for k in (0, 2, 1, 3)]).astype(jnp.int32)
    doc = doc.reshape(4, 2, half_rows)
    doc = jnp.where(this_half == 0, doc, doc[:, ::-1]).reshape(4, length)
    halves = jnp.stack([this_half, 1 - this_half]) * half_rows
    index = (halves[:, None] + jnp.arange(half_rows, dtype=jnp.int32)).reshape(1, length)
    index = jnp.broadcast_to(index, (4, length)).astype(jnp.int32)
    b_up_here = lax.dynamic_slice_in_dim(b_up, place_here * hidden, hidden)
    b_qkv_here = lax.dynamic_slice_in_dim(b_qkv, place_here * width, width, axis=1).reshape(-1)

    tables = rotary_tables(doc, index)

    pair, pair_t, tables = lax.optimization_barrier((pair, pair_t, tables))
    hidden_pair, up_sums = hidden_units(pair, b_up_here, weights)
    mlp_grads, mlp_sums = mlp_weight_grads(pair_t, hidden_pair, up_sums, weights)
    mlp_grads = scatter_plane(mlp_grads)

    pair, pair_t, hidden_pair = lax.optimization_barrier((pair, pair_t, hidden_pair))
    right = heads(pair, weights, b_qkv_here, tables, length)

    chunks = head_grads(
        coords, pair_t, right, weights, layernorm_gain, layernorm_bias, mlp_sums, up_sums, cot_sums
    )
    chunks, hidden_pair = lax.optimization_barrier((chunks, hidden_pair))
    own, one, three, two_low, two_high = chunks
    low, high = hop(two_low, "y", 1), hop(two_high, "y", 3)
    mine, theirs = combine(hidden_pair, right, weights)
    low, high, mine, theirs = lax.optimization_barrier((low, high, mine, theirs))
    theirs = flip(theirs, "c")
    one, three = hop(bump(one, high, 1), "y", 1), hop(bump(three, low, 0), "y", 3)
    keep, sends = fold(mine, theirs)
    near, far = flip(sends[1], "zl"), flip(sends[2], "zl", "mp")
    one, three, near, far, keep, opposite = lax.optimization_barrier(
        (one, three, near, far, keep, sends[0])
    )
    along_z = [near, far, flip(opposite, "mp")]
    blocks = near_sums(own, one, three)
    blocks = [blocks[0]] + [hop(part, "x", bits) for part, bits in zip(blocks[1:], (1, 2, 3))]
    parts = exchange(cut(coords, mlp_grads, blocks))
    mixed, d_tokens = leave(
        tokens, cotangent, layernorm_gain, b_out + b_down, [keep] + along_z
    )
    grad_up_w, grad_down_w, grad_qkv_w, grad_out_w, vectors, grad_b_up, grad_b_qkv = unpack(
        coords, parts, hidden, width
    )
    vectors = (vectors + flip(vectors, "mp"))[:6].reshape(3, depth)
    return (
        mixed,
        d_tokens,
        vectors[0],
        vectors[1],
        grad_qkv_w.transpose(1, 0, 2),
        grad_b_qkv,
        grad_out_w.T,
        vectors[2],
        grad_up_w,
        grad_b_up[0],
        grad_down_w.T,
        vectors[2],
    )


def solution(mesh):
    fine = Mesh(mesh.devices.reshape(SIZES), AXES)
    dp = ("zl", "x", "y", "c")
    in_specs = (
        P(AXES, None),
        P(),
        P(),
        P(dp, None, "mp"),
        P(None, "mp"),
        P("mp", dp),
        P(),
        P(dp, "mp"),
        P("mp"),
        P("mp", dp),
        P(),
        P(dp),
        P(AXES, None),
    )
    out_specs = (
        P(AXES, None),
        P(AXES, None),
        P(),
        P(),
        P(dp, None, "mp"),
        P(None, "mp"),
        P("mp", dp),
        P(),
        P(dp, "mp"),
        P("mp"),
        P("mp", dp),
        P(),
    )
    return jax.shard_map(
        per_device, mesh=fine, in_specs=in_specs, out_specs=out_specs, check_vma=False
    )
```

```python
import functools

import jax
import jax.numpy as jnp
from jax import lax
from jax.experimental import pallas as pl
from jax.experimental.pallas import tpu as pltpu
from jax.sharding import Mesh, PartitionSpec as P

HEAD_DIM = 64
ROT = 32
HALF = ROT // 2
LANES = 128
EPSILON = 1e-05

AXES = ("zl", "x", "y", "c", "mp")
SIZES = (2, 4, 4, 2, 2)
PLANE = ("x", "y")
PAIR = ("zl", "c")

BF16 = jnp.bfloat16
F32 = jnp.float32
MIB = 1024 * 1024
GIGA = 1000 * MIB
ANY = pl.BlockSpec(memory_space=pl.ANY)
WHOLE = pl.BlockSpec(memory_space=pltpu.VMEM)
SCALARS = pl.BlockSpec(memory_space=pltpu.SMEM)


def flip(value, *axes):
    count = 2 ** len(axes)
    return lax.ppermute(value, axes, [(i, count - 1 - i) for i in range(count)])


def hop(value, axis, bits):
    return lax.ppermute(value, axis, [(i, i ^ bits) for i in range(4)])


def fold_kernel(mine_ref, theirs_ref, keep_ref, *sends):
    rows = keep_ref.shape[1]
    for which in range(2):
        for i in range(4):
            block = slice(i * rows, (i + 1) * rows)
            total = mine_ref[which, block, :].astype(F32) + theirs_ref[which, block, :].astype(F32)
            if i == 0:
                keep_ref[which] = total
            else:
                sends[i - 1][which] = total.astype(BF16)


def fold(mine, theirs):
    _, rows, depth = mine.shape
    rows, tile = rows // 4, depth // 4
    keep, *sends = pl.pallas_call(
        fold_kernel,
        grid=(4,),
        in_specs=[pl.BlockSpec((2, 4 * rows, tile), lambda j: (0, 0, j))] * 2,
        out_specs=[pl.BlockSpec((2, rows, tile), lambda j: (0, 0, j))] * 4,
        out_shape=[like((2, rows, depth), F32)] + [like((2, rows, depth))] * 3,
        compiler_params=params(16),
        cost_estimate=cost(0, 26 * rows * depth),
        name="fold",
    )(mine, theirs)
    return keep, sends


def lane_sums(value):
    total = value[:, :LANES]
    for start in range(LANES, value.shape[1], LANES):
        total = total + value[:, start : start + LANES]
    return total


def across(columns):
    ones = jnp.ones((8, columns.shape[1]), F32)
    contract = (((1,), (1,)), ((), ()))
    return lax.dot_general(
        ones, columns, contract, precision=lax.Precision.HIGHEST, preferred_element_type=F32
    )[:1]


def heads_kernel(
    pair_hbm,
    pair_t_hbm,
    weights_hbm,
    bias_ref,
    trig_ref,
    segment_col,
    segment_row,
    index_col,
    index_row,
    right_hbm,
    grads_hbm,
    bias_sums_ref,
    sums_ref,
    pair_ref,
    pair_t_ref,
    weights_ref,
    right_ref,
    grads_ref,
    linear_ref,
    query_ref,
    key_ref,
    value_ref,
    grad_ref,
    grad_query_ref,
    grad_key_ref,
    attended_ref,
    product_ref,
    level_ref,
    sems,
):
    length, width = grad_ref.shape
    count, columns = segment_row.shape[0], weights_ref.shape[1]
    tile = grads_ref.shape[2]
    scale = HEAD_DIM ** (-0.5)

    def rows_of(i):
        return pl.ds(pl.multiple_of(i * length, length), length)

    def load_tokens(i):
        some = rows_of(i)
        return pltpu.make_async_copy(pair_hbm.at[:, some, :], pair_ref.at[:, some, :], sems.at[i])

    load_weights = pltpu.make_async_copy(
        weights_hbm.at[:, pl.ds(0, columns)], weights_ref, sems.at[count]
    )
    load_features = [
        pltpu.make_async_copy(pair_t_hbm.at[i], pair_t_ref.at[i], sems.at[count + 1 + i]) for i in range(2)
    ]
    store_right = pltpu.make_async_copy(right_ref, right_hbm, sems.at[count + 3])

    def store_grads(j):
        lanes = pl.ds(pl.multiple_of(j * tile, tile), tile)
        return pltpu.make_async_copy(grads_ref.at[j], grads_hbm.at[:, lanes], sems.at[count + 4 + j])

    load_weights.start()
    for i in range(count):
        load_tokens(i).start()
    for load in load_features:
        load.start()
    load_weights.wait()
    both = (((1,), (1,)), ((), ()))

    def one_sequence(i, carry):
        some = rows_of(i)
        load_tokens(i).wait()
        linear_ref[...] = (
            jnp.dot(pair_ref[0, some, :], weights_ref[:, : 3 * width], preferred_element_type=F32)
            + bias_ref[...]
        )
        grad_ref[...] = jnp.dot(
            pair_ref[1, some, :], weights_ref[:, 3 * width :], preferred_element_type=F32
        ).astype(BF16)
        trig = trig_ref[some, :]

        def rotated(value, sign):
            ahead = pltpu.roll(value, LANES - HALF, 1)
            behind = pltpu.roll(value, HALF, 1)
            turned = ahead * trig[:, LANES : 2 * LANES] + behind * trig[:, 2 * LANES :]
            return value * trig[:, :LANES] + turned * sign

        for start in range(0, width, LANES):
            lanes = slice(start, start + LANES)
            query_ref[:, lanes] = (rotated(linear_ref[:, lanes], 1.0) * scale).astype(BF16)
            keys = linear_ref[:, width + start : width + start + LANES]
            key_ref[:, lanes] = rotated(keys, 1.0).astype(BF16)
            values = linear_ref[:, 2 * width + start : 2 * width + start + LANES]
            value_ref[:, lanes] = values.astype(BF16)
        allowed = (segment_row[i] == segment_col[some, :]) & (index_row[i] >= index_col[some, :])
        value_t, key_t = value_ref[...].T, key_ref[...].T
        for start in range(0, width, HEAD_DIM):
            lanes = slice(start, start + HEAD_DIM)
            query, key, value = query_ref[:, lanes], key_ref[:, lanes], value_ref[:, lanes]
            grad = grad_ref[:, lanes]
            scores = lax.dot_general(key, query, both, preferred_element_type=F32)
            scores = jnp.where(allowed, scores, -1000000000.0)
            expo = jnp.exp(scores - jnp.max(scores, axis=0, keepdims=True))
            probs = expo * (1.0 / jnp.sum(expo, axis=0, keepdims=True))
            low_probs = probs.astype(BF16)
            attended_ref[lanes, :] = jnp.dot(value_t[lanes], low_probs, preferred_element_type=F32)
            grad_probs = lax.dot_general(value, grad, both, preferred_element_type=F32)
            grad_values = jnp.dot(low_probs, grad, preferred_element_type=F32)
            weighted = probs * grad_probs
            delta = jnp.sum(weighted, axis=0, keepdims=True)
            grad_scores = (weighted - probs * delta).astype(BF16)
            grad_queries = jnp.dot(key_t[lanes], grad_scores, preferred_element_type=F32)
            grad_query_ref[lanes, :] = grad_queries * scale
            grad_key_ref[:, lanes] = jnp.dot(grad_scores, query, preferred_element_type=F32)
            right_ref[some, 2 * width + start : 2 * width + start + HEAD_DIM] = grad_values.astype(BF16)
        right_ref[some, 3 * width :] = attended_ref[...].T.astype(BF16)
        linear_ref[:, :width] = grad_query_ref[...].T
        for start in range(0, width, LANES):
            lanes = slice(start, start + LANES)
            right_ref[some, lanes] = rotated(linear_ref[:, lanes], -1.0).astype(BF16)
            right_ref[some, width + start : width + start + LANES] = rotated(
                grad_key_ref[:, lanes], -1.0
            ).astype(BF16)
        return carry

    lax.fori_loop(0, count, one_sequence, 0)
    store_right.start()
    for load in load_features:
        load.wait()
    product_ref[...] = jnp.zeros_like(product_ref)
    level_ref[...] = jnp.zeros_like(level_ref)

    def one_tile(j, carry):
        lanes = pl.ds(pl.multiple_of(j * tile, tile), tile)
        right = right_ref[:, lanes]
        product = jnp.dot(pair_t_ref[j // 3], right, preferred_element_type=F32)
        grads_ref[j] = product.astype(BF16)
        store_grads(j).start()
        inner = jnp.where(j < 3, 1.0, 0.0)
        sums = jnp.sum(right.astype(F32), axis=0, keepdims=True) * inner
        bias_sums_ref[:, lanes] = sums
        weights = weights_ref[:, lanes].astype(F32)
        product_ref[...] += lane_sums(weights * product) * inner
        level_ref[...] += lane_sums(weights * sums)
        return carry

    lax.fori_loop(0, 4, one_tile, 0)
    sums_ref[0:1, :] = across(level_ref[...])
    sums_ref[1:2, :] = across(product_ref[...])
    store_right.wait()
    for j in range(4):
        store_grads(j).wait()


def heads(pair, pair_t, weights, bias, tables, length):
    _, rows, depth = pair.shape
    width = bias.shape[0] // 3
    columns, count = 4 * width, rows // length
    return pl.pallas_call(
        heads_kernel,
        in_specs=[ANY] * 3 + [WHOLE] * 6,
        out_specs=[ANY, ANY, WHOLE, WHOLE],
        out_shape=[
            like((rows, columns)),
            like((depth, columns)),
            like((1, columns), F32),
            like((2, depth), F32),
        ],
        scratch_shapes=[
            pltpu.VMEM((2, rows, depth), BF16),
            pltpu.VMEM((2, depth, rows), BF16),
            pltpu.VMEM((depth, columns), BF16),
            pltpu.VMEM((rows, columns), BF16),
            pltpu.VMEM((4, depth, width), BF16),
            pltpu.VMEM((length, 3 * width), F32),
        ]
        + [pltpu.VMEM((length, width), BF16)] * 4
        + [
            pltpu.VMEM((width, length), F32),
            pltpu.VMEM((length, width), F32),
            pltpu.VMEM((width, length), F32),
            pltpu.VMEM((depth, LANES), F32),
            pltpu.VMEM((depth, LANES), F32),
            pltpu.SemaphoreType.DMA((count + 8,)),
        ],
        compiler_params=params(60),
        cost_estimate=cost(30 * GIGA, 10 * MIB),
        name="heads",
    )(pair, pair_t, weights, bias.reshape(1, -1), *tables)


def tables_kernel(cos_ref, sin_ref, *refs):
    inputs, outputs = refs[:4], refs[5:]
    trig_ref = refs[4]
    cos, sin = cos_ref[...], sin_ref[...]
    trig_ref[...] = jnp.zeros_like(trig_ref)
    for start in range(0, LANES, HEAD_DIM):
        rest = (cos.shape[0], HEAD_DIM - ROT)
        trig_ref[:, start : start + HALF] = cos
        trig_ref[:, start + HALF : start + ROT] = cos
        trig_ref[:, start + ROT : start + HEAD_DIM] = jnp.ones(rest, F32)
        trig_ref[:, LANES + start : LANES + start + HALF] = -sin
        trig_ref[:, 2 * LANES + start + HALF : 2 * LANES + start + ROT] = sin
    for source, target in zip(inputs, outputs):
        target[...] = source[...]


def rotary_tables(doc, index):
    count, length = doc.shape
    rows = count * length
    same_doc = doc[:, :, None] == doc[:, None, :]
    doc_start = jnp.min(jnp.where(same_doc, index[:, None, :], length), axis=2)
    positions = (index - doc_start).astype(F32).reshape(-1)
    inv_freq = 10000.0 ** (-(jnp.arange(HALF, dtype=F32) * 2.0 / ROT))
    angles = positions[:, None] * inv_freq
    column, row = (rows, 1), (count, 1, length)
    shapes = [column, row, column, row]
    passed = [value.reshape(shape) for value, shape in zip((doc, doc, index, index), shapes)]
    return pl.pallas_call(
        tables_kernel,
        in_specs=[WHOLE] * 6,
        out_specs=[WHOLE] * 5,
        out_shape=[like((rows, 3 * LANES), F32)] + [like(shape, jnp.int32) for shape in shapes],
        compiler_params=params(16),
        name="tables",
    )(jnp.cos(angles), jnp.sin(angles), *passed)


def like(shape, dtype=BF16):
    return jax.ShapeDtypeStruct(shape, dtype)


def params(mib):
    return pltpu.CompilerParams(vmem_limit_bytes=mib * MIB)


def cost(flops, moved):
    return pl.CostEstimate(flops=flops, bytes_accessed=moved, transcendentals=0)


def slot_of(coords, bits):
    return (coords[0] * 2 + coords[3]) ^ bits


def pack_kernel(coords, up_ref, down_ref, qkv_ref, out_ref, segment_ref, *refs):
    parts, sems = refs[:4], refs[4]
    hidden, width = up_ref.shape[1] // 4, out_ref.shape[1] // 4
    copies = []

    def copy(source, target):
        copies.append(pltpu.make_async_copy(source, target, sems.at[len(copies)]))
        copies[-1].start()

    for bits in (1, 2, 3, 0):
        slot = slot_of(coords, bits)
        wide = pl.ds(pl.multiple_of(slot * hidden, hidden), hidden)
        narrow = pl.ds(pl.multiple_of(slot * width, width), width)
        part = parts[bits]
        for kind in range(3):
            copy(qkv_ref.at[kind, :, narrow], part.at[:, pl.ds(kind * width, width)])
        copy(out_ref.at[:, narrow], part.at[:, pl.ds(3 * width, width)])
        copy(up_ref.at[:, wide], part.at[:, pl.ds(4 * width, hidden)])
        copy(down_ref.at[:, wide], part.at[:, pl.ds(4 * width + hidden, hidden)])
    segments = segment_ref[...].astype(F32).astype(BF16)
    segments = jnp.broadcast_to(segments, (up_ref.shape[0], segments.shape[1]))
    for part in parts:
        part[:, 4 * width + 2 * hidden :] = segments
    for each in copies:
        each.wait()


def pack(coords, w_up, down_t, qkv_t, out_t, segments):
    rows, hidden, width = w_up.shape[0], w_up.shape[1] // 4, out_t.shape[1] // 4
    return pl.pallas_call(
        pack_kernel,
        in_specs=[SCALARS] + [ANY] * 4 + [WHOLE],
        out_specs=[WHOLE] * 4,
        out_shape=[like((rows, 2 * hidden + 4 * width + segments.shape[0]))] * 4,
        scratch_shapes=[pltpu.SemaphoreType.DMA((24,))],
        compiler_params=params(60),
        name="pack",
    )(coords, w_up, down_t, qkv_t, out_t, segments.reshape(1, -1))


def order_kernel(coords, *refs):
    parts, out = refs[:4], refs[4]
    for bits in range(4):
        out[coords[0] ^ (bits >> 1), coords[3] ^ (bits & 1)] = parts[bits][:, : out.shape[3]]


def order(coords, parts, columns):
    rows = parts[0].shape[0]
    out = pl.pallas_call(
        order_kernel,
        in_specs=[SCALARS] + [WHOLE] * 4,
        out_specs=WHOLE,
        out_shape=like((2, 2, rows, columns)),
        compiler_params=params(16),
        name="order",
    )(coords, *parts)
    return out.reshape(4 * rows, columns)


def join_kernel(*refs):
    parts, out, sem = refs[:-2], refs[-2], refs[-1]
    copies = []
    for i, part in enumerate(parts):
        copies.append(pltpu.make_async_copy(part, out.at[i], sem.at[i]))
        copies[-1].start()
    for copy in copies:
        copy.wait()


def join(*parts):
    return pl.pallas_call(
        join_kernel,
        in_specs=[ANY] * len(parts),
        out_specs=ANY,
        out_shape=like((len(parts),) + parts[0].shape),
        scratch_shapes=[pltpu.SemaphoreType.DMA((len(parts),))],
        compiler_params=params(16),
        name="join",
    )(*parts)


def tokens_kernel(mine_ref, other_ref, rows_ref, columns_ref):
    @pl.when(pl.program_id(1) == 0)
    def _():
        rows_ref[0] = mine_ref[0, 0]
        columns_ref[0] = mine_ref[0, 0].T

    @pl.when(pl.program_id(1) == 1)
    def _():
        rows_ref[0] = other_ref[0, 0]
        columns_ref[0] = other_ref[0, 0].T


def gather_tokens(*pairs):
    mine = join(*pairs)
    other = flip(mine, "c")
    _, _, rows, depth = mine.shape
    block = (1, 1, rows, depth)
    return pl.pallas_call(
        tokens_kernel,
        grid=(2, 2, 4),
        in_specs=[
            pl.BlockSpec(block, lambda w, c, z: (jnp.where(c == 0, z, 3), w, 0, 0)),
            pl.BlockSpec(block, lambda w, c, z: (jnp.where(c == 1, z, 0), w, 0, 0)),
        ],
        out_specs=[
            pl.BlockSpec((1, rows, depth), lambda w, c, z: (w, 4 * c + z, 0)),
            pl.BlockSpec((1, depth, rows), lambda w, c, z: (w, 0, 4 * c + z)),
        ],
        out_shape=[like((2, 8 * rows, depth)), like((2, depth, 8 * rows))],
        compiler_params=params(12),
        cost_estimate=cost(0, 8 * mine.size * 2),
        name="tokens",
    )(mine, other)


def split(rows):
    high = rows.astype(BF16)
    return high, (rows - high.astype(F32)).astype(BF16)


def whole(rows):
    count = rows.shape[0] // 2
    return rows[:count].astype(F32) + rows[count:].astype(F32)


GROUPS = ((0, 4), (4, 4), (8, 4), (12, 2), (14, 2))


def place_of(first_bits, second_bits):
    return (0, 4, 12, 8)[first_bits] + second_bits


def mlp_kernel(
    coords,
    pair_hbm,
    pair_t_hbm,
    weights_hbm,
    bias_ref,
    gain_ref,
    shift_ref,
    cot_ref,
    head_sums_ref,
    head_bias_ref,
    hidden_hbm,
    *refs,
):
    up_outs, down_outs = refs[:5], refs[5:10]
    (
        pair_ref,
        pair_t_ref,
        up_ref,
        down_ref,
        hidden_ref,
        up_blocks,
        down_blocks,
        staged_ref,
        bias_sums_ref,
        rows_ref,
        turned_ref,
        product_ref,
        level_ref,
        load_sems,
        store_sems,
    ) = refs[10:]
    x, y = coords[1], coords[2]
    tiles, depth, tile = up_ref.shape
    hidden, half = tiles * tile, pair_ref.shape[1] // 2
    block = down_blocks.shape[1]
    start = weights_hbm.shape[1] - 2 * hidden
    slope = 0.7978845608028654

    def load_weights(j, which):
        lanes = pl.ds(pl.multiple_of(start + which * hidden + j * tile, tile), tile)
        target = (up_ref, down_ref)[which].at[j]
        return pltpu.make_async_copy(weights_hbm.at[:, lanes], target, load_sems.at[2 * j + which])

    def load_tokens(i):
        some = pl.ds(i * half, half)
        return pltpu.make_async_copy(
            pair_hbm.at[:, some, :], pair_ref.at[:, some, :], load_sems.at[2 * tiles + i]
        )

    load_features = [
        pltpu.make_async_copy(pair_t_hbm.at[i], pair_t_ref.at[i], load_sems.at[2 * tiles + 2 + i])
        for i in range(2)
    ]
    store_hidden = pltpu.make_async_copy(hidden_ref, hidden_hbm, store_sems.at[tiles, 0])

    def store_blocks(j):
        lanes = pl.ds(pl.multiple_of(j * tile, tile), tile)
        some = pl.ds(0, block)
        copies = []
        for blocks, outs in ((up_blocks, up_outs), (down_blocks, down_outs)):
            for (first, count), out in zip(GROUPS, outs):
                source = blocks.at[pl.ds(first, count), some, lanes]
                sem = store_sems.at[j, len(copies)]
                copies.append(pltpu.make_async_copy(source, out.at[:, some, lanes], sem))
        return copies

    load_tokens(0).start()
    for j in range(tiles):
        for which in range(2):
            load_weights(j, which).start()
        if j == 0:
            load_tokens(1).start()
    for load in load_features:
        load.start()

    def units(i):
        some = pl.ds(i * half, half)
        load_tokens(i).wait()

        def one_tile(j, carry):
            if i == 0:
                load_weights(j, 0).wait()
                load_weights(j, 1).wait()
            lanes = pl.ds(pl.multiple_of(j * tile, tile), tile)
            up = jnp.dot(pair_ref[0, some, :], up_ref[j], preferred_element_type=F32) + bias_ref[:, lanes]
            square = up * up
            wave = jnp.tanh(up * (slope + (slope * 0.044715) * square))
            gate = 0.5 + 0.5 * wave
            hidden_ref[1, some, lanes] = (up * gate).astype(BF16)
            rise = gate + up * (1.0 - wave * wave) * (0.5 * slope + (1.5 * slope * 0.044715) * square)
            grad = jnp.dot(pair_ref[1, some, :], down_ref[j], preferred_element_type=F32) * rise
            low = grad.astype(BF16)
            hidden_ref[0, some, lanes] = low
            sums = jnp.sum(low.astype(F32), axis=0, keepdims=True)
            bias_sums_ref[:, lanes] = sums if i == 0 else bias_sums_ref[:, lanes] + sums
            return carry

        lax.fori_loop(0, tiles, one_tile, 0)

    units(0)
    units(1)
    store_hidden.start()
    for load in load_features:
        load.wait()
    product_ref[...] = jnp.zeros_like(product_ref)
    level_ref[...] = jnp.zeros_like(level_ref)

    def one_tile(j, carry):
        lanes = pl.ds(pl.multiple_of(j * tile, tile), tile)
        product = jnp.dot(pair_t_ref[0], hidden_ref[0, :, lanes], preferred_element_type=F32)
        staged_ref[0] = product.astype(BF16).reshape(staged_ref.shape[1:])
        weights = up_ref[j].astype(F32)
        product_ref[...] += lane_sums(weights * product)
        level_ref[...] += lane_sums(weights * bias_sums_ref[:, lanes])
        product = jnp.dot(pair_t_ref[1], hidden_ref[1, :, lanes], preferred_element_type=F32)
        staged_ref[1] = product.astype(BF16).reshape(staged_ref.shape[1:])
        for x_bits in range(4):
            for y_bits in range(4):
                chip = (x ^ x_bits) * 4 + (y ^ y_bits)
                up_blocks[place_of(y_bits, x_bits), :block, lanes] = staged_ref[0, chip]
                down_blocks[place_of(x_bits, y_bits), :, lanes] = staged_ref[1, chip]
        for copy in store_blocks(j):
            copy.start()
        return carry

    lax.fori_loop(0, tiles, one_tile, 0)

    level = head_sums_ref[0:1, :] + across(level_ref[...])
    product = head_sums_ref[1:2, :] + across(product_ref[...])
    turn(turned_ref, jnp.concatenate([product, level], axis=0), True)
    level = turned_ref[1:2, :]
    by_gain = (turned_ref[0:1, :] - shift_ref[...] * level) / gain_ref[...]
    for i, row in enumerate((by_gain, level, cot_ref[...])):
        rows_ref[2 * i : 2 * i + 1, :] = row[:, :hidden]
        rows_ref[2 * i + 1 : 2 * i + 2, :] = row[:, hidden:]
    rows_ref[6:7, :] = bias_sums_ref[...]
    rows_ref[7:8, :] = head_bias_ref[...]
    high, low = split(rows_ref[...])
    vectors = jnp.concatenate([high.astype(F32), low.astype(F32)], axis=0).astype(BF16)
    for i in range(16):
        up_blocks[i, block:, :] = vectors
    copies = []
    for (first, count), out in zip(GROUPS, up_outs):
        source = up_blocks.at[pl.ds(first, count), pl.ds(block, 16), :]
        sem = store_sems.at[tiles, 1 + len(copies)]
        copies.append(pltpu.make_async_copy(source, out.at[:, pl.ds(block, 16), :], sem))
        copies[-1].start()
    store_hidden.wait()
    for j in range(tiles):
        copies += store_blocks(j)
    for copy in copies:
        copy.wait()


def mlp(coords, pair, pair_t, weights, bias, gain, shift, cot_sums, head_sums, head_bias):
    _, rows, depth = pair.shape
    hidden = bias.shape[0]
    tiles, block = 4, depth // 16
    tile = hidden // tiles
    ups = [like((count, block + 16, hidden)) for _, count in GROUPS]
    downs = [like((count, block, hidden)) for _, count in GROUPS]
    outs = pl.pallas_call(
        mlp_kernel,
        in_specs=[SCALARS] + [ANY] * 3 + [WHOLE] * 6,
        out_specs=[ANY] * 11,
        out_shape=[like((2, rows, hidden)), *ups, *downs],
        scratch_shapes=[
            pltpu.VMEM((2, rows, depth), BF16),
            pltpu.VMEM((2, depth, rows), BF16),
            pltpu.VMEM((tiles, depth, tile), BF16),
            pltpu.VMEM((tiles, depth, tile), BF16),
            pltpu.VMEM((2, rows, hidden), BF16),
            pltpu.VMEM((16, block + 16, hidden), BF16),
            pltpu.VMEM((16, block, hidden), BF16),
            pltpu.VMEM((2, 16, block, tile), BF16),
            pltpu.VMEM((1, hidden), F32),
            pltpu.VMEM((8, hidden), F32),
            pltpu.VMEM((2, depth), F32),
            pltpu.VMEM((depth, LANES), F32),
            pltpu.VMEM((depth, LANES), F32),
            pltpu.SemaphoreType.DMA((2 * tiles + 4,)),
            pltpu.SemaphoreType.DMA((tiles + 1, 10)),
        ],
        compiler_params=params(60),
        cost_estimate=cost(8 * rows * depth * hidden, 40 * MIB),
        name="mlp",
    )(
        coords,
        pair,
        pair_t,
        weights,
        bias.reshape(1, -1),
        gain.reshape(1, -1),
        shift.reshape(1, -1),
        cot_sums,
        head_sums,
        head_bias,
    )
    return outs[0], outs[1:6], outs[6:]


def add_blocks(parts, target, vectors):
    end = parts[0].shape[0] - 16 if vectors else parts[0].shape[0]
    data = parts[0][:end].astype(F32)
    for part in parts[1:]:
        data = data + part[:end].astype(F32)
    target[:end, :] = data.astype(target.dtype)
    if vectors:
        rows = whole(parts[0][end:])
        for part in parts[1:]:
            rows = rows + whole(part[end:])
        if target.dtype == F32:
            target[end:, :] = rows
        else:
            high, low = split(rows)
            target[end:, :] = jnp.concatenate([high.astype(F32), low.astype(F32)], axis=0).astype(BF16)


def bump_kernel(*refs):
    for i in range(4):
        chunk, part, out = refs[2 * i], refs[2 * i + 1], refs[8 + i]
        for k in range(2):
            add_blocks([chunk[k], part[k]], out.at[k], i < 2)


def bump(*chunks):
    specs, arrays, outs = [], [], []
    for chunk, part, half in chunks:
        shape = part.shape
        spec = pl.BlockSpec(shape, lambda i, half=half: (half, 0, 0))
        specs += [spec, pl.BlockSpec(shape, lambda i: (0, 0, 0))]
        arrays += [chunk, part]
        outs.append(spec)
    return pl.pallas_call(
        bump_kernel,
        grid=(1,),
        in_specs=specs,
        out_specs=outs,
        out_shape=[like(chunk.shape) for chunk, _, _ in chunks],
        input_output_aliases={0: 0, 2: 1, 4: 2, 6: 3},
        compiler_params=params(24),
        name="bump",
    )(*arrays)


def near_kernel(*refs):
    for side in range(2):
        own, one, three = refs[3 * side : 3 * side + 3]
        outs = refs[6 + 4 * side : 10 + 4 * side]
        for i in range(4):
            add_blocks([own[i], one[i], three[i]], outs[i], side == 0)


def near_sums(*chunks):
    shapes = []
    for chunk, less in ((chunks[0], 8), (chunks[3], 0)):
        rows, columns = chunk.shape[1:]
        shapes += [like((rows - less, columns), F32)] + [like((rows, columns))] * 3
    outs = pl.pallas_call(
        near_kernel,
        in_specs=[WHOLE] * 6,
        out_specs=[WHOLE] * 8,
        out_shape=shapes,
        compiler_params=params(24),
        name="near",
    )(*chunks)
    return outs[:4], outs[4:]


def cut_heads_kernel(coords, heads_ref, *outs):
    rows = outs[0].shape[0]
    for bits in range(4):
        some = pl.ds(pl.multiple_of(slot_of(coords, bits) * rows, rows), rows)
        outs[bits][...] = heads_ref[some, :]


def cut_heads(coords, grads):
    rows, columns = grads.shape[0] // 4, grads.shape[1]
    return pl.pallas_call(
        cut_heads_kernel,
        in_specs=[SCALARS, WHOLE],
        out_specs=[WHOLE] * 4,
        out_shape=[like((rows, columns))] * 4,
        compiler_params=params(16),
        name="cut_heads",
    )(coords, grads)


def cut_kernel(coords, *refs):
    up, down, heads, outs = refs[:4], refs[4:8], refs[8:12], refs[12:]
    rows, hidden = outs[0].shape[0], up[0].shape[1]
    block = 4 * rows
    vectors = up[0][block:, :]
    for other in up[1:]:
        vectors = vectors + whole(other[block:, :])
    high, low = split(vectors)
    vectors = jnp.concatenate([high.astype(F32), low.astype(F32)], axis=0).astype(BF16)
    for bits in range(4):
        some = pl.ds(pl.multiple_of(slot_of(coords, bits) * rows, rows), rows)
        out = outs[bits]
        for side, blocks in enumerate((up, down)):
            total = blocks[0][some, :]
            for other in blocks[1:]:
                total = total + other[some, :].astype(F32)
            out[:, side * hidden : (side + 1) * hidden] = total.astype(BF16)
        end = 2 * hidden + heads[bits].shape[1]
        out[:, 2 * hidden : end] = heads[bits][...]
        out[:16, end:] = vectors[:, : hidden // 2]
        out[16:, end:] = vectors[:, hidden // 2 :]


def cut(coords, up, down, heads):
    rows, hidden = heads[0].shape[0], up[0].shape[1]
    columns = 2 * hidden + heads[0].shape[1] + hidden // 2
    return pl.pallas_call(
        cut_kernel,
        in_specs=[SCALARS] + [WHOLE] * 12,
        out_specs=[WHOLE] * 4,
        out_shape=[like((rows, columns))] * 4,
        compiler_params=params(16),
        name="cut",
    )(coords, *up, *down, *heads)


def combine_kernel(hidden_ref, right_ref, weights_ref, mine_ref, theirs_ref):
    contract = (((1,), (1,)), ((), ()))
    hidden, columns = hidden_ref.shape[2], right_ref.shape[1]
    inner = columns * 3 // 4
    half = mine_ref.shape[1]

    def product(left, start):
        weights = weights_ref[:, start : start + left.shape[1]]
        return lax.dot_general(left, weights, contract, preferred_element_type=F32)

    total = product(hidden_ref[0], columns) + product(right_ref[:, :inner], 0)
    mine_ref[0] = total[:half].astype(BF16)
    theirs_ref[0] = total[half:].astype(BF16)
    total = product(hidden_ref[1], columns + hidden) + product(right_ref[:, inner:], inner)
    mine_ref[1] = total[:half].astype(BF16)
    theirs_ref[1] = total[half:].astype(BF16)


def combine(hidden_pair, right, weights):
    _, rows, hidden = hidden_pair.shape
    depth, columns = weights.shape
    tile = depth // 4
    block = pl.BlockSpec((2, rows // 2, tile), lambda i: (0, 0, i))
    return pl.pallas_call(
        combine_kernel,
        grid=(4,),
        in_specs=[WHOLE, WHOLE, pl.BlockSpec((tile, columns), lambda i: (i, 0))],
        out_specs=[block] * 2,
        out_shape=[like((2, rows // 2, depth))] * 2,
        compiler_params=params(40),
        cost_estimate=cost(2 * rows * depth * columns, 16 * MIB),
        name="combine",
    )(hidden_pair, right, weights)


def exchange(parts):
    return [parts[0], flip(parts[1], "c"), flip(parts[2], "zl"), flip(parts[3], "zl", "c")]


def unpack_kernel(coords, *refs):
    parts, (up_ref, down_ref, qkv_ref, out_ref, rows_ref, up_sums_ref, qkv_sums_ref) = refs[:4], refs[4:]
    hidden, width = up_ref.shape[1] // 4, out_ref.shape[1] // 4
    for bits in range(4):
        slot, part = slot_of(coords, bits), parts[bits]
        wide = pl.ds(pl.multiple_of(slot * hidden, hidden), hidden)
        narrow = pl.ds(pl.multiple_of(slot * width, width), width)
        up_ref[:, wide] = part[:, :hidden].astype(F32)
        down_ref[:, wide] = part[:, hidden : 2 * hidden].astype(F32)
        start = 2 * hidden
        for kind in range(3):
            qkv_ref[kind, :, narrow] = part[:, start + kind * width : start + (kind + 1) * width].astype(F32)
        out_ref[:, narrow] = part[:, start + 3 * width : start + 4 * width].astype(F32)
        start += 4 * width
        vectors = jnp.concatenate([whole(part[:16, start:]), whole(part[16:, start:])], axis=1)
        rows_ref[...] = vectors if bits == 0 else rows_ref[...] + vectors
        up_sums_ref[:, wide] = vectors[6:7, :]
        for kind in range(3):
            qkv_sums_ref[kind : kind + 1, narrow] = vectors[7:8, kind * width : (kind + 1) * width]


def unpack(coords, parts, hidden, width):
    rows = parts[0].shape[0]
    wide, narrow = (rows, 4 * hidden), (rows, 4 * width)
    shapes = [wide, wide, (3,) + narrow, narrow, (8, hidden), (1, 4 * hidden), (3, 4 * width)]
    return pl.pallas_call(
        unpack_kernel,
        in_specs=[SCALARS] + [WHOLE] * 4,
        out_specs=[WHOLE] * 7,
        out_shape=[like(shape, F32) for shape in shapes],
        compiler_params=params(16),
        name="unpack",
    )(coords, *parts)


def turn(dest, value, back):
    block = value.shape[1] // 32
    for chip in range(16):
        for zl in range(2):
            natural, inside = (zl * 16 + chip) * block, (chip * 2 + zl) * block
            source, target = (inside, natural) if back else (natural, inside)
            dest[:, target : target + block] = value[:, source : source + block].astype(dest.dtype)


def standardize(tokens):
    rows = tokens.astype(F32)
    centered = rows - jnp.mean(rows, axis=1, keepdims=True)
    scale = lax.rsqrt(jnp.mean(centered * centered, axis=1, keepdims=True) + EPSILON)
    return rows, centered * scale, scale


def enter_kernel(tokens_ref, cot_ref, gain_ref, bias_ref, pair_ref, sums_ref):
    _, standard, _ = standardize(tokens_ref[...])
    turn(pair_ref.at[0], (standard * gain_ref[...] + bias_ref[...]).astype(BF16), False)
    turn(pair_ref.at[1], cot_ref[...], False)
    sums_ref[...] = jnp.sum(cot_ref[...].astype(F32), axis=0, keepdims=True)


def enter(tokens, cotangent, gain, bias):
    return pl.pallas_call(
        enter_kernel,
        in_specs=[WHOLE] * 4,
        out_specs=[WHOLE] * 2,
        out_shape=[like((2,) + tokens.shape), like((1, tokens.shape[1]), F32)],
        compiler_params=params(16),
        name="enter",
    )(tokens, cotangent, gain.reshape(1, -1), bias.reshape(1, -1))


def leave_kernel(tokens_ref, cot_ref, gain_ref, bias_ref, *refs):
    mixed_ref, grad_ref, branch_ref, normed_ref = refs[-4:]
    for which, target in ((0, normed_ref), (1, branch_ref)):
        total = refs[0][which]
        for part in refs[1:4]:
            total = total + part[which].astype(F32)
        turn(target, total, True)
    rows, standard, scale = standardize(tokens_ref[...])
    mixed_ref[...] = (rows + branch_ref[...] + bias_ref[...]).astype(BF16)
    grad = normed_ref[...] * gain_ref[...]
    level = jnp.mean(grad, axis=1, keepdims=True)
    slope = jnp.mean(grad * standard, axis=1, keepdims=True)
    grad_ref[...] = cot_ref[...].astype(F32) + scale * (grad - level - standard * slope)


def leave(tokens, cotangent, gain, bias, sums):
    shape = tokens.shape
    return pl.pallas_call(
        leave_kernel,
        in_specs=[WHOLE] * 8,
        out_specs=[WHOLE] * 2,
        out_shape=[like(shape), like(shape, F32)],
        scratch_shapes=[pltpu.VMEM(shape, F32)] * 2,
        compiler_params=params(24),
        name="leave",
    )(tokens, cotangent, gain.reshape(1, -1), bias.reshape(1, -1), *sums)


def scatter_plane(grads):
    return lax.psum_scatter(grads, PLANE, scatter_dimension=0, tiled=True)


def per_device(
    tokens,
    layernorm_gain,
    layernorm_bias,
    w_qkv,
    b_qkv,
    w_out,
    b_out,
    w_up,
    b_up,
    w_down,
    b_down,
    segments,
    cotangent,
):
    depth = tokens.shape[1]
    length = segments.shape[0]
    half_rows = tokens.shape[0]
    width = w_out.shape[0] // 4
    hidden = w_down.shape[0] // 4
    rows = w_up.shape[0]
    coords = jnp.stack([lax.axis_index(axis) for axis in AXES]).astype(jnp.int32)
    place_here = coords[0] * 2 + coords[3]
    this_half = coords[4]

    parts = exchange(pack(coords, w_up, w_down.T, w_qkv.transpose(1, 0, 2), w_out.T, segments))
    shard = order(coords, parts, 2 * hidden + 4 * width)
    weights = lax.all_gather(shard, PLANE, axis=0, tiled=True)

    pair, cot_sums = enter(tokens, cotangent, layernorm_gain, layernorm_bias)
    _, pair = lax.optimization_barrier((shard, pair))
    near, far, opposite = flip(pair, "zl"), flip(pair, "zl", "mp"), flip(pair, "mp")
    pair, pair_t = gather_tokens(pair, opposite, near, far)

    doc = jnp.stack([parts[k][0, -length:] for k in (0, 2, 1, 3)]).astype(jnp.int32)
    doc = doc.reshape(4, 2, half_rows)
    doc = jnp.where(this_half == 0, doc, doc[:, ::-1]).reshape(4, length)
    halves = jnp.stack([this_half, 1 - this_half]) * half_rows
    index = (halves[:, None] + jnp.arange(half_rows, dtype=jnp.int32)).reshape(1, length)
    index = jnp.broadcast_to(index, (4, length)).astype(jnp.int32)
    b_up_here = lax.dynamic_slice_in_dim(b_up, place_here * hidden, hidden)
    b_qkv_here = lax.dynamic_slice_in_dim(b_qkv, place_here * width, width, axis=1).reshape(-1)

    tables = rotary_tables(doc, index)

    pair, pair_t, tables = lax.optimization_barrier((pair, pair_t, tables))
    right, head_grads, head_bias, head_sums = heads(pair, pair_t, weights, b_qkv_here, tables, length)
    head_grads = scatter_plane(head_grads)

    right, pair, pair_t = lax.optimization_barrier((right, pair, pair_t))
    hidden_pair, up_blocks, down_blocks = mlp(
        coords,
        pair,
        pair_t,
        weights,
        b_up_here,
        layernorm_gain,
        layernorm_bias,
        cot_sums,
        head_sums,
        head_bias,
    )

    up_blocks, down_blocks, hidden_pair = lax.optimization_barrier((up_blocks, down_blocks, hidden_pair))
    up_own, up_one, up_three, up_low, up_high = up_blocks
    down_own, down_one, down_three, down_low, down_high = down_blocks
    low = [hop(up_low, "y", 1), hop(down_low, "x", 1)]
    high = [hop(up_high, "y", 3), hop(down_high, "x", 3)]
    mine, theirs = combine(hidden_pair, right, weights)
    low, high, mine, theirs = lax.optimization_barrier((low, high, mine, theirs))
    theirs = flip(theirs, "c")
    up_one, up_three, down_one, down_three = bump(
        (up_one, high[0], 1), (up_three, low[0], 0), (down_one, high[1], 1), (down_three, low[1], 0)
    )
    up_one, up_three = hop(up_one, "y", 1), hop(up_three, "y", 3)
    down_one, down_three = hop(down_one, "x", 1), hop(down_three, "x", 3)
    keep, sends = fold(mine, theirs)
    near = flip(sends[1], "zl")
    head_parts = cut_heads(coords, head_grads)
    up_one, up_three, down_one, down_three, near, keep, far, opposite, head_parts = lax.optimization_barrier(
        (up_one, up_three, down_one, down_three, near, keep, sends[2], sends[0], head_parts)
    )
    along_z = [near, flip(far, "zl", "mp"), flip(opposite, "mp")]
    up_sums, down_sums = near_sums(up_own, up_one, up_three, down_own, down_one, down_three)
    up_sums = [up_sums[0]] + [hop(part, "x", bits) for part, bits in zip(up_sums[1:], (1, 2, 3))]
    down_sums = [down_sums[0]] + [hop(part, "y", bits) for part, bits in zip(down_sums[1:], (1, 2, 3))]
    parts = exchange(cut(coords, up_sums, down_sums, head_parts))
    mixed, d_tokens = leave(
        tokens, cotangent, layernorm_gain, b_out + b_down, [keep] + along_z
    )
    grad_up_w, grad_down_w, grad_qkv_w, grad_out_w, vectors, grad_b_up, grad_b_qkv = unpack(
        coords, parts, hidden, width
    )
    swapped, mixed, d_tokens = lax.optimization_barrier((flip(vectors, "mp"), mixed, d_tokens))
    vectors = (vectors + swapped)[:6].reshape(3, depth)
    return (
        mixed,
        d_tokens,
        vectors[0],
        vectors[1],
        grad_qkv_w.transpose(1, 0, 2),
        grad_b_qkv,
        grad_out_w.T,
        vectors[2],
        grad_up_w,
        grad_b_up[0],
        grad_down_w.T,
        vectors[2],
    )


def solution(mesh):
    fine = Mesh(mesh.devices.reshape(SIZES), AXES)
    dp = ("zl", "x", "y", "c")
    in_specs = (
        P(AXES, None),
        P(),
        P(),
        P(dp, None, "mp"),
        P(None, "mp"),
        P("mp", dp),
        P(),
        P(dp, "mp"),
        P("mp"),
        P("mp", dp),
        P(),
        P(dp),
        P(AXES, None),
    )
    out_specs = (
        P(AXES, None),
        P(AXES, None),
        P(),
        P(),
        P(dp, None, "mp"),
        P(None, "mp"),
        P("mp", dp),
        P(),
        P(dp, "mp"),
        P("mp"),
        P("mp", dp),
        P(),
    )
    return jax.shard_map(
        per_device, mesh=fine, in_specs=in_specs, out_specs=out_specs, check_vma=False
    )
```

```python
import functools

import jax
import jax.numpy as jnp
from jax import lax
from jax.experimental import pallas as pl
from jax.experimental.pallas import tpu as pltpu
from jax.sharding import Mesh, PartitionSpec as P

HEAD_DIM = 64
ROT = 32
HALF = ROT // 2
LANES = 128
EPSILON = 1e-05

AXES = ("zl", "x", "y", "c", "mp")
SIZES = (2, 4, 4, 2, 2)
PLANE = ("x", "y")
PAIR = ("zl", "c")

BF16 = jnp.bfloat16
F32 = jnp.float32
MIB = 1024 * 1024
GIGA = 1000 * MIB
ANY = pl.BlockSpec(memory_space=pl.ANY)
WHOLE = pl.BlockSpec(memory_space=pltpu.VMEM)
SCALARS = pl.BlockSpec(memory_space=pltpu.SMEM)


def flip(value, *axes):
    count = 2 ** len(axes)
    return lax.ppermute(value, axes, [(i, count - 1 - i) for i in range(count)])


def hop(value, axis, bits):
    return lax.ppermute(value, axis, [(i, i ^ bits) for i in range(4)])


def fold_kernel(mine_ref, theirs_ref, keep_ref, *sends):
    rows = keep_ref.shape[1]
    for which in range(2):
        for i in range(4):
            block = slice(i * rows, (i + 1) * rows)
            total = mine_ref[which, block, :].astype(F32) + theirs_ref[which, block, :].astype(F32)
            if i == 0:
                keep_ref[which] = total
            else:
                sends[i - 1][which] = total.astype(BF16)


def fold(mine, theirs):
    _, rows, depth = mine.shape
    rows, tile = rows // 4, depth // 4
    keep, *sends = pl.pallas_call(
        fold_kernel,
        grid=(4,),
        in_specs=[pl.BlockSpec((2, 4 * rows, tile), lambda j: (0, 0, j))] * 2,
        out_specs=[pl.BlockSpec((2, rows, tile), lambda j: (0, 0, j))] * 4,
        out_shape=[like((2, rows, depth), F32)] + [like((2, rows, depth))] * 3,
        compiler_params=params(16),
        cost_estimate=cost(0, 26 * rows * depth),
        name="fold",
    )(mine, theirs)
    return keep, sends


def lane_sums(value):
    total = value[:, :LANES]
    for start in range(LANES, value.shape[1], LANES):
        total = total + value[:, start : start + LANES]
    return total


def across(columns):
    ones = jnp.ones((8, columns.shape[1]), F32)
    contract = (((1,), (1,)), ((), ()))
    return lax.dot_general(
        ones, columns, contract, precision=lax.Precision.HIGHEST, preferred_element_type=F32
    )[:1]


def heads_kernel(
    pair_hbm,
    pair_t_hbm,
    weights_hbm,
    bias_ref,
    trig_ref,
    segment_col,
    segment_row,
    index_col,
    index_row,
    right_hbm,
    grads_hbm,
    bias_sums_ref,
    sums_ref,
    pair_ref,
    pair_t_ref,
    weights_ref,
    right_ref,
    grads_ref,
    linear_ref,
    query_ref,
    key_ref,
    value_ref,
    grad_ref,
    grad_query_ref,
    grad_key_ref,
    attended_ref,
    product_ref,
    level_ref,
    sems,
):
    length, width = grad_ref.shape
    count, columns = segment_row.shape[0], weights_ref.shape[1]
    tile = grads_ref.shape[2]
    scale = HEAD_DIM ** (-0.5)

    def rows_of(i):
        return pl.ds(pl.multiple_of(i * length, length), length)

    def load_tokens(i):
        some = rows_of(i)
        return pltpu.make_async_copy(pair_hbm.at[:, some, :], pair_ref.at[:, some, :], sems.at[i])

    load_weights = pltpu.make_async_copy(
        weights_hbm.at[:, pl.ds(0, columns)], weights_ref, sems.at[count]
    )
    load_features = [
        pltpu.make_async_copy(pair_t_hbm.at[i], pair_t_ref.at[i], sems.at[count + 1 + i]) for i in range(2)
    ]
    store_right = pltpu.make_async_copy(right_ref, right_hbm, sems.at[count + 3])

    def store_grads(j):
        lanes = pl.ds(pl.multiple_of(j * tile, tile), tile)
        return pltpu.make_async_copy(grads_ref.at[j], grads_hbm.at[:, lanes], sems.at[count + 4 + j])

    load_weights.start()
    for i in range(count):
        load_tokens(i).start()
    for load in load_features:
        load.start()
    load_weights.wait()
    both = (((1,), (1,)), ((), ()))

    def one_sequence(i, carry):
        some = rows_of(i)
        load_tokens(i).wait()
        linear_ref[...] = (
            jnp.dot(pair_ref[0, some, :], weights_ref[:, : 3 * width], preferred_element_type=F32)
            + bias_ref[...]
        )
        grad_ref[...] = jnp.dot(
            pair_ref[1, some, :], weights_ref[:, 3 * width :], preferred_element_type=F32
        ).astype(BF16)
        trig = trig_ref[some, :]

        def rotated(value, sign):
            ahead = pltpu.roll(value, LANES - HALF, 1)
            behind = pltpu.roll(value, HALF, 1)
            turned = ahead * trig[:, LANES : 2 * LANES] + behind * trig[:, 2 * LANES :]
            return value * trig[:, :LANES] + turned * sign

        for start in range(0, width, LANES):
            lanes = slice(start, start + LANES)
            query_ref[:, lanes] = (rotated(linear_ref[:, lanes], 1.0) * scale).astype(BF16)
            keys = linear_ref[:, width + start : width + start + LANES]
            key_ref[:, lanes] = rotated(keys, 1.0).astype(BF16)
            values = linear_ref[:, 2 * width + start : 2 * width + start + LANES]
            value_ref[:, lanes] = values.astype(BF16)
        allowed = (segment_row[i] == segment_col[some, :]) & (index_row[i] >= index_col[some, :])
        value_t, key_t = value_ref[...].T, key_ref[...].T
        for start in range(0, width, HEAD_DIM):
            lanes = slice(start, start + HEAD_DIM)
            query, key, value = query_ref[:, lanes], key_ref[:, lanes], value_ref[:, lanes]
            grad = grad_ref[:, lanes]
            scores = lax.dot_general(key, query, both, preferred_element_type=F32)
            scores = jnp.where(allowed, scores, -1000000000.0)
            expo = jnp.exp(scores - jnp.max(scores, axis=0, keepdims=True))
            probs = expo * (1.0 / jnp.sum(expo, axis=0, keepdims=True))
            low_probs = probs.astype(BF16)
            attended_ref[lanes, :] = jnp.dot(value_t[lanes], low_probs, preferred_element_type=F32)
            grad_probs = lax.dot_general(value, grad, both, preferred_element_type=F32)
            grad_values = jnp.dot(low_probs, grad, preferred_element_type=F32)
            weighted = probs * grad_probs
            delta = jnp.sum(weighted, axis=0, keepdims=True)
            grad_scores = (weighted - probs * delta).astype(BF16)
            grad_queries = jnp.dot(key_t[lanes], grad_scores, preferred_element_type=F32)
            grad_query_ref[lanes, :] = grad_queries * scale
            grad_key_ref[:, lanes] = jnp.dot(grad_scores, query, preferred_element_type=F32)
            right_ref[some, 2 * width + start : 2 * width + start + HEAD_DIM] = grad_values.astype(BF16)
        right_ref[some, 3 * width :] = attended_ref[...].T.astype(BF16)
        linear_ref[:, :width] = grad_query_ref[...].T
        for start in range(0, width, LANES):
            lanes = slice(start, start + LANES)
            right_ref[some, lanes] = rotated(linear_ref[:, lanes], -1.0).astype(BF16)
            right_ref[some, width + start : width + start + LANES] = rotated(
                grad_key_ref[:, lanes], -1.0
            ).astype(BF16)
        return carry

    lax.fori_loop(0, count, one_sequence, 0)
    store_right.start()
    for load in load_features:
        load.wait()
    product_ref[...] = jnp.zeros_like(product_ref)
    level_ref[...] = jnp.zeros_like(level_ref)

    def one_tile(j, carry):
        lanes = pl.ds(pl.multiple_of(j * tile, tile), tile)
        right = right_ref[:, lanes]
        product = jnp.dot(pair_t_ref[j // 3], right, preferred_element_type=F32)
        grads_ref[j] = product.astype(BF16)
        store_grads(j).start()
        inner = jnp.where(j < 3, 1.0, 0.0)
        sums = jnp.sum(right.astype(F32), axis=0, keepdims=True) * inner
        bias_sums_ref[:, lanes] = sums
        weights = weights_ref[:, lanes].astype(F32)
        product_ref[...] += lane_sums(weights * product) * inner
        level_ref[...] += lane_sums(weights * sums)
        return carry

    lax.fori_loop(0, 4, one_tile, 0)
    sums_ref[0:1, :] = across(level_ref[...])
    sums_ref[1:2, :] = across(product_ref[...])
    store_right.wait()
    for j in range(4):
        store_grads(j).wait()


def heads(pair, pair_t, weights, bias, tables, length):
    _, rows, depth = pair.shape
    width = bias.shape[0] // 3
    columns, count = 4 * width, rows // length
    return pl.pallas_call(
        heads_kernel,
        in_specs=[ANY] * 3 + [WHOLE] * 6,
        out_specs=[ANY, ANY, WHOLE, WHOLE],
        out_shape=[
            like((rows, columns)),
            like((depth, columns)),
            like((1, columns), F32),
            like((2, depth), F32),
        ],
        scratch_shapes=[
            pltpu.VMEM((2, rows, depth), BF16),
            pltpu.VMEM((2, depth, rows), BF16),
            pltpu.VMEM((depth, columns), BF16),
            pltpu.VMEM((rows, columns), BF16),
            pltpu.VMEM((4, depth, width), BF16),
            pltpu.VMEM((length, 3 * width), F32),
        ]
        + [pltpu.VMEM((length, width), BF16)] * 4
        + [
            pltpu.VMEM((width, length), F32),
            pltpu.VMEM((length, width), F32),
            pltpu.VMEM((width, length), F32),
            pltpu.VMEM((depth, LANES), F32),
            pltpu.VMEM((depth, LANES), F32),
            pltpu.SemaphoreType.DMA((count + 8,)),
        ],
        compiler_params=params(60),
        cost_estimate=cost(30 * GIGA, 10 * MIB),
        name="heads",
    )(pair, pair_t, weights, bias.reshape(1, -1), *tables)


def tables_kernel(cos_ref, sin_ref, *refs):
    inputs, outputs = refs[:4], refs[5:]
    trig_ref = refs[4]
    cos, sin = cos_ref[...], sin_ref[...]
    trig_ref[...] = jnp.zeros_like(trig_ref)
    for start in range(0, LANES, HEAD_DIM):
        rest = (cos.shape[0], HEAD_DIM - ROT)
        trig_ref[:, start : start + HALF] = cos
        trig_ref[:, start + HALF : start + ROT] = cos
        trig_ref[:, start + ROT : start + HEAD_DIM] = jnp.ones(rest, F32)
        trig_ref[:, LANES + start : LANES + start + HALF] = -sin
        trig_ref[:, 2 * LANES + start + HALF : 2 * LANES + start + ROT] = sin
    for source, target in zip(inputs, outputs):
        target[...] = source[...]


def rotary_tables(doc, index):
    count, length = doc.shape
    rows = count * length
    same_doc = doc[:, :, None] == doc[:, None, :]
    doc_start = jnp.min(jnp.where(same_doc, index[:, None, :], length), axis=2)
    positions = (index - doc_start).astype(F32).reshape(-1)
    inv_freq = 10000.0 ** (-(jnp.arange(HALF, dtype=F32) * 2.0 / ROT))
    angles = positions[:, None] * inv_freq
    column, row = (rows, 1), (count, 1, length)
    shapes = [column, row, column, row]
    passed = [value.reshape(shape) for value, shape in zip((doc, doc, index, index), shapes)]
    return pl.pallas_call(
        tables_kernel,
        in_specs=[WHOLE] * 6,
        out_specs=[WHOLE] * 5,
        out_shape=[like((rows, 3 * LANES), F32)] + [like(shape, jnp.int32) for shape in shapes],
        compiler_params=params(16),
        name="tables",
    )(jnp.cos(angles), jnp.sin(angles), *passed)


def like(shape, dtype=BF16):
    return jax.ShapeDtypeStruct(shape, dtype)


def params(mib):
    return pltpu.CompilerParams(vmem_limit_bytes=mib * MIB)


def cost(flops, moved):
    return pl.CostEstimate(flops=flops, bytes_accessed=moved, transcendentals=0)


def slot_of(coords, bits):
    return (coords[0] * 2 + coords[3]) ^ bits


def pack_kernel(coords, up_ref, down_ref, qkv_ref, out_ref, segment_ref, *refs):
    parts, sems = refs[:4], refs[4]
    hidden, width = up_ref.shape[1] // 4, out_ref.shape[1] // 4
    copies = []

    def copy(source, target):
        copies.append(pltpu.make_async_copy(source, target, sems.at[len(copies)]))
        copies[-1].start()

    for bits in (1, 2, 3, 0):
        slot = slot_of(coords, bits)
        wide = pl.ds(pl.multiple_of(slot * hidden, hidden), hidden)
        narrow = pl.ds(pl.multiple_of(slot * width, width), width)
        part = parts[bits]
        for kind in range(3):
            copy(qkv_ref.at[kind, :, narrow], part.at[:, pl.ds(kind * width, width)])
        copy(out_ref.at[:, narrow], part.at[:, pl.ds(3 * width, width)])
        copy(up_ref.at[:, wide], part.at[:, pl.ds(4 * width, hidden)])
        copy(down_ref.at[:, wide], part.at[:, pl.ds(4 * width + hidden, hidden)])
    segments = segment_ref[...].astype(F32).astype(BF16)
    segments = jnp.broadcast_to(segments, (up_ref.shape[0], segments.shape[1]))
    for part in parts:
        part[:, 4 * width + 2 * hidden :] = segments
    for each in copies:
        each.wait()


def pack(coords, w_up, down_t, qkv_t, out_t, segments):
    rows, hidden, width = w_up.shape[0], w_up.shape[1] // 4, out_t.shape[1] // 4
    return pl.pallas_call(
        pack_kernel,
        in_specs=[SCALARS] + [ANY] * 4 + [WHOLE],
        out_specs=[WHOLE] * 4,
        out_shape=[like((rows, 2 * hidden + 4 * width + segments.shape[0]))] * 4,
        scratch_shapes=[pltpu.SemaphoreType.DMA((24,))],
        compiler_params=params(60),
        name="pack",
    )(coords, w_up, down_t, qkv_t, out_t, segments.reshape(1, -1))


def order_kernel(coords, *refs):
    parts, out = refs[:4], refs[4]
    for bits in range(4):
        out[coords[0] ^ (bits >> 1), coords[3] ^ (bits & 1)] = parts[bits][:, : out.shape[3]]


def order(coords, parts, columns):
    rows = parts[0].shape[0]
    out = pl.pallas_call(
        order_kernel,
        in_specs=[SCALARS] + [WHOLE] * 4,
        out_specs=WHOLE,
        out_shape=like((2, 2, rows, columns)),
        compiler_params=params(16),
        name="order",
    )(coords, *parts)
    return out.reshape(4 * rows, columns)


def join_kernel(*refs):
    parts, out, sem = refs[:-2], refs[-2], refs[-1]
    copies = []
    for i, part in enumerate(parts):
        copies.append(pltpu.make_async_copy(part, out.at[i], sem.at[i]))
        copies[-1].start()
    for copy in copies:
        copy.wait()


def join(*parts):
    return pl.pallas_call(
        join_kernel,
        in_specs=[ANY] * len(parts),
        out_specs=ANY,
        out_shape=like((len(parts),) + parts[0].shape),
        scratch_shapes=[pltpu.SemaphoreType.DMA((len(parts),))],
        compiler_params=params(16),
        name="join",
    )(*parts)


def tokens_kernel(mine_ref, other_ref, rows_ref, columns_ref):
    @pl.when(pl.program_id(1) == 0)
    def _():
        rows_ref[0] = mine_ref[0, 0]
        columns_ref[0] = mine_ref[0, 0].T

    @pl.when(pl.program_id(1) == 1)
    def _():
        rows_ref[0] = other_ref[0, 0]
        columns_ref[0] = other_ref[0, 0].T


def gather_tokens(*pairs):
    mine = join(*pairs)
    other = flip(mine, "c")
    _, _, rows, depth = mine.shape
    block = (1, 1, rows, depth)
    return pl.pallas_call(
        tokens_kernel,
        grid=(2, 2, 4),
        in_specs=[
            pl.BlockSpec(block, lambda w, c, z: (jnp.where(c == 0, z, 3), w, 0, 0)),
            pl.BlockSpec(block, lambda w, c, z: (jnp.where(c == 1, z, 0), w, 0, 0)),
        ],
        out_specs=[
            pl.BlockSpec((1, rows, depth), lambda w, c, z: (w, 4 * c + z, 0)),
            pl.BlockSpec((1, depth, rows), lambda w, c, z: (w, 0, 4 * c + z)),
        ],
        out_shape=[like((2, 8 * rows, depth)), like((2, depth, 8 * rows))],
        compiler_params=params(12),
        cost_estimate=cost(0, 8 * mine.size * 2),
        name="tokens",
    )(mine, other)


def split(rows):
    high = rows.astype(BF16)
    return high, (rows - high.astype(F32)).astype(BF16)


def whole(rows):
    count = rows.shape[0] // 2
    return rows[:count].astype(F32) + rows[count:].astype(F32)


GROUPS = ((0, 4), (4, 4), (8, 4), (12, 2), (14, 2))


def place_of(first_bits, second_bits):
    return (0, 4, 12, 8)[first_bits] + second_bits


def mlp_kernel(
    coords,
    pair_hbm,
    pair_t_hbm,
    weights_hbm,
    bias_ref,
    gain_ref,
    shift_ref,
    cot_ref,
    head_sums_ref,
    head_bias_ref,
    hidden_hbm,
    *refs,
):
    up_outs, down_outs = refs[:5], refs[5:10]
    (
        pair_ref,
        pair_t_ref,
        up_ref,
        down_ref,
        hidden_ref,
        up_blocks,
        down_blocks,
        staged_ref,
        bias_sums_ref,
        rows_ref,
        turned_ref,
        product_ref,
        level_ref,
        load_sems,
        store_sems,
    ) = refs[10:]
    x, y = coords[1], coords[2]
    tiles, depth, tile = up_ref.shape
    hidden, half = tiles * tile, pair_ref.shape[1] // 2
    block = down_blocks.shape[1]
    start = weights_hbm.shape[1] - 2 * hidden
    slope = 0.7978845608028654

    def load_weights(j, which):
        lanes = pl.ds(pl.multiple_of(start + which * hidden + j * tile, tile), tile)
        target = (up_ref, down_ref)[which].at[j]
        return pltpu.make_async_copy(weights_hbm.at[:, lanes], target, load_sems.at[2 * j + which])

    def load_tokens(i):
        some = pl.ds(i * half, half)
        return pltpu.make_async_copy(
            pair_hbm.at[:, some, :], pair_ref.at[:, some, :], load_sems.at[2 * tiles + i]
        )

    load_features = [
        pltpu.make_async_copy(pair_t_hbm.at[i], pair_t_ref.at[i], load_sems.at[2 * tiles + 2 + i])
        for i in range(2)
    ]
    store_hidden = pltpu.make_async_copy(hidden_ref, hidden_hbm, store_sems.at[tiles, 0])

    def store_blocks(j):
        lanes = pl.ds(pl.multiple_of(j * tile, tile), tile)
        some = pl.ds(0, block)
        copies = []
        for blocks, outs in ((up_blocks, up_outs), (down_blocks, down_outs)):
            for (first, count), out in zip(GROUPS, outs):
                source = blocks.at[pl.ds(first, count), some, lanes]
                sem = store_sems.at[j, len(copies)]
                copies.append(pltpu.make_async_copy(source, out.at[:, some, lanes], sem))
        return copies

    load_tokens(0).start()
    for j in range(tiles):
        for which in range(2):
            load_weights(j, which).start()
        if j == 0:
            load_tokens(1).start()
    for load in load_features:
        load.start()

    def units(i):
        some = pl.ds(i * half, half)
        load_tokens(i).wait()

        def one_tile(j, carry):
            if i == 0:
                load_weights(j, 0).wait()
                load_weights(j, 1).wait()
            lanes = pl.ds(pl.multiple_of(j * tile, tile), tile)
            up = jnp.dot(pair_ref[0, some, :], up_ref[j], preferred_element_type=F32) + bias_ref[:, lanes]
            square = up * up
            wave = jnp.tanh(up * (slope + (slope * 0.044715) * square))
            gate = 0.5 + 0.5 * wave
            hidden_ref[1, some, lanes] = (up * gate).astype(BF16)
            rise = gate + up * (1.0 - wave * wave) * (0.5 * slope + (1.5 * slope * 0.044715) * square)
            grad = jnp.dot(pair_ref[1, some, :], down_ref[j], preferred_element_type=F32) * rise
            low = grad.astype(BF16)
            hidden_ref[0, some, lanes] = low
            sums = jnp.sum(low.astype(F32), axis=0, keepdims=True)
            bias_sums_ref[:, lanes] = sums if i == 0 else bias_sums_ref[:, lanes] + sums
            return carry

        lax.fori_loop(0, tiles, one_tile, 0)

    units(0)
    units(1)
    store_hidden.start()
    for load in load_features:
        load.wait()
    product_ref[...] = jnp.zeros_like(product_ref)
    level_ref[...] = jnp.zeros_like(level_ref)

    def one_tile(j, carry):
        lanes = pl.ds(pl.multiple_of(j * tile, tile), tile)
        product = jnp.dot(pair_t_ref[0], hidden_ref[0, :, lanes], preferred_element_type=F32)
        staged_ref[0] = product.astype(BF16).reshape(staged_ref.shape[1:])
        weights = up_ref[j].astype(F32)
        product_ref[...] += lane_sums(weights * product)
        level_ref[...] += lane_sums(weights * bias_sums_ref[:, lanes])
        product = jnp.dot(pair_t_ref[1], hidden_ref[1, :, lanes], preferred_element_type=F32)
        staged_ref[1] = product.astype(BF16).reshape(staged_ref.shape[1:])
        for x_bits in range(4):
            for y_bits in range(4):
                chip = (x ^ x_bits) * 4 + (y ^ y_bits)
                up_blocks[place_of(y_bits, x_bits), :block, lanes] = staged_ref[0, chip]
                down_blocks[place_of(x_bits, y_bits), :, lanes] = staged_ref[1, chip]
        for copy in store_blocks(j):
            copy.start()
        return carry

    lax.fori_loop(0, tiles, one_tile, 0)

    level = head_sums_ref[0:1, :] + across(level_ref[...])
    product = head_sums_ref[1:2, :] + across(product_ref[...])
    turn(turned_ref, jnp.concatenate([product, level], axis=0), True)
    level = turned_ref[1:2, :]
    by_gain = (turned_ref[0:1, :] - shift_ref[...] * level) / gain_ref[...]
    for i, row in enumerate((by_gain, level, cot_ref[...])):
        rows_ref[2 * i : 2 * i + 1, :] = row[:, :hidden]
        rows_ref[2 * i + 1 : 2 * i + 2, :] = row[:, hidden:]
    rows_ref[6:7, :] = bias_sums_ref[...]
    rows_ref[7:8, :] = head_bias_ref[...]
    high, low = split(rows_ref[...])
    vectors = jnp.concatenate([high.astype(F32), low.astype(F32)], axis=0).astype(BF16)
    for i in range(16):
        up_blocks[i, block:, :] = vectors
    copies = []
    for (first, count), out in zip(GROUPS, up_outs):
        source = up_blocks.at[pl.ds(first, count), pl.ds(block, 16), :]
        sem = store_sems.at[tiles, 1 + len(copies)]
        copies.append(pltpu.make_async_copy(source, out.at[:, pl.ds(block, 16), :], sem))
        copies[-1].start()
    store_hidden.wait()
    for j in range(tiles):
        copies += store_blocks(j)
    for copy in copies:
        copy.wait()


def mlp(coords, pair, pair_t, weights, bias, gain, shift, cot_sums, head_sums, head_bias):
    _, rows, depth = pair.shape
    hidden = bias.shape[0]
    tiles, block = 4, depth // 16
    tile = hidden // tiles
    ups = [like((count, block + 16, hidden)) for _, count in GROUPS]
    downs = [like((count, block, hidden)) for _, count in GROUPS]
    outs = pl.pallas_call(
        mlp_kernel,
        in_specs=[SCALARS] + [ANY] * 3 + [WHOLE] * 6,
        out_specs=[ANY] * 11,
        out_shape=[like((2, rows, hidden)), *ups, *downs],
        scratch_shapes=[
            pltpu.VMEM((2, rows, depth), BF16),
            pltpu.VMEM((2, depth, rows), BF16),
            pltpu.VMEM((tiles, depth, tile), BF16),
            pltpu.VMEM((tiles, depth, tile), BF16),
            pltpu.VMEM((2, rows, hidden), BF16),
            pltpu.VMEM((16, block + 16, hidden), BF16),
            pltpu.VMEM((16, block, hidden), BF16),
            pltpu.VMEM((2, 16, block, tile), BF16),
            pltpu.VMEM((1, hidden), F32),
            pltpu.VMEM((8, hidden), F32),
            pltpu.VMEM((2, depth), F32),
            pltpu.VMEM((depth, LANES), F32),
            pltpu.VMEM((depth, LANES), F32),
            pltpu.SemaphoreType.DMA((2 * tiles + 4,)),
            pltpu.SemaphoreType.DMA((tiles + 1, 10)),
        ],
        compiler_params=params(60),
        cost_estimate=cost(8 * rows * depth * hidden, 40 * MIB),
        name="mlp",
    )(
        coords,
        pair,
        pair_t,
        weights,
        bias.reshape(1, -1),
        gain.reshape(1, -1),
        shift.reshape(1, -1),
        cot_sums,
        head_sums,
        head_bias,
    )
    return outs[0], outs[1:6], outs[6:]


def add_blocks(parts, target, vectors):
    end = parts[0].shape[0] - 16 if vectors else parts[0].shape[0]
    data = parts[0][:end].astype(F32)
    for part in parts[1:]:
        data = data + part[:end].astype(F32)
    target[:end, :] = data.astype(target.dtype)
    if vectors:
        rows = whole(parts[0][end:])
        for part in parts[1:]:
            rows = rows + whole(part[end:])
        if target.dtype == F32:
            target[end:, :] = rows
        else:
            high, low = split(rows)
            target[end:, :] = jnp.concatenate([high.astype(F32), low.astype(F32)], axis=0).astype(BF16)


def bump_kernel(*refs):
    for i in range(4):
        chunk, part, out = refs[2 * i], refs[2 * i + 1], refs[8 + i]
        for k in range(2):
            add_blocks([chunk[k], part[k]], out.at[k], i < 2)


def bump(*chunks):
    specs, arrays, outs = [], [], []
    for chunk, part, half in chunks:
        shape = part.shape
        spec = pl.BlockSpec(shape, lambda i, half=half: (half, 0, 0))
        specs += [spec, pl.BlockSpec(shape, lambda i: (0, 0, 0))]
        arrays += [chunk, part]
        outs.append(spec)
    return pl.pallas_call(
        bump_kernel,
        grid=(1,),
        in_specs=specs,
        out_specs=outs,
        out_shape=[like(chunk.shape) for chunk, _, _ in chunks],
        input_output_aliases={0: 0, 2: 1, 4: 2, 6: 3},
        compiler_params=params(24),
        name="bump",
    )(*arrays)


def near_kernel(coords, *refs):
    for side in range(2):
        own, one, three = refs[3 * side : 3 * side + 3]
        for i in range(4):
            target = refs[6 + i] if side == 0 else refs[10].at[coords[2] ^ i]
            add_blocks([own[i], one[i], three[i]], target, side == 0)


def near_sums(coords, *chunks):
    rows, columns = chunks[0].shape[1:]
    shapes = [like((rows - 8, columns), F32)] + [like((rows, columns))] * 3 + [like(chunks[3].shape)]
    outs = pl.pallas_call(
        near_kernel,
        in_specs=[SCALARS] + [WHOLE] * 6,
        out_specs=[WHOLE] * 5,
        out_shape=shapes,
        compiler_params=params(60),
        name="near",
    )(coords, *chunks)
    return outs[:4], outs[4]


def settle_kernel(sum_ref, out_ref):
    out_ref[...] = sum_ref[...]


def settle(summed):
    return pl.pallas_call(
        settle_kernel,
        in_specs=[WHOLE],
        out_specs=WHOLE,
        out_shape=like(summed.shape),
        compiler_params=params(60),
        name="settle",
    )(summed)


def cut_summed_kernel(coords, down_ref, heads_ref, *outs):
    rows, wide = outs[0].shape[0], down_ref.shape[1]
    for bits in range(4):
        some = pl.ds(pl.multiple_of(slot_of(coords, bits) * rows, rows), rows)
        outs[bits][:, :wide] = down_ref[some, :]
        outs[bits][:, wide:] = heads_ref[some, :]


def cut_summed(coords, down, heads):
    rows = down.shape[0] // 4
    return pl.pallas_call(
        cut_summed_kernel,
        in_specs=[SCALARS] + [WHOLE] * 2,
        out_specs=[WHOLE] * 4,
        out_shape=[like((rows, down.shape[1] + heads.shape[1]))] * 4,
        compiler_params=params(16),
        name="cut_summed",
    )(coords, down, heads)


def cut_kernel(coords, *refs):
    up, summed, outs = refs[:4], refs[4:8], refs[8:]
    rows, hidden = outs[0].shape[0], up[0].shape[1]
    block = 4 * rows
    vectors = up[0][block:, :]
    for other in up[1:]:
        vectors = vectors + whole(other[block:, :])
    high, low = split(vectors)
    vectors = jnp.concatenate([high.astype(F32), low.astype(F32)], axis=0).astype(BF16)
    for bits in range(4):
        some = pl.ds(pl.multiple_of(slot_of(coords, bits) * rows, rows), rows)
        out = outs[bits]
        total = up[0][some, :]
        for other in up[1:]:
            total = total + other[some, :].astype(F32)
        out[:, :hidden] = total.astype(BF16)
        end = hidden + summed[bits].shape[1]
        out[:, hidden:end] = summed[bits][...]
        out[:16, end:] = vectors[:, : hidden // 2]
        out[16:, end:] = vectors[:, hidden // 2 :]


def cut(coords, up, summed):
    rows, hidden = summed[0].shape[0], up[0].shape[1]
    columns = hidden + summed[0].shape[1] + hidden // 2
    return pl.pallas_call(
        cut_kernel,
        in_specs=[SCALARS] + [WHOLE] * 8,
        out_specs=[WHOLE] * 4,
        out_shape=[like((rows, columns))] * 4,
        compiler_params=params(16),
        name="cut",
    )(coords, *up, *summed)


def combine_kernel(hidden_ref, right_ref, weights_ref, mine_ref, theirs_ref):
    contract = (((1,), (1,)), ((), ()))
    hidden, columns = hidden_ref.shape[2], right_ref.shape[1]
    inner = columns * 3 // 4
    half = mine_ref.shape[1]

    def product(left, start):
        weights = weights_ref[:, start : start + left.shape[1]]
        return lax.dot_general(left, weights, contract, preferred_element_type=F32)

    total = product(hidden_ref[0], columns) + product(right_ref[:, :inner], 0)
    mine_ref[0] = total[:half].astype(BF16)
    theirs_ref[0] = total[half:].astype(BF16)
    total = product(hidden_ref[1], columns + hidden) + product(right_ref[:, inner:], inner)
    mine_ref[1] = total[:half].astype(BF16)
    theirs_ref[1] = total[half:].astype(BF16)


def combine(hidden_pair, right, weights):
    _, rows, hidden = hidden_pair.shape
    depth, columns = weights.shape
    tile = depth // 4
    block = pl.BlockSpec((2, rows // 2, tile), lambda i: (0, 0, i))
    return pl.pallas_call(
        combine_kernel,
        grid=(4,),
        in_specs=[WHOLE, WHOLE, pl.BlockSpec((tile, columns), lambda i: (i, 0))],
        out_specs=[block] * 2,
        out_shape=[like((2, rows // 2, depth))] * 2,
        compiler_params=params(40),
        cost_estimate=cost(2 * rows * depth * columns, 16 * MIB),
        name="combine",
    )(hidden_pair, right, weights)


def exchange(parts):
    return [parts[0], flip(parts[1], "c"), flip(parts[2], "zl"), flip(parts[3], "zl", "c")]


def unpack_kernel(coords, *refs):
    parts, (up_ref, down_ref, qkv_ref, out_ref, rows_ref, up_sums_ref, qkv_sums_ref) = refs[:4], refs[4:]
    hidden, width = up_ref.shape[1] // 4, out_ref.shape[1] // 4
    for bits in range(4):
        slot, part = slot_of(coords, bits), parts[bits]
        wide = pl.ds(pl.multiple_of(slot * hidden, hidden), hidden)
        narrow = pl.ds(pl.multiple_of(slot * width, width), width)
        up_ref[:, wide] = part[:, :hidden].astype(F32)
        down_ref[:, wide] = part[:, hidden : 2 * hidden].astype(F32)
        start = 2 * hidden
        for kind in range(3):
            qkv_ref[kind, :, narrow] = part[:, start + kind * width : start + (kind + 1) * width].astype(F32)
        out_ref[:, narrow] = part[:, start + 3 * width : start + 4 * width].astype(F32)
        start += 4 * width
        vectors = jnp.concatenate([whole(part[:16, start:]), whole(part[16:, start:])], axis=1)
        rows_ref[...] = vectors if bits == 0 else rows_ref[...] + vectors
        up_sums_ref[:, wide] = vectors[6:7, :]
        for kind in range(3):
            qkv_sums_ref[kind : kind + 1, narrow] = vectors[7:8, kind * width : (kind + 1) * width]


def unpack(coords, parts, hidden, width):
    rows = parts[0].shape[0]
    wide, narrow = (rows, 4 * hidden), (rows, 4 * width)
    shapes = [wide, wide, (3,) + narrow, narrow, (8, hidden), (1, 4 * hidden), (3, 4 * width)]
    return pl.pallas_call(
        unpack_kernel,
        in_specs=[SCALARS] + [WHOLE] * 4,
        out_specs=[WHOLE] * 7,
        out_shape=[like(shape, F32) for shape in shapes],
        compiler_params=params(16),
        name="unpack",
    )(coords, *parts)


def turn(dest, value, back):
    block = value.shape[1] // 32
    for chip in range(16):
        for zl in range(2):
            natural, inside = (zl * 16 + chip) * block, (chip * 2 + zl) * block
            source, target = (inside, natural) if back else (natural, inside)
            dest[:, target : target + block] = value[:, source : source + block].astype(dest.dtype)


def standardize(tokens):
    rows = tokens.astype(F32)
    centered = rows - jnp.mean(rows, axis=1, keepdims=True)
    scale = lax.rsqrt(jnp.mean(centered * centered, axis=1, keepdims=True) + EPSILON)
    return rows, centered * scale, scale


def enter_kernel(tokens_ref, cot_ref, gain_ref, bias_ref, pair_ref, sums_ref):
    _, standard, _ = standardize(tokens_ref[...])
    turn(pair_ref.at[0], (standard * gain_ref[...] + bias_ref[...]).astype(BF16), False)
    turn(pair_ref.at[1], cot_ref[...], False)
    sums_ref[...] = jnp.sum(cot_ref[...].astype(F32), axis=0, keepdims=True)


def enter(tokens, cotangent, gain, bias):
    return pl.pallas_call(
        enter_kernel,
        in_specs=[WHOLE] * 4,
        out_specs=[WHOLE] * 2,
        out_shape=[like((2,) + tokens.shape), like((1, tokens.shape[1]), F32)],
        compiler_params=params(16),
        name="enter",
    )(tokens, cotangent, gain.reshape(1, -1), bias.reshape(1, -1))


def leave_kernel(tokens_ref, cot_ref, gain_ref, bias_ref, *refs):
    mixed_ref, grad_ref, branch_ref, normed_ref = refs[-4:]
    for which, target in ((0, normed_ref), (1, branch_ref)):
        total = refs[0][which]
        for part in refs[1:4]:
            total = total + part[which].astype(F32)
        turn(target, total, True)
    rows, standard, scale = standardize(tokens_ref[...])
    mixed_ref[...] = (rows + branch_ref[...] + bias_ref[...]).astype(BF16)
    grad = normed_ref[...] * gain_ref[...]
    level = jnp.mean(grad, axis=1, keepdims=True)
    slope = jnp.mean(grad * standard, axis=1, keepdims=True)
    grad_ref[...] = cot_ref[...].astype(F32) + scale * (grad - level - standard * slope)


def leave(tokens, cotangent, gain, bias, sums):
    shape = tokens.shape
    return pl.pallas_call(
        leave_kernel,
        in_specs=[WHOLE] * 8,
        out_specs=[WHOLE] * 2,
        out_shape=[like(shape), like(shape, F32)],
        scratch_shapes=[pltpu.VMEM(shape, F32)] * 2,
        compiler_params=params(24),
        cost_estimate=cost(5 * GIGA, 4 * MIB),
        name="leave",
    )(tokens, cotangent, gain.reshape(1, -1), bias.reshape(1, -1), *sums)


def scatter_plane(grads):
    return lax.psum_scatter(grads, PLANE, scatter_dimension=0, tiled=True)


def per_device(
    tokens,
    layernorm_gain,
    layernorm_bias,
    w_qkv,
    b_qkv,
    w_out,
    b_out,
    w_up,
    b_up,
    w_down,
    b_down,
    segments,
    cotangent,
):
    depth = tokens.shape[1]
    length = segments.shape[0]
    half_rows = tokens.shape[0]
    width = w_out.shape[0] // 4
    hidden = w_down.shape[0] // 4
    rows = w_up.shape[0]
    coords = jnp.stack([lax.axis_index(axis) for axis in AXES]).astype(jnp.int32)
    place_here = coords[0] * 2 + coords[3]
    this_half = coords[4]

    parts = exchange(pack(coords, w_up, w_down.T, w_qkv.transpose(1, 0, 2), w_out.T, segments))
    shard = order(coords, parts, 2 * hidden + 4 * width)
    weights = lax.all_gather(shard, PLANE, axis=0, tiled=True)

    pair, cot_sums = enter(tokens, cotangent, layernorm_gain, layernorm_bias)
    _, pair = lax.optimization_barrier((shard, pair))
    near, far, opposite = flip(pair, "zl"), flip(pair, "zl", "mp"), flip(pair, "mp")
    pair, pair_t = gather_tokens(pair, opposite, near, far)

    doc = jnp.stack([parts[k][0, -length:] for k in (0, 2, 1, 3)]).astype(jnp.int32)
    doc = doc.reshape(4, 2, half_rows)
    doc = jnp.where(this_half == 0, doc, doc[:, ::-1]).reshape(4, length)
    halves = jnp.stack([this_half, 1 - this_half]) * half_rows
    index = (halves[:, None] + jnp.arange(half_rows, dtype=jnp.int32)).reshape(1, length)
    index = jnp.broadcast_to(index, (4, length)).astype(jnp.int32)
    b_up_here = lax.dynamic_slice_in_dim(b_up, place_here * hidden, hidden)
    b_qkv_here = lax.dynamic_slice_in_dim(b_qkv, place_here * width, width, axis=1).reshape(-1)

    tables = rotary_tables(doc, index)

    pair, pair_t, tables = lax.optimization_barrier((pair, pair_t, tables))
    right, head_grads, head_bias, head_sums = heads(pair, pair_t, weights, b_qkv_here, tables, length)
    head_grads = scatter_plane(head_grads)

    right, pair, pair_t = lax.optimization_barrier((right, pair, pair_t))
    hidden_pair, up_blocks, down_blocks = mlp(
        coords,
        pair,
        pair_t,
        weights,
        b_up_here,
        layernorm_gain,
        layernorm_bias,
        cot_sums,
        head_sums,
        head_bias,
    )

    up_blocks, down_blocks, hidden_pair = lax.optimization_barrier((up_blocks, down_blocks, hidden_pair))
    up_own, up_one, up_three, up_low, up_high = up_blocks
    down_own, down_one, down_three, down_low, down_high = down_blocks
    low = [hop(up_low, "y", 1), hop(down_low, "x", 1)]
    high = [hop(up_high, "y", 3), hop(down_high, "x", 3)]
    mine, theirs = combine(hidden_pair, right, weights)
    low, high, mine, theirs = lax.optimization_barrier((low, high, mine, theirs))
    theirs = flip(theirs, "c")
    up_one, up_three, down_one, down_three = bump(
        (up_one, high[0], 1), (up_three, low[0], 0), (down_one, high[1], 1), (down_three, low[1], 0)
    )
    up_one, up_three = hop(up_one, "y", 1), hop(up_three, "y", 3)
    down_one, down_three = hop(down_one, "x", 1), hop(down_three, "x", 3)
    keep, sends = fold(mine, theirs)
    opposite = flip(sends[0], "mp")
    up_one, up_three, down_one, down_three, opposite, keep, near, far, head_grads = lax.optimization_barrier(
        (up_one, up_three, down_one, down_three, opposite, keep, sends[1], sends[2], settle(head_grads))
    )
    along_z = [opposite, flip(near, "zl"), flip(far, "zl", "mp")]
    up_sums, down_sums = near_sums(coords, up_own, up_one, up_three, down_own, down_one, down_three)
    up_sums = [up_sums[0]] + [hop(part, "x", bits) for part, bits in zip(up_sums[1:], (1, 2, 3))]
    down_sums = lax.psum_scatter(
        down_sums.reshape(-1, hidden), "y", scatter_dimension=0, tiled=True
    )
    up_sums, summed = lax.optimization_barrier((up_sums, cut_summed(coords, down_sums, head_grads)))
    parts = exchange(cut(coords, up_sums, summed))
    mixed, d_tokens = leave(
        tokens, cotangent, layernorm_gain, b_out + b_down, [keep] + along_z
    )
    mixed, d_tokens, *parts = lax.optimization_barrier((mixed, d_tokens, *parts))
    grad_up_w, grad_down_w, grad_qkv_w, grad_out_w, vectors, grad_b_up, grad_b_qkv = unpack(
        coords, parts, hidden, width
    )
    vectors = (vectors + flip(vectors, "mp"))[:6].reshape(3, depth)
    return (
        mixed,
        d_tokens,
        vectors[0],
        vectors[1],
        grad_qkv_w.transpose(1, 0, 2),
        grad_b_qkv,
        grad_out_w.T,
        vectors[2],
        grad_up_w,
        grad_b_up[0],
        grad_down_w.T,
        vectors[2],
    )


def solution(mesh):
    fine = Mesh(mesh.devices.reshape(SIZES), AXES)
    dp = ("zl", "x", "y", "c")
    in_specs = (
        P(AXES, None),
        P(),
        P(),
        P(dp, None, "mp"),
        P(None, "mp"),
        P("mp", dp),
        P(),
        P(dp, "mp"),
        P("mp"),
        P("mp", dp),
        P(),
        P(dp),
        P(AXES, None),
    )
    out_specs = (
        P(AXES, None),
        P(AXES, None),
        P(),
        P(),
        P(dp, None, "mp"),
        P(None, "mp"),
        P("mp", dp),
        P(),
        P(dp, "mp"),
        P("mp"),
        P("mp", dp),
        P(),
    )
    return jax.shard_map(
        per_device, mesh=fine, in_specs=in_specs, out_specs=out_specs, check_vma=False
    )
```

```python
import functools

import jax
import jax.numpy as jnp
from jax import lax
from jax.experimental import pallas as pl
from jax.experimental.pallas import tpu as pltpu
from jax.sharding import Mesh, PartitionSpec as P

HEAD_DIM = 64
ROT = 32
HALF = ROT // 2
LANES = 128
EPSILON = 1e-05

AXES = ("zl", "x", "y", "c", "mp")
SIZES = (2, 4, 4, 2, 2)
PLANE = ("x", "y")
PAIR = ("zl", "c")

BF16 = jnp.bfloat16
F32 = jnp.float32
MIB = 1024 * 1024
GIGA = 1000 * MIB
ANY = pl.BlockSpec(memory_space=pl.ANY)
WHOLE = pl.BlockSpec(memory_space=pltpu.VMEM)
SCALARS = pl.BlockSpec(memory_space=pltpu.SMEM)


def flip(value, *axes):
    count = 2 ** len(axes)
    return lax.ppermute(value, axes, [(i, count - 1 - i) for i in range(count)])


def hop(value, axis, bits):
    return lax.ppermute(value, axis, [(i, i ^ bits) for i in range(4)])


def fold_kernel(mine_ref, theirs_ref, keep_ref, *sends):
    rows = keep_ref.shape[1]
    for which in range(2):
        for i in range(4):
            block = slice(i * rows, (i + 1) * rows)
            total = mine_ref[which, block, :].astype(F32) + theirs_ref[which, block, :].astype(F32)
            if i == 0:
                keep_ref[which] = total.astype(BF16)
            else:
                sends[i - 1][which] = total.astype(BF16)


def fold(mine, theirs):
    _, rows, depth = mine.shape
    rows, tile = rows // 4, depth // 4
    keep, *sends = pl.pallas_call(
        fold_kernel,
        grid=(4,),
        in_specs=[pl.BlockSpec((2, 4 * rows, tile), lambda j: (0, 0, j))] * 2,
        out_specs=[pl.BlockSpec((2, rows, tile), lambda j: (0, 0, j))] * 4,
        out_shape=[like((2, rows, depth))] * 4,
        compiler_params=params(16),
        cost_estimate=cost(0, 26 * rows * depth),
        name="fold",
    )(mine, theirs)
    return keep, sends


def lane_sums(value):
    total = value[:, :LANES]
    for start in range(LANES, value.shape[1], LANES):
        total = total + value[:, start : start + LANES]
    return total


def across(columns):
    ones = jnp.ones((8, columns.shape[1]), F32)
    contract = (((1,), (1,)), ((), ()))
    return lax.dot_general(
        ones, columns, contract, precision=lax.Precision.HIGHEST, preferred_element_type=F32
    )[:1]


def heads_kernel(
    pair_hbm,
    pair_t_hbm,
    weights_hbm,
    bias_ref,
    trig_ref,
    segment_col,
    segment_row,
    index_col,
    index_row,
    right_hbm,
    grads_hbm,
    bias_sums_ref,
    sums_ref,
    pair_ref,
    pair_t_ref,
    weights_ref,
    right_ref,
    grads_ref,
    linear_ref,
    query_ref,
    key_ref,
    value_ref,
    grad_ref,
    grad_query_ref,
    grad_key_ref,
    attended_ref,
    product_ref,
    level_ref,
    sems,
):
    length, width = grad_ref.shape
    count, columns = segment_row.shape[0], weights_ref.shape[1]
    tile = grads_ref.shape[2]
    scale = HEAD_DIM ** (-0.5)

    def rows_of(i):
        return pl.ds(pl.multiple_of(i * length, length), length)

    def load_tokens(i):
        some = rows_of(i)
        return pltpu.make_async_copy(pair_hbm.at[:, some, :], pair_ref.at[:, some, :], sems.at[i])

    load_weights = pltpu.make_async_copy(
        weights_hbm.at[:, pl.ds(0, columns)], weights_ref, sems.at[count]
    )
    load_features = [
        pltpu.make_async_copy(pair_t_hbm.at[i], pair_t_ref.at[i], sems.at[count + 1 + i]) for i in range(2)
    ]
    store_right = pltpu.make_async_copy(right_ref, right_hbm, sems.at[count + 3])

    def store_grads(j):
        lanes = pl.ds(pl.multiple_of(j * tile, tile), tile)
        return pltpu.make_async_copy(grads_ref.at[j], grads_hbm.at[:, lanes], sems.at[count + 4 + j])

    load_weights.start()
    for i in range(count):
        load_tokens(i).start()
    for load in load_features:
        load.start()
    load_weights.wait()
    both = (((1,), (1,)), ((), ()))

    def one_sequence(i, carry):
        some = rows_of(i)
        load_tokens(i).wait()
        linear_ref[...] = (
            jnp.dot(pair_ref[0, some, :], weights_ref[:, : 3 * width], preferred_element_type=F32)
            + bias_ref[...]
        )
        grad_ref[...] = jnp.dot(
            pair_ref[1, some, :], weights_ref[:, 3 * width :], preferred_element_type=F32
        ).astype(BF16)
        trig = trig_ref[some, :]

        def rotated(value, sign):
            ahead = pltpu.roll(value, LANES - HALF, 1)
            behind = pltpu.roll(value, HALF, 1)
            turned = ahead * trig[:, LANES : 2 * LANES] + behind * trig[:, 2 * LANES :]
            return value * trig[:, :LANES] + turned * sign

        for start in range(0, width, LANES):
            lanes = slice(start, start + LANES)
            query_ref[:, lanes] = (rotated(linear_ref[:, lanes], 1.0) * scale).astype(BF16)
            keys = linear_ref[:, width + start : width + start + LANES]
            key_ref[:, lanes] = rotated(keys, 1.0).astype(BF16)
            values = linear_ref[:, 2 * width + start : 2 * width + start + LANES]
            value_ref[:, lanes] = values.astype(BF16)
        allowed = (segment_row[i] == segment_col[some, :]) & (index_row[i] >= index_col[some, :])
        value_t, key_t = value_ref[...].T, key_ref[...].T
        for start in range(0, width, HEAD_DIM):
            lanes = slice(start, start + HEAD_DIM)
            query, key, value = query_ref[:, lanes], key_ref[:, lanes], value_ref[:, lanes]
            grad = grad_ref[:, lanes]
            scores = lax.dot_general(key, query, both, preferred_element_type=F32)
            scores = jnp.where(allowed, scores, -1000000000.0)
            expo = jnp.exp(scores - jnp.max(scores, axis=0, keepdims=True))
            probs = expo * (1.0 / jnp.sum(expo, axis=0, keepdims=True))
            low_probs = probs.astype(BF16)
            attended_ref[lanes, :] = jnp.dot(value_t[lanes], low_probs, preferred_element_type=F32)
            grad_probs = lax.dot_general(value, grad, both, preferred_element_type=F32)
            grad_values = jnp.dot(low_probs, grad, preferred_element_type=F32)
            weighted = probs * grad_probs
            delta = jnp.sum(weighted, axis=0, keepdims=True)
            grad_scores = (weighted - probs * delta).astype(BF16)
            grad_queries = jnp.dot(key_t[lanes], grad_scores, preferred_element_type=F32)
            grad_query_ref[lanes, :] = grad_queries * scale
            grad_key_ref[:, lanes] = jnp.dot(grad_scores, query, preferred_element_type=F32)
            right_ref[some, 2 * width + start : 2 * width + start + HEAD_DIM] = grad_values.astype(BF16)
        right_ref[some, 3 * width :] = attended_ref[...].T.astype(BF16)
        linear_ref[:, :width] = grad_query_ref[...].T
        for start in range(0, width, LANES):
            lanes = slice(start, start + LANES)
            right_ref[some, lanes] = rotated(linear_ref[:, lanes], -1.0).astype(BF16)
            right_ref[some, width + start : width + start + LANES] = rotated(
                grad_key_ref[:, lanes], -1.0
            ).astype(BF16)
        return carry

    lax.fori_loop(0, count, one_sequence, 0)
    store_right.start()
    for load in load_features:
        load.wait()
    product_ref[...] = jnp.zeros_like(product_ref)
    level_ref[...] = jnp.zeros_like(level_ref)

    def one_tile(j, carry):
        lanes = pl.ds(pl.multiple_of(j * tile, tile), tile)
        right = right_ref[:, lanes]
        product = jnp.dot(pair_t_ref[j // 3], right, preferred_element_type=F32)
        grads_ref[j] = product.astype(BF16)
        store_grads(j).start()
        inner = jnp.where(j < 3, 1.0, 0.0)
        sums = jnp.sum(right.astype(F32), axis=0, keepdims=True) * inner
        bias_sums_ref[:, lanes] = sums
        weights = weights_ref[:, lanes].astype(F32)
        product_ref[...] += lane_sums(weights * product) * inner
        level_ref[...] += lane_sums(weights * sums)
        return carry

    lax.fori_loop(0, 4, one_tile, 0)
    sums_ref[0:1, :] = across(level_ref[...])
    sums_ref[1:2, :] = across(product_ref[...])
    store_right.wait()
    for j in range(4):
        store_grads(j).wait()


def heads(pair, pair_t, weights, bias, tables, length):
    _, rows, depth = pair.shape
    width = bias.shape[0] // 3
    columns, count = 4 * width, rows // length
    return pl.pallas_call(
        heads_kernel,
        in_specs=[ANY] * 3 + [WHOLE] * 6,
        out_specs=[ANY, ANY, WHOLE, WHOLE],
        out_shape=[
            like((rows, columns)),
            like((depth, columns)),
            like((1, columns), F32),
            like((2, depth), F32),
        ],
        scratch_shapes=[
            pltpu.VMEM((2, rows, depth), BF16),
            pltpu.VMEM((2, depth, rows), BF16),
            pltpu.VMEM((depth, columns), BF16),
            pltpu.VMEM((rows, columns), BF16),
            pltpu.VMEM((4, depth, width), BF16),
            pltpu.VMEM((length, 3 * width), F32),
        ]
        + [pltpu.VMEM((length, width), BF16)] * 4
        + [
            pltpu.VMEM((width, length), F32),
            pltpu.VMEM((length, width), F32),
            pltpu.VMEM((width, length), F32),
            pltpu.VMEM((depth, LANES), F32),
            pltpu.VMEM((depth, LANES), F32),
            pltpu.SemaphoreType.DMA((count + 8,)),
        ],
        compiler_params=params(60),
        cost_estimate=cost(30 * GIGA, 10 * MIB),
        name="heads",
    )(pair, pair_t, weights, bias.reshape(1, -1), *tables)


def tables_kernel(cos_ref, sin_ref, *refs):
    inputs, outputs = refs[:4], refs[5:]
    trig_ref = refs[4]
    cos, sin = cos_ref[...], sin_ref[...]
    trig_ref[...] = jnp.zeros_like(trig_ref)
    for start in range(0, LANES, HEAD_DIM):
        rest = (cos.shape[0], HEAD_DIM - ROT)
        trig_ref[:, start : start + HALF] = cos
        trig_ref[:, start + HALF : start + ROT] = cos
        trig_ref[:, start + ROT : start + HEAD_DIM] = jnp.ones(rest, F32)
        trig_ref[:, LANES + start : LANES + start + HALF] = -sin
        trig_ref[:, 2 * LANES + start + HALF : 2 * LANES + start + ROT] = sin
    for source, target in zip(inputs, outputs):
        target[...] = source[...]


def rotary_tables(doc, index):
    count, length = doc.shape
    rows = count * length
    same_doc = doc[:, :, None] == doc[:, None, :]
    doc_start = jnp.min(jnp.where(same_doc, index[:, None, :], length), axis=2)
    positions = (index - doc_start).astype(F32).reshape(-1)
    inv_freq = 10000.0 ** (-(jnp.arange(HALF, dtype=F32) * 2.0 / ROT))
    angles = positions[:, None] * inv_freq
    column, row = (rows, 1), (count, 1, length)
    shapes = [column, row, column, row]
    passed = [value.reshape(shape) for value, shape in zip((doc, doc, index, index), shapes)]
    return pl.pallas_call(
        tables_kernel,
        in_specs=[WHOLE] * 6,
        out_specs=[WHOLE] * 5,
        out_shape=[like((rows, 3 * LANES), F32)] + [like(shape, jnp.int32) for shape in shapes],
        compiler_params=params(16),
        name="tables",
    )(jnp.cos(angles), jnp.sin(angles), *passed)


def like(shape, dtype=BF16):
    return jax.ShapeDtypeStruct(shape, dtype)


def params(mib):
    return pltpu.CompilerParams(vmem_limit_bytes=mib * MIB)


def cost(flops, moved):
    return pl.CostEstimate(flops=flops, bytes_accessed=moved, transcendentals=0)


def slot_of(coords, bits):
    return (coords[0] * 2 + coords[3]) ^ bits


def pack_kernel(coords, up_ref, down_ref, qkv_ref, out_ref, segment_ref, *refs):
    parts, sems = refs[:4], refs[4]
    hidden, width = up_ref.shape[1] // 4, out_ref.shape[1] // 4
    copies = []

    def copy(source, target):
        copies.append(pltpu.make_async_copy(source, target, sems.at[len(copies)]))
        copies[-1].start()

    for bits in (1, 2, 3, 0):
        slot = slot_of(coords, bits)
        wide = pl.ds(pl.multiple_of(slot * hidden, hidden), hidden)
        narrow = pl.ds(pl.multiple_of(slot * width, width), width)
        part = parts[bits]
        for kind in range(3):
            copy(qkv_ref.at[kind, :, narrow], part.at[:, pl.ds(kind * width, width)])
        copy(out_ref.at[:, narrow], part.at[:, pl.ds(3 * width, width)])
        copy(up_ref.at[:, wide], part.at[:, pl.ds(4 * width, hidden)])
        copy(down_ref.at[:, wide], part.at[:, pl.ds(4 * width + hidden, hidden)])
    segments = segment_ref[...].astype(F32).astype(BF16)
    segments = jnp.broadcast_to(segments, (up_ref.shape[0], segments.shape[1]))
    for part in parts:
        part[:, 4 * width + 2 * hidden :] = segments
    for each in copies:
        each.wait()


def pack(coords, w_up, down_t, qkv_t, out_t, segments):
    rows, hidden, width = w_up.shape[0], w_up.shape[1] // 4, out_t.shape[1] // 4
    return pl.pallas_call(
        pack_kernel,
        in_specs=[SCALARS] + [ANY] * 4 + [WHOLE],
        out_specs=[WHOLE] * 4,
        out_shape=[like((rows, 2 * hidden + 4 * width + segments.shape[0]))] * 4,
        scratch_shapes=[pltpu.SemaphoreType.DMA((24,))],
        compiler_params=params(60),
        name="pack",
    )(coords, w_up, down_t, qkv_t, out_t, segments.reshape(1, -1))


def order_kernel(coords, *refs):
    parts, out = refs[:4], refs[4]
    for bits in range(4):
        out[coords[0] ^ (bits >> 1), coords[3] ^ (bits & 1)] = parts[bits][:, : out.shape[3]]


def order(coords, parts, columns):
    rows = parts[0].shape[0]
    out = pl.pallas_call(
        order_kernel,
        in_specs=[SCALARS] + [WHOLE] * 4,
        out_specs=WHOLE,
        out_shape=like((2, 2, rows, columns)),
        compiler_params=params(16),
        name="order",
    )(coords, *parts)
    return out.reshape(4 * rows, columns)


def join_kernel(*refs):
    parts, out, sem = refs[:-2], refs[-2], refs[-1]
    copies = []
    for i, part in enumerate(parts):
        copies.append(pltpu.make_async_copy(part, out.at[i], sem.at[i]))
        copies[-1].start()
    for copy in copies:
        copy.wait()


def join(*parts):
    return pl.pallas_call(
        join_kernel,
        in_specs=[ANY] * len(parts),
        out_specs=ANY,
        out_shape=like((len(parts),) + parts[0].shape),
        scratch_shapes=[pltpu.SemaphoreType.DMA((len(parts),))],
        compiler_params=params(16),
        name="join",
    )(*parts)


def tokens_kernel(mine_ref, other_ref, rows_ref, columns_ref):
    @pl.when(pl.program_id(1) == 0)
    def _():
        rows_ref[0] = mine_ref[0, 0]
        columns_ref[0] = mine_ref[0, 0].T

    @pl.when(pl.program_id(1) == 1)
    def _():
        rows_ref[0] = other_ref[0, 0]
        columns_ref[0] = other_ref[0, 0].T


def gather_tokens(*pairs):
    mine = join(*pairs)
    other = flip(mine, "c")
    _, _, rows, depth = mine.shape
    block = (1, 1, rows, depth)
    return pl.pallas_call(
        tokens_kernel,
        grid=(2, 2, 4),
        in_specs=[
            pl.BlockSpec(block, lambda w, c, z: (jnp.where(c == 0, z, 3), w, 0, 0)),
            pl.BlockSpec(block, lambda w, c, z: (jnp.where(c == 1, z, 0), w, 0, 0)),
        ],
        out_specs=[
            pl.BlockSpec((1, rows, depth), lambda w, c, z: (w, 4 * c + z, 0)),
            pl.BlockSpec((1, depth, rows), lambda w, c, z: (w, 0, 4 * c + z)),
        ],
        out_shape=[like((2, 8 * rows, depth)), like((2, depth, 8 * rows))],
        compiler_params=params(12),
        cost_estimate=cost(0, 8 * mine.size * 2),
        name="tokens",
    )(mine, other)


def split(rows):
    high = rows.astype(BF16)
    return high, (rows - high.astype(F32)).astype(BF16)


def whole(rows):
    count = rows.shape[0] // 2
    return rows[:count].astype(F32) + rows[count:].astype(F32)


GROUPS = ((0, 4), (4, 4), (8, 4), (12, 2), (14, 2))


def place_of(first_bits, second_bits):
    return (0, 4, 12, 8)[first_bits] + second_bits


def mlp_kernel(
    coords,
    pair_hbm,
    pair_t_hbm,
    weights_hbm,
    bias_ref,
    gain_ref,
    shift_ref,
    cot_ref,
    head_sums_ref,
    head_bias_ref,
    hidden_hbm,
    *refs,
):
    up_outs, down_outs = refs[:5], refs[5:10]
    (
        pair_ref,
        pair_t_ref,
        up_ref,
        down_ref,
        hidden_ref,
        up_blocks,
        down_blocks,
        staged_ref,
        bias_sums_ref,
        rows_ref,
        turned_ref,
        product_ref,
        level_ref,
        load_sems,
        store_sems,
    ) = refs[10:]
    x, y = coords[1], coords[2]
    tiles, depth, tile = up_ref.shape
    hidden, half = tiles * tile, pair_ref.shape[1] // 2
    block = down_blocks.shape[1]
    start = weights_hbm.shape[1] - 2 * hidden
    slope = 0.7978845608028654

    def load_weights(j, which):
        lanes = pl.ds(pl.multiple_of(start + which * hidden + j * tile, tile), tile)
        target = (up_ref, down_ref)[which].at[j]
        return pltpu.make_async_copy(weights_hbm.at[:, lanes], target, load_sems.at[2 * j + which])

    def load_tokens(i):
        some = pl.ds(i * half, half)
        return pltpu.make_async_copy(
            pair_hbm.at[:, some, :], pair_ref.at[:, some, :], load_sems.at[2 * tiles + i]
        )

    load_features = [
        pltpu.make_async_copy(pair_t_hbm.at[i], pair_t_ref.at[i], load_sems.at[2 * tiles + 2 + i])
        for i in range(2)
    ]
    store_hidden = pltpu.make_async_copy(hidden_ref, hidden_hbm, store_sems.at[tiles, 0])

    def store_blocks(j):
        lanes = pl.ds(pl.multiple_of(j * tile, tile), tile)
        some = pl.ds(0, block)
        copies = []
        for blocks, outs in ((up_blocks, up_outs), (down_blocks, down_outs)):
            for (first, count), out in zip(GROUPS, outs):
                source = blocks.at[pl.ds(first, count), some, lanes]
                sem = store_sems.at[j, len(copies)]
                copies.append(pltpu.make_async_copy(source, out.at[:, some, lanes], sem))
        return copies

    load_tokens(0).start()
    for j in range(tiles):
        for which in range(2):
            load_weights(j, which).start()
        if j == 0:
            load_tokens(1).start()
    for load in load_features:
        load.start()

    def units(i):
        some = pl.ds(i * half, half)
        load_tokens(i).wait()

        def one_tile(j, carry):
            if i == 0:
                load_weights(j, 0).wait()
                load_weights(j, 1).wait()
            lanes = pl.ds(pl.multiple_of(j * tile, tile), tile)
            up = jnp.dot(pair_ref[0, some, :], up_ref[j], preferred_element_type=F32) + bias_ref[:, lanes]
            square = up * up
            wave = jnp.tanh(up * (slope + (slope * 0.044715) * square))
            gate = 0.5 + 0.5 * wave
            hidden_ref[1, some, lanes] = (up * gate).astype(BF16)
            rise = gate + up * (1.0 - wave * wave) * (0.5 * slope + (1.5 * slope * 0.044715) * square)
            grad = jnp.dot(pair_ref[1, some, :], down_ref[j], preferred_element_type=F32) * rise
            low = grad.astype(BF16)
            hidden_ref[0, some, lanes] = low
            sums = jnp.sum(low.astype(F32), axis=0, keepdims=True)
            bias_sums_ref[:, lanes] = sums if i == 0 else bias_sums_ref[:, lanes] + sums
            return carry

        lax.fori_loop(0, tiles, one_tile, 0)

    units(0)
    units(1)
    store_hidden.start()
    for load in load_features:
        load.wait()
    product_ref[...] = jnp.zeros_like(product_ref)
    level_ref[...] = jnp.zeros_like(level_ref)

    def one_tile(j, carry):
        lanes = pl.ds(pl.multiple_of(j * tile, tile), tile)
        product = jnp.dot(pair_t_ref[0], hidden_ref[0, :, lanes], preferred_element_type=F32)
        staged_ref[0] = product.astype(BF16).reshape(staged_ref.shape[1:])
        weights = up_ref[j].astype(F32)
        product_ref[...] += lane_sums(weights * product)
        level_ref[...] += lane_sums(weights * bias_sums_ref[:, lanes])
        product = jnp.dot(pair_t_ref[1], hidden_ref[1, :, lanes], preferred_element_type=F32)
        staged_ref[1] = product.astype(BF16).reshape(staged_ref.shape[1:])
        for x_bits in range(4):
            for y_bits in range(4):
                chip = (x ^ x_bits) * 4 + (y ^ y_bits)
                up_blocks[place_of(y_bits, x_bits), :block, lanes] = staged_ref[0, chip]
                down_blocks[place_of(x_bits, y_bits), :, lanes] = staged_ref[1, chip]
        for copy in store_blocks(j):
            copy.start()
        return carry

    lax.fori_loop(0, tiles, one_tile, 0)

    level = head_sums_ref[0:1, :] + across(level_ref[...])
    product = head_sums_ref[1:2, :] + across(product_ref[...])
    turn(turned_ref, jnp.concatenate([product, level], axis=0), True)
    level = turned_ref[1:2, :]
    by_gain = (turned_ref[0:1, :] - shift_ref[...] * level) / gain_ref[...]
    for i, row in enumerate((by_gain, level, cot_ref[...])):
        rows_ref[2 * i : 2 * i + 1, :] = row[:, :hidden]
        rows_ref[2 * i + 1 : 2 * i + 2, :] = row[:, hidden:]
    rows_ref[6:7, :] = bias_sums_ref[...]
    rows_ref[7:8, :] = head_bias_ref[...]
    high, low = split(rows_ref[...])
    vectors = jnp.concatenate([high.astype(F32), low.astype(F32)], axis=0).astype(BF16)
    for i in range(16):
        up_blocks[i, block:, :] = vectors
    copies = []
    for (first, count), out in zip(GROUPS, up_outs):
        source = up_blocks.at[pl.ds(first, count), pl.ds(block, 16), :]
        sem = store_sems.at[tiles, 1 + len(copies)]
        copies.append(pltpu.make_async_copy(source, out.at[:, pl.ds(block, 16), :], sem))
        copies[-1].start()
    store_hidden.wait()
    for j in range(tiles):
        copies += store_blocks(j)
    for copy in copies:
        copy.wait()


def mlp(coords, pair, pair_t, weights, bias, gain, shift, cot_sums, head_sums, head_bias):
    _, rows, depth = pair.shape
    hidden = bias.shape[0]
    tiles, block = 4, depth // 16
    tile = hidden // tiles
    ups = [like((count, block + 16, hidden)) for _, count in GROUPS]
    downs = [like((count, block, hidden)) for _, count in GROUPS]
    outs = pl.pallas_call(
        mlp_kernel,
        in_specs=[SCALARS] + [ANY] * 3 + [WHOLE] * 6,
        out_specs=[ANY] * 11,
        out_shape=[like((2, rows, hidden)), *ups, *downs],
        scratch_shapes=[
            pltpu.VMEM((2, rows, depth), BF16),
            pltpu.VMEM((2, depth, rows), BF16),
            pltpu.VMEM((tiles, depth, tile), BF16),
            pltpu.VMEM((tiles, depth, tile), BF16),
            pltpu.VMEM((2, rows, hidden), BF16),
            pltpu.VMEM((16, block + 16, hidden), BF16),
            pltpu.VMEM((16, block, hidden), BF16),
            pltpu.VMEM((2, 16, block, tile), BF16),
            pltpu.VMEM((1, hidden), F32),
            pltpu.VMEM((8, hidden), F32),
            pltpu.VMEM((2, depth), F32),
            pltpu.VMEM((depth, LANES), F32),
            pltpu.VMEM((depth, LANES), F32),
            pltpu.SemaphoreType.DMA((2 * tiles + 4,)),
            pltpu.SemaphoreType.DMA((tiles + 1, 10)),
        ],
        compiler_params=params(60),
        cost_estimate=cost(8 * rows * depth * hidden, 40 * MIB),
        name="mlp",
    )(
        coords,
        pair,
        pair_t,
        weights,
        bias.reshape(1, -1),
        gain.reshape(1, -1),
        shift.reshape(1, -1),
        cot_sums,
        head_sums,
        head_bias,
    )
    return outs[0], outs[1:6], outs[6:]


def add_blocks(parts, target, vectors):
    end = parts[0].shape[0] - 16 if vectors else parts[0].shape[0]
    data = parts[0][:end].astype(F32)
    for part in parts[1:]:
        data = data + part[:end].astype(F32)
    target[:end, :] = data.astype(target.dtype)
    if vectors:
        rows = whole(parts[0][end:])
        for part in parts[1:]:
            rows = rows + whole(part[end:])
        if target.dtype == F32:
            target[end:, :] = rows
        else:
            high, low = split(rows)
            target[end:, :] = jnp.concatenate([high.astype(F32), low.astype(F32)], axis=0).astype(BF16)


def bump_kernel(*refs):
    for i in range(4):
        chunk, part, out = refs[2 * i], refs[2 * i + 1], refs[8 + i]
        for k in range(2):
            add_blocks([chunk[k], part[k]], out.at[k], i < 2)


def bump(*chunks):
    specs, arrays, outs = [], [], []
    for chunk, part, half in chunks:
        shape = part.shape
        spec = pl.BlockSpec(shape, lambda i, half=half: (half, 0, 0))
        specs += [spec, pl.BlockSpec(shape, lambda i: (0, 0, 0))]
        arrays += [chunk, part]
        outs.append(spec)
    return pl.pallas_call(
        bump_kernel,
        grid=(1,),
        in_specs=specs,
        out_specs=outs,
        out_shape=[like(chunk.shape) for chunk, _, _ in chunks],
        input_output_aliases={0: 0, 2: 1, 4: 2, 6: 3},
        compiler_params=params(24),
        name="bump",
    )(*arrays)


def near_up_kernel(own, one, three, *outs):
    for i in range(4):
        add_blocks([own[i], one[i], three[i]], outs[i], True)


def near_up(own, one, three):
    rows, columns = own.shape[1:]
    return pl.pallas_call(
        near_up_kernel,
        in_specs=[WHOLE] * 3,
        out_specs=[WHOLE] * 4,
        out_shape=[like((rows - 8, columns), F32)] + [like((rows, columns))] * 3,
        compiler_params=params(60),
        name="near_up",
    )(own, one, three)


def near_down_kernel(coords, own, one, three, out):
    for i in range(4):
        add_blocks([own[i], one[i], three[i]], out.at[coords[2] ^ i], False)


def near_down(coords, own, one, three):
    return pl.pallas_call(
        near_down_kernel,
        in_specs=[SCALARS] + [WHOLE] * 3,
        out_specs=WHOLE,
        out_shape=like(own.shape),
        compiler_params=params(60),
        name="near_down",
    )(coords, own, one, three)


def settle_kernel(sum_ref, out_ref):
    out_ref[...] = sum_ref[...]


def settle(summed):
    return pl.pallas_call(
        settle_kernel,
        in_specs=[WHOLE],
        out_specs=WHOLE,
        out_shape=like(summed.shape),
        compiler_params=params(60),
        name="settle",
    )(summed)


def cut_summed_kernel(coords, down_ref, heads_ref, *outs):
    rows, wide = outs[0].shape[0], down_ref.shape[1]
    for bits in range(4):
        some = pl.ds(pl.multiple_of(slot_of(coords, bits) * rows, rows), rows)
        outs[bits][:, :wide] = down_ref[some, :]
        outs[bits][:, wide:] = heads_ref[some, :]


def cut_summed(coords, down, heads):
    rows = down.shape[0] // 4
    return pl.pallas_call(
        cut_summed_kernel,
        in_specs=[SCALARS] + [WHOLE] * 2,
        out_specs=[WHOLE] * 4,
        out_shape=[like((rows, down.shape[1] + heads.shape[1]))] * 4,
        compiler_params=params(16),
        name="cut_summed",
    )(coords, down, heads)


def cut_kernel(coords, *refs):
    up, summed, outs = refs[:4], refs[4:8], refs[8:]
    rows, hidden = outs[0].shape[0], up[0].shape[1]
    block = 4 * rows
    vectors = up[0][block:, :]
    for other in up[1:]:
        vectors = vectors + whole(other[block:, :])
    high, low = split(vectors)
    vectors = jnp.concatenate([high.astype(F32), low.astype(F32)], axis=0).astype(BF16)
    for bits in range(4):
        some = pl.ds(pl.multiple_of(slot_of(coords, bits) * rows, rows), rows)
        out = outs[bits]
        total = up[0][some, :]
        for other in up[1:]:
            total = total + other[some, :].astype(F32)
        out[:, :hidden] = total.astype(BF16)
        end = hidden + summed[bits].shape[1]
        out[:, hidden:end] = summed[bits][...]
        out[:16, end:] = vectors[:, : hidden // 2]
        out[16:, end:] = vectors[:, hidden // 2 :]


def cut(coords, up, summed):
    rows, hidden = summed[0].shape[0], up[0].shape[1]
    columns = hidden + summed[0].shape[1] + hidden // 2
    return pl.pallas_call(
        cut_kernel,
        in_specs=[SCALARS] + [WHOLE] * 8,
        out_specs=[WHOLE] * 4,
        out_shape=[like((rows, columns))] * 4,
        compiler_params=params(16),
        name="cut",
    )(coords, *up, *summed)


def combine_kernel(hidden_ref, right_ref, weights_ref, mine_ref, theirs_ref):
    contract = (((1,), (1,)), ((), ()))
    hidden, columns = hidden_ref.shape[2], right_ref.shape[1]
    inner = columns * 3 // 4
    half = mine_ref.shape[1]

    def product(left, start):
        weights = weights_ref[:, start : start + left.shape[1]]
        return lax.dot_general(left, weights, contract, preferred_element_type=F32)

    total = product(hidden_ref[0], columns) + product(right_ref[:, :inner], 0)
    mine_ref[0] = total[:half].astype(BF16)
    theirs_ref[0] = total[half:].astype(BF16)
    total = product(hidden_ref[1], columns + hidden) + product(right_ref[:, inner:], inner)
    mine_ref[1] = total[:half].astype(BF16)
    theirs_ref[1] = total[half:].astype(BF16)


def combine(hidden_pair, right, weights):
    _, rows, hidden = hidden_pair.shape
    depth, columns = weights.shape
    tile = depth // 4
    block = pl.BlockSpec((2, rows // 2, tile), lambda i: (0, 0, i))
    return pl.pallas_call(
        combine_kernel,
        grid=(4,),
        in_specs=[WHOLE, WHOLE, pl.BlockSpec((tile, columns), lambda i: (i, 0))],
        out_specs=[block] * 2,
        out_shape=[like((2, rows // 2, depth))] * 2,
        compiler_params=params(40),
        cost_estimate=cost(2 * rows * depth * columns, 16 * MIB),
        name="combine",
    )(hidden_pair, right, weights)


def exchange(parts):
    return [parts[0], flip(parts[1], "c"), flip(parts[2], "zl"), flip(parts[3], "zl", "c")]


def unpack_kernel(coords, *refs):
    parts, (up_ref, down_ref, qkv_ref, out_ref) = refs[:4], refs[4:]
    hidden, width = up_ref.shape[1] // 4, out_ref.shape[1] // 4
    for bits in range(4):
        slot, part = slot_of(coords, bits), parts[bits]
        wide = pl.ds(pl.multiple_of(slot * hidden, hidden), hidden)
        narrow = pl.ds(pl.multiple_of(slot * width, width), width)
        up_ref[:, wide] = part[:, :hidden].astype(F32)
        down_ref[:, wide] = part[:, hidden : 2 * hidden].astype(F32)
        start = 2 * hidden
        for kind in range(3):
            qkv_ref[kind, :, narrow] = part[:, start + kind * width : start + (kind + 1) * width].astype(F32)
        out_ref[:, narrow] = part[:, start + 3 * width : start + 4 * width].astype(F32)


def unpack(coords, parts, hidden, width):
    rows = parts[0].shape[0]
    wide, narrow = (rows, 4 * hidden), (rows, 4 * width)
    return pl.pallas_call(
        unpack_kernel,
        in_specs=[SCALARS] + [WHOLE] * 4,
        out_specs=[WHOLE] * 4,
        out_shape=[like(shape, F32) for shape in (wide, wide, (3,) + narrow, narrow)],
        compiler_params=params(16),
        name="unpack",
    )(coords, *parts)


def vectors_kernel(coords, *refs):
    parts, (rows_ref, up_sums_ref, qkv_sums_ref) = refs[:4], refs[4:]
    hidden, width = up_sums_ref.shape[1] // 4, qkv_sums_ref.shape[1] // 4
    for bits in range(4):
        slot, part = slot_of(coords, bits), parts[bits]
        wide = pl.ds(pl.multiple_of(slot * hidden, hidden), hidden)
        narrow = pl.ds(pl.multiple_of(slot * width, width), width)
        vectors = jnp.concatenate([whole(part[:16, :]), whole(part[16:, :])], axis=1)
        rows_ref[...] = vectors if bits == 0 else rows_ref[...] + vectors
        up_sums_ref[:, wide] = vectors[6:7, :]
        for kind in range(3):
            qkv_sums_ref[kind : kind + 1, narrow] = vectors[7:8, kind * width : (kind + 1) * width]


def unpack_vectors(coords, parts, hidden, width):
    rows, columns = parts[0].shape
    half = hidden // 2
    last = columns // half - 1
    shapes = [(8, hidden), (1, 4 * hidden), (3, 4 * width)]
    return pl.pallas_call(
        vectors_kernel,
        grid=(1,),
        in_specs=[SCALARS] + [pl.BlockSpec((rows, half), lambda i: (0, last))] * 4,
        out_specs=[pl.BlockSpec(shape, lambda i: (0, 0)) for shape in shapes],
        out_shape=[like(shape, F32) for shape in shapes],
        compiler_params=params(16),
        name="vectors",
    )(coords, *parts)


def turn(dest, value, back):
    block = value.shape[1] // 32
    for chip in range(16):
        for zl in range(2):
            natural, inside = (zl * 16 + chip) * block, (chip * 2 + zl) * block
            source, target = (inside, natural) if back else (natural, inside)
            dest[:, target : target + block] = value[:, source : source + block].astype(dest.dtype)


def standardize(tokens):
    rows = tokens.astype(F32)
    centered = rows - jnp.mean(rows, axis=1, keepdims=True)
    scale = lax.rsqrt(jnp.mean(centered * centered, axis=1, keepdims=True) + EPSILON)
    return rows, centered * scale, scale


def enter_kernel(tokens_ref, cot_ref, gain_ref, bias_ref, pair_ref, sums_ref):
    _, standard, _ = standardize(tokens_ref[...])
    turn(pair_ref.at[0], (standard * gain_ref[...] + bias_ref[...]).astype(BF16), False)
    turn(pair_ref.at[1], cot_ref[...], False)
    sums_ref[...] = jnp.sum(cot_ref[...].astype(F32), axis=0, keepdims=True)


def enter(tokens, cotangent, gain, bias):
    return pl.pallas_call(
        enter_kernel,
        in_specs=[WHOLE] * 4,
        out_specs=[WHOLE] * 2,
        out_shape=[like((2,) + tokens.shape), like((1, tokens.shape[1]), F32)],
        compiler_params=params(16),
        name="enter",
    )(tokens, cotangent, gain.reshape(1, -1), bias.reshape(1, -1))


def leave_kernel(tokens_ref, cot_ref, gain_ref, bias_ref, *refs):
    mixed_ref, grad_ref, branch_ref, normed_ref = refs[-4:]
    for which, target in ((0, normed_ref), (1, branch_ref)):
        total = refs[0][which].astype(F32)
        for part in refs[1:4]:
            total = total + part[which].astype(F32)
        turn(target, total, True)
    rows, standard, scale = standardize(tokens_ref[...])
    mixed_ref[...] = (rows + branch_ref[...] + bias_ref[...]).astype(BF16)
    grad = normed_ref[...] * gain_ref[...]
    level = jnp.mean(grad, axis=1, keepdims=True)
    slope = jnp.mean(grad * standard, axis=1, keepdims=True)
    grad_ref[...] = cot_ref[...].astype(F32) + scale * (grad - level - standard * slope)


def leave(tokens, cotangent, gain, bias, sums):
    shape = tokens.shape
    return pl.pallas_call(
        leave_kernel,
        in_specs=[WHOLE] * 8,
        out_specs=[WHOLE] * 2,
        out_shape=[like(shape), like(shape, F32)],
        scratch_shapes=[pltpu.VMEM(shape, F32)] * 2,
        compiler_params=params(24),
        cost_estimate=cost(5 * GIGA, 4 * MIB),
        name="leave",
    )(tokens, cotangent, gain.reshape(1, -1), bias.reshape(1, -1), *sums)


def scatter_plane(grads):
    return lax.psum_scatter(grads, PLANE, scatter_dimension=0, tiled=True)


def per_device(
    tokens,
    layernorm_gain,
    layernorm_bias,
    w_qkv,
    b_qkv,
    w_out,
    b_out,
    w_up,
    b_up,
    w_down,
    b_down,
    segments,
    cotangent,
):
    depth = tokens.shape[1]
    length = segments.shape[0]
    half_rows = tokens.shape[0]
    width = w_out.shape[0] // 4
    hidden = w_down.shape[0] // 4
    rows = w_up.shape[0]
    coords = jnp.stack([lax.axis_index(axis) for axis in AXES]).astype(jnp.int32)
    place_here = coords[0] * 2 + coords[3]
    this_half = coords[4]

    parts = exchange(pack(coords, w_up, w_down.T, w_qkv.transpose(1, 0, 2), w_out.T, segments))
    shard = order(coords, parts, 2 * hidden + 4 * width)
    weights = lax.all_gather(shard, PLANE, axis=0, tiled=True)

    pair, cot_sums = enter(tokens, cotangent, layernorm_gain, layernorm_bias)
    _, pair = lax.optimization_barrier((shard, pair))
    near, far, opposite = flip(pair, "zl"), flip(pair, "zl", "mp"), flip(pair, "mp")
    pair, pair_t = gather_tokens(pair, opposite, near, far)

    doc = jnp.stack([parts[k][0, -length:] for k in (0, 2, 1, 3)]).astype(jnp.int32)
    doc = doc.reshape(4, 2, half_rows)
    doc = jnp.where(this_half == 0, doc, doc[:, ::-1]).reshape(4, length)
    halves = jnp.stack([this_half, 1 - this_half]) * half_rows
    index = (halves[:, None] + jnp.arange(half_rows, dtype=jnp.int32)).reshape(1, length)
    index = jnp.broadcast_to(index, (4, length)).astype(jnp.int32)
    b_up_here = lax.dynamic_slice_in_dim(b_up, place_here * hidden, hidden)
    b_qkv_here = lax.dynamic_slice_in_dim(b_qkv, place_here * width, width, axis=1).reshape(-1)

    tables = rotary_tables(doc, index)

    pair, pair_t, tables = lax.optimization_barrier((pair, pair_t, tables))
    right, head_grads, head_bias, head_sums = heads(pair, pair_t, weights, b_qkv_here, tables, length)
    head_grads = scatter_plane(head_grads)

    right, pair, pair_t = lax.optimization_barrier((right, pair, pair_t))
    hidden_pair, up_blocks, down_blocks = mlp(
        coords,
        pair,
        pair_t,
        weights,
        b_up_here,
        layernorm_gain,
        layernorm_bias,
        cot_sums,
        head_sums,
        head_bias,
    )

    up_blocks, down_blocks, hidden_pair = lax.optimization_barrier((up_blocks, down_blocks, hidden_pair))
    up_own, up_one, up_three, up_low, up_high = up_blocks
    down_own, down_one, down_three, down_low, down_high = down_blocks
    low = [hop(up_low, "y", 1), hop(down_low, "x", 1)]
    high = [hop(up_high, "y", 3), hop(down_high, "x", 3)]
    mine, theirs = combine(hidden_pair, right, weights)
    low, high, mine, theirs = lax.optimization_barrier((low, high, mine, theirs))
    theirs = flip(theirs, "c")
    up_one, up_three, down_one, down_three = bump(
        (up_one, high[0], 1), (up_three, low[0], 0), (down_one, high[1], 1), (down_three, low[1], 0)
    )
    up_one, up_three = hop(up_one, "y", 1), hop(up_three, "y", 3)
    down_one, down_three = hop(down_one, "x", 1), hop(down_three, "x", 3)
    keep, sends = fold(mine, theirs)
    opposite = flip(sends[0], "mp")
    up_one, up_three, down_one, down_three, opposite, keep, near, far, head_grads = lax.optimization_barrier(
        (up_one, up_three, down_one, down_three, opposite, keep, sends[1], sends[2], settle(head_grads))
    )
    along_z = [opposite, flip(near, "zl"), flip(far, "zl", "mp")]
    down_sums = near_down(coords, down_own, down_one, down_three)
    up_sums = near_up(up_own, up_one, up_three)
    up_sums = [up_sums[0]] + [hop(part, "x", bits) for part, bits in zip(up_sums[1:], (1, 2, 3))]
    down_sums = lax.psum_scatter(
        down_sums.reshape(-1, hidden), "y", scatter_dimension=0, tiled=True
    )
    up_sums, summed = lax.optimization_barrier((up_sums, cut_summed(coords, down_sums, head_grads)))
    parts = exchange(cut(coords, up_sums, summed))
    mixed, d_tokens = leave(
        tokens, cotangent, layernorm_gain, b_out + b_down, [keep] + along_z
    )
    mixed, d_tokens, *parts = lax.optimization_barrier((mixed, d_tokens, *parts))
    vectors, grad_b_up, grad_b_qkv = unpack_vectors(coords, parts, hidden, width)
    swapped = flip(vectors, "mp")
    grad_up_w, grad_down_w, grad_qkv_w, grad_out_w = unpack(coords, parts, hidden, width)
    vectors, swapped, grad_up_w = lax.optimization_barrier((vectors, swapped, grad_up_w))
    vectors = (vectors + swapped)[:6].reshape(3, depth)
    return (
        mixed,
        d_tokens,
        vectors[0],
        vectors[1],
        grad_qkv_w.transpose(1, 0, 2),
        grad_b_qkv,
        grad_out_w.T,
        vectors[2],
        grad_up_w,
        grad_b_up[0],
        grad_down_w.T,
        vectors[2],
    )


def solution(mesh):
    fine = Mesh(mesh.devices.reshape(SIZES), AXES)
    dp = ("zl", "x", "y", "c")
    in_specs = (
        P(AXES, None),
        P(),
        P(),
        P(dp, None, "mp"),
        P(None, "mp"),
        P("mp", dp),
        P(),
        P(dp, "mp"),
        P("mp"),
        P("mp", dp),
        P(),
        P(dp),
        P(AXES, None),
    )
    out_specs = (
        P(AXES, None),
        P(AXES, None),
        P(),
        P(),
        P(dp, None, "mp"),
        P(None, "mp"),
        P("mp", dp),
        P(),
        P(dp, "mp"),
        P("mp"),
        P("mp", dp),
        P(),
    )
    return jax.shard_map(
        per_device, mesh=fine, in_specs=in_specs, out_specs=out_specs, check_vma=False
    )
```
